128 devices in a mesh: lat: 8 (over z_lo, x), lon: 16 (over y, z_hi, core).
Axes of the slice: x: 4, y: 4, z: 4 (z_hi: 2, z_lo: 2; z = z_hi * 2 + z_lo), core: 2. Of those that a mesh axis runs over, the one named last changes fastest.
Arguments:
- grid_state: bfloat16 [96, 256, 1024], P('lat', 'lon'), may hold values from -7 to 7
- observations: bfloat16 [32768, 1024], P(('lat', 'lon')), may hold values from -6 to 6
- obs_tile: int32 [32768, 1], P(('lat', 'lon')), may hold values from 0 to 127; in each aligned block of 256 rows (0 to 255, 256 to 511, ...) at most 4 rows name the same one
- obs_cell: int32 [32768, 1], P(('lat', 'lon')), may hold values from 0 to 191
- cotangent: bfloat16 [96, 256, 1024], P('lat', 'lon'), may hold values from -6 to 6
- norm_gains: float32 [3, 1024], replicated, may hold values from 0.5 to 1.5
- w_cross_query: bfloat16 [1024, 1024], replicated, may hold values from -0.25 to 0.25
- w_cross_pairs: bfloat16 [1024, 2048], replicated, may hold values from -0.25 to 0.25
- w_cross_out: bfloat16 [1024, 1024], replicated, may hold values from -0.1875 to 0.1875
- w_near_proj: bfloat16 [1024, 3072], replicated, may hold values from -0.25 to 0.25
- w_near_out: bfloat16 [1024, 1024], replicated, may hold values from -0.1875 to 0.1875
- w_up: bfloat16 [1024, 2048], replicated, may hold values from -0.1875 to 0.1875
- w_down: bfloat16 [2048, 1024], replicated, may hold values from -0.125 to 0.125
Outputs:
- encoded: bfloat16 [96, 256, 1024], P('lat', 'lon')
- grid_grad: bfloat16 [96, 256, 1024], P('lat', 'lon')
- obs_grad: bfloat16 [32768, 1024], P(('lat', 'lon'))
The draws below stay inside these ranges and needn't reach their ends.
Inputs may be any that keep to these rules, and one draw needn't show every extreme that they name: `obs_tile`: tile index of the row's observation; among the rows of one device at most 4 name one tile, and every tile is named by some row. `obs_cell`: In-tile cell of the row's observation, row-major within the tile.
All inputs are finite; a program needn't handle non-finite values.
Results may differ from the reference program's by a relative error of at most 0.035.
Values may be sent and summed in bfloat16 or wider, within the bound.
No kernel may reach another device: no remote copies, remote signals or barrier semaphores. Data moves between devices by JAX's collectives and lax.ppermute only.
A program may use at most 192 MiB of HBM per device.

```python
import math
import jax
import jax.numpy as jnp
import numpy as np
from jax import lax

HEADS = 16
HEAD_DIM = 64
D = 1024
FF = 2048
TH = 12
TW = 16
RADIUS = 6
OBS_DEV = 256
TILES = 128
CAP = 4
NLAT = 96
NLON = 256
NOBS = 32768
SLOTS = 512
N_LAT = 8
N_LON = 16


def base_weight(key, row_count, col_count):
    values = jax.random.normal(key, (row_count, col_count), jnp.float32)
    return jnp.clip(values, -6.0, 6.0) * row_count ** (-0.5)


def draw_grid_state(key, part):
    key = jax.random.fold_in(key, 5)
    values = jnp.clip(jax.random.normal(key, (NLAT, NLON, D), jnp.float32), -6.0, 6.0)
    return values.astype(jnp.bfloat16)


def draw_observations(key, part):
    key = jax.random.fold_in(key, 7)
    values = jnp.clip(jax.random.normal(key, (NOBS, D), jnp.float32), -6.0, 6.0)
    return values.astype(jnp.bfloat16)


def draw_w_cross_query(key, part):
    key = jax.random.fold_in(key, 3)
    values = base_weight(key, D, D)
    return values.astype(jnp.bfloat16)


def draw_w_cross_pairs(key, part):
    key = jax.random.fold_in(key, 4)
    values = base_weight(key, D, 2 * D)
    return values.astype(jnp.bfloat16)


def draw_w_near_proj(key, part):
    key = jax.random.fold_in(key, 6)
    values = base_weight(key, D, 3 * D)
    return values.astype(jnp.bfloat16)


def set_ends(values, own_key, smallest, top_value):
    extent = values.shape
    place = [jax.random.randint(jax.random.fold_in(own_key, axis), (), 0, extent[axis]) for axis in range(len(extent))]
    values = values.at[tuple(place)].set(smallest)
    longest = extent.index(max(extent))
    place[longest] = (place[longest] + 1) % extent[longest]
    return values.at[tuple(place)].set(top_value)


def levels(stream_key, dims, split, least, top_value):
    def one(dim, parts):
        heights = jax.random.uniform(jax.random.fold_in(jax.random.fold_in(stream_key, 6), dim), (parts,), jnp.float32, least / len(split), top_value / len(split))
        return jnp.repeat(jnp.exp(heights), dims[dim] // parts).reshape((-1,) + (1,) * (len(dims) - dim - 1))

    factor_of = one(*split[0])
    for cut in split[1:]:
        factor_of = factor_of * one(*cut)
    return factor_of


def shared_out(rng, own, number, rows, count, top, reach, skew):
    sequence = jax.random.permutation(rng, count)
    crowded, ordinary = shares(count, rows * top, reach, skew, True), shares(count, rows * top, reach, skew, False)
    places = jnp.arange(count)

    def named(tallies, turn):
        used = int((tallies > 0).sum())
        fixed = max(1, used // 4)
        shifted = fixed + (places - fixed + turn * (used - fixed)) % max(1, count - fixed)
        return jnp.zeros((count,), jnp.int32).at[sequence[jnp.where(places < fixed, places, shifted)]].set(jnp.asarray(tallies, jnp.int32))

    tallies = jnp.where(number % 4 == 0, named(crowded, number // 4), named(ordinary, number - number // 4 - 1))
    mixed = jax.random.permutation(jax.random.fold_in(own, 3), count)
    source_of, sink = mixed[0:count // 2 * 2:2], mixed[1:count // 2 * 2:2]
    margin = jnp.minimum(tallies[source_of] - 1, reach - tallies[sink]) // 2
    margin = jnp.where((source_of == sequence[0]) | (sink == sequence[0]) | (tallies[sink] == 0), 0, jnp.maximum(margin, 0))
    shifted = jax.random.randint(jax.random.fold_in(own, 4), (count // 2,), 0, 1 << 20) % (margin + 1)
    tallies = tallies.at[source_of].add(-shifted).at[sink].add(shifted)
    labels = jnp.searchsorted(jnp.cumsum(tallies), jnp.arange(rows * top), side="right").astype(jnp.int32)
    table = labels.reshape(top, rows).T
    table = table[jax.random.permutation(jax.random.fold_in(own, 1), rows)]
    turn = jax.random.randint(jax.random.fold_in(own, 2), (rows, 1), 0, top)
    return jnp.take_along_axis(table, (jnp.arange(top)[None, :] + turn) % top, axis=1)


def shares(number_of, total, reach, skew, full):
    weights = [(1 << 20) // math.isqrt(standing ** skew) + 1 for standing in range(1, number_of + 1)]
    largest = reach if full else min(reach, max(-(-total // number_of), total * weights[0] // sum(weights)))
    least = 1 if total - largest >= number_of - 1 else 0
    holding, spare = [largest] + [least] * (number_of - 1), total - largest - least * (number_of - 1)
    while spare > 0:
        free = [i for i in range(1, number_of) if holding[i] < largest] or [i for i in range(1, number_of) if holding[i] < reach]
        mass, budget = sum([weights[i] for i in free]), spare
        for i in free:
            addition = min(reach - holding[i], max(1, budget * weights[i] // mass), spare)
            holding[i] = holding[i] + addition
            spare = spare - addition
    return np.array(holding)


def centred(stream_key, extent, deviation, reach, cuts=(), held_as=jnp.bfloat16):
    array = jax.random.normal(stream_key, extent, jnp.float32) * deviation
    if len(cuts) > 0:
        array = levels(stream_key, extent, cuts, -0.22, 0.18) * array
    return jnp.clip(array, min=-reach, max=reach).astype(held_as)


def setup_inputs(seed: int = 0) -> dict:
    keys = jax.random.split(jax.random.key(seed), 14)
    grid_state = draw_grid_state(jax.random.fold_in(keys[13], 71), 0)
    observations = draw_observations(jax.random.fold_in(keys[13], 71), 0)
    obs_tile_keys = jax.random.split(jax.random.fold_in(keys[2], 1), NOBS // OBS_DEV)
    obs_tile_turns = jax.random.permutation(jax.random.fold_in(keys[2], 3), NOBS // OBS_DEV)
    obs_tile = jax.vmap(lambda own, number: shared_out(jax.random.fold_in(keys[2], 2), own, number, OBS_DEV, TILES, 1, CAP, 2))(obs_tile_keys, obs_tile_turns).reshape((NOBS, 1))
    obs_cell = set_ends(jax.random.randint(keys[3], (NOBS, 1), 0, TH * TW), jax.random.fold_in(keys[3], 1), 0, (TH * TW) - 1).astype(jnp.int32)
    cotangent = centred(keys[4], (NLAT, NLON, D), 1.0, 6.0, ((0, 8), (1, 16)))
    norm_gains = jnp.clip(1.0 + 0.1 * jax.random.normal(keys[5], (3, D), jnp.float32), 0.5, 1.5)
    w_cross_query = draw_w_cross_query(jax.random.fold_in(keys[13], 71), 0)
    w_cross_pairs = draw_w_cross_pairs(jax.random.fold_in(keys[13], 71), 0)
    w_cross_out = centred(keys[8], (D, D), D ** -0.5, 0.1875)
    w_near_proj = draw_w_near_proj(jax.random.fold_in(keys[13], 71), 0)
    w_near_out = centred(keys[10], (D, D), D ** -0.5, 0.1875)
    w_up = centred(keys[11], (D, FF), D ** -0.5, 0.1875)
    w_down = centred(keys[12], (FF, D), FF ** -0.5, 0.125)
    return {"grid_state": grid_state, "observations": observations, "obs_tile": obs_tile, "obs_cell": obs_cell, "cotangent": cotangent, "norm_gains": norm_gains, "w_cross_query": w_cross_query, "w_cross_pairs": w_cross_pairs, "w_cross_out": w_cross_out, "w_near_proj": w_near_proj, "w_near_out": w_near_out, "w_up": w_up, "w_down": w_down}


EPSILON = 1e-05
SPREAD = 32.0
LOW_SCORE = -1e+30

def layer_norm(values, gain):
    values = values.astype(jnp.float32)
    center = values - lax.optimization_barrier(jnp.mean(values, -1, keepdims=True))
    second = lax.optimization_barrier(jnp.mean(center * center, -1, keepdims=True))
    return (center * lax.rsqrt(second + EPSILON) * gain).astype(jnp.bfloat16)

def matmul(left, right):
    return jnp.dot(left, right, preferred_element_type=jnp.float32)

def split_heads(values):
    return values.astype(jnp.float32).reshape(values.shape[0], HEADS, HEAD_DIM)

def cross_attend(queries, own_pairs, slot_pairs, slot_rows, slot_cols, slot_valid):
    query_heads = split_heads(queries)
    key_slots = split_heads(slot_pairs[:, :D])
    value_slots = split_heads(slot_pairs[:, D:])
    key_own = split_heads(own_pairs[:, :D])
    value_own = split_heads(own_pairs[:, D:])
    score_scale = HEAD_DIM ** (-0.5)
    scores = jnp.einsum('qhd,khd->hqk', query_heads, key_slots) * score_scale
    cell_ids = lax.iota(jnp.int32, TH * TW)
    row_gap = (cell_ids // TW)[:, None] - slot_rows[None, :]
    col_gap = (cell_ids % TW)[:, None] - slot_cols[None, :]
    locality = -(row_gap * row_gap + col_gap * col_gap).astype(jnp.float32) / SPREAD
    scores = jnp.where(slot_valid[None, None, :], scores + locality[None], LOW_SCORE)
    own_score = jnp.einsum('qhd,qhd->hq', query_heads, key_own) * score_scale
    row_peak = jnp.maximum(lax.optimization_barrier(jnp.max(scores, -1)), own_score)
    weights = jnp.exp(scores - row_peak[:, :, None])
    own_weight = jnp.exp(own_score - row_peak)
    totals = lax.optimization_barrier(jnp.sum(weights, -1)) + own_weight
    weights = (weights / totals[:, :, None]).astype(jnp.bfloat16)
    own_weight = (own_weight / totals).astype(jnp.bfloat16)
    mixed_heads = jnp.einsum('hqk,khd->qhd', weights.astype(jnp.float32), value_slots)
    mixed_heads = mixed_heads + own_weight.astype(jnp.float32).T[:, :, None] * value_own
    return mixed_heads.reshape(TH * TW, D).astype(jnp.bfloat16)

def near_attend(queries, pairs, lat_start):
    wide_rows = TH + 2 * RADIUS
    wide_cols = TW + 2 * RADIUS
    query_heads = split_heads(queries.reshape(TH * TW, D))
    flat_pairs = pairs.reshape(wide_rows * wide_cols, 2 * D)
    key_cells = split_heads(flat_pairs[:, :D])
    value_cells = split_heads(flat_pairs[:, D:])
    scores = jnp.einsum('qhd,khd->hqk', query_heads, key_cells) * HEAD_DIM ** (-0.5)
    query_ids = lax.iota(jnp.int32, TH * TW)
    key_ids = lax.iota(jnp.int32, wide_rows * wide_cols)
    row_gap = (key_ids // wide_cols)[None, :] - RADIUS - (query_ids // TW)[:, None]
    col_gap = (key_ids % wide_cols)[None, :] - RADIUS - (query_ids % TW)[:, None]
    key_lat = lat_start + key_ids // wide_cols - RADIUS
    inside = (key_lat >= 0) & (key_lat < NLAT)
    allowed = (jnp.abs(row_gap) <= RADIUS) & (jnp.abs(col_gap) <= RADIUS) & inside[None, :]
    scores = jnp.where(allowed[None], scores, LOW_SCORE)
    row_peak = lax.optimization_barrier(jnp.max(scores, -1, keepdims=True))
    weights = jnp.exp(scores - row_peak)
    weights = (weights / lax.optimization_barrier(jnp.sum(weights, -1, keepdims=True))).astype(jnp.bfloat16)
    mixed_heads = jnp.einsum('hqk,khd->qhd', weights.astype(jnp.float32), value_cells)
    return mixed_heads.reshape(TH * TW, D).astype(jnp.bfloat16)

def to_tiles(values):
    width_here = values.shape[-1]
    shaped = values.reshape(N_LAT, TH, N_LON, TW, width_here).transpose(0, 2, 1, 3, 4)
    return shaped.reshape(TILES, TH, TW, width_here)

def from_tiles(values):
    width_here = values.shape[-1]
    shaped = values.reshape(N_LAT, N_LON, TH, TW, width_here).transpose(0, 2, 1, 3, 4)
    return shaped.reshape(NLAT * NLON, width_here)

def reference(grid_state, observations, obs_tile, obs_cell, cotangent, norm_gains, w_cross_query, w_cross_pairs, w_cross_out, w_near_proj, w_near_out, w_up, w_down):
    dest_tile = obs_tile[:, 0].astype(jnp.int32)
    order = jnp.argsort(dest_tile, stable=True).astype(jnp.int32)
    counts = jax.ops.segment_sum(jnp.ones_like(dest_tile), dest_tile, num_segments=TILES).astype(jnp.int32)
    starts = (jnp.cumsum(counts) - counts).astype(jnp.int32)
    cells = obs_cell[:, 0].astype(jnp.int32)
    pad_ints = jnp.zeros((SLOTS,), jnp.int32)
    sorted_rows = jnp.concatenate([(cells // TW)[order], pad_ints])
    sorted_cols = jnp.concatenate([(cells % TW)[order], pad_ints])
    tile_ids = lax.iota(jnp.int32, TILES)

    def encode_all(grid_in, obs_in):
        flat = grid_in.reshape(NLAT * NLON, D)
        normal = layer_norm(flat, norm_gains[0])
        queries = matmul(normal, w_cross_query).astype(jnp.bfloat16)
        own_pairs = matmul(normal, w_cross_pairs).astype(jnp.bfloat16)
        obs_pairs = matmul(obs_in, w_cross_pairs).astype(jnp.bfloat16)
        sorted_pairs = jnp.concatenate([obs_pairs[order], jnp.zeros((SLOTS, 2 * D), jnp.bfloat16)])
        query_tiles = to_tiles(queries.reshape(NLAT, NLON, D)).reshape(TILES, TH * TW, D)
        own_tiles = to_tiles(own_pairs.reshape(NLAT, NLON, 2 * D)).reshape(TILES, TH * TW, 2 * D)

        def cross_one(tile_items):
            start, count, query_tile, own_tile = tile_items
            window = lax.dynamic_slice_in_dim(sorted_pairs, start, SLOTS, 0)
            rows_win = lax.dynamic_slice_in_dim(sorted_rows, start, SLOTS, 0)
            cols_win = lax.dynamic_slice_in_dim(sorted_cols, start, SLOTS, 0)
            valid = lax.iota(jnp.int32, SLOTS) < count
            return cross_attend(query_tile, own_tile, window, rows_win, cols_win, valid)
        cross_mixed = lax.map(jax.checkpoint(cross_one), (starts, counts, query_tiles, own_tiles))
        state = flat.astype(jnp.float32) + matmul(from_tiles(cross_mixed), w_cross_out)
        normal = layer_norm(state, norm_gains[1])
        both_proj = matmul(normal, w_near_proj)
        near_queries = both_proj[:, :D].astype(jnp.bfloat16)
        near_pairs = both_proj[:, D:].astype(jnp.bfloat16).reshape(NLAT, NLON, 2 * D)
        padded = jnp.pad(near_pairs, ((RADIUS, RADIUS), (0, 0), (0, 0)))
        padded = jnp.concatenate([padded[:, NLON - RADIUS:], padded, padded[:, :RADIUS]], 1)
        near_tiles = to_tiles(near_queries.reshape(NLAT, NLON, D))

        def near_one(tile_items):
            tile_index, query_tile = tile_items
            lat_band = tile_index // N_LON
            lon_band = tile_index % N_LON
            zero_index = jnp.zeros((), jnp.int32)
            window = lax.dynamic_slice(padded, ((lat_band * TH).astype(jnp.int32), (lon_band * TW).astype(jnp.int32), zero_index), (TH + 2 * RADIUS, TW + 2 * RADIUS, 2 * D))
            return near_attend(query_tile, window, lat_band * TH)
        near_mixed = lax.map(jax.checkpoint(near_one), (tile_ids, near_tiles))
        after = state + matmul(from_tiles(near_mixed), w_near_out)
        normal = layer_norm(after, norm_gains[2])
        hidden = jax.nn.gelu(matmul(normal, w_up)).astype(jnp.bfloat16)
        return (after + matmul(hidden, w_down)).astype(jnp.bfloat16).reshape(NLAT, NLON, D)
    encoded, pullback = jax.vjp(encode_all, grid_state, observations)
    grid_grad, obs_grad = pullback(cotangent)
    return (encoded, grid_grad, obs_grad)
```

```python
import functools

import jax
import jax.numpy as jnp
import numpy as np
from jax import lax
from jax.experimental import pallas as pl
from jax.experimental.pallas import tpu as pltpu
from jax.sharding import PartitionSpec as P

HEADS = 16
RADIUS = 6
EPSILON = 1e-05
SPREAD = 32.0
LOW_SCORE = -1e30

BF = jnp.bfloat16
F32 = jnp.float32
NN = (((1,), (0,)), ((), ()))
NT = (((1,), (1,)), ((), ()))
TN = (((0,), (0,)), ((), ()))
CHUNK = 32
TILE = 256
PAIR = 128
HALF = 64
VMEM_BYTES = 56 * 2**20
GELU_C = 0.7978845608028654
GELU_A = 0.044715


def dot(left, right, dims=NN):
    return lax.dot_general(left, right, dims, preferred_element_type=F32)


def iota(shape, dim):
    return lax.broadcasted_iota(jnp.int32, shape, dim)


def tiles_of(count, body, tile=TILE):
    @pl.loop(0, count // tile)
    def _(i):
        body(pl.multiple_of(i * tile, tile))


def row_chunks(count):
    return [pl.ds(i, CHUNK) for i in range(0, count, CHUNK)]


def unit(values):
    center = values - jnp.mean(values, -1, keepdims=True)
    scale = lax.rsqrt(jnp.mean(center * center, -1, keepdims=True) + EPSILON)
    return center * scale, scale


def norm_pull(values, gain, grad):
    normed, scale = unit(values)
    inner = grad * gain
    return scale * (
        inner
        - jnp.mean(inner, -1, keepdims=True)
        - normed * jnp.mean(inner * normed, -1, keepdims=True)
    )


def head_masks():
    left = (iota((1, PAIR), 1) < HALF).astype(F32)
    return left.astype(BF), (1.0 - left).astype(BF)


def stacked(values):
    left, right = head_masks()
    return jnp.concatenate([values * left, values * right], axis=0)


def merged(values):
    count = values.shape[0] // 2
    lanes = iota((count, PAIR), 1) < HALF
    return jnp.where(lanes, values[:count], values[count:])


def lane_sums(values):
    lanes = iota(values.shape, 1) < HALF
    first = jnp.sum(jnp.where(lanes, values, 0.0), -1, keepdims=True)
    second = jnp.sum(jnp.where(lanes, 0.0, values), -1, keepdims=True)
    return first, second


def fetch(sources, targets, sems):
    copies = [
        pltpu.make_async_copy(source, target, sems.at[i])
        for i, (source, target) in enumerate(zip(sources, targets))
    ]
    for copy in copies:
        copy.start()
    return copies


def call(body, ins, kinds, outs, scratch, flops, name):
    any_spec = pl.BlockSpec(memory_space=pl.ANY)
    vmem_spec = pl.BlockSpec(memory_space=pltpu.VMEM)
    moved = sum(x.size * x.dtype.itemsize for x in ins)
    moved += sum(int(np.prod(s)) * jnp.dtype(t).itemsize for s, t in outs)
    single = len(outs) == 1
    shapes = [jax.ShapeDtypeStruct(s, t) for s, t in outs]
    return pl.pallas_call(
        body,
        name=name,
        out_shape=shapes[0] if single else shapes,
        in_specs=[any_spec if k == "h" else vmem_spec for k in kinds],
        out_specs=vmem_spec if single else [vmem_spec] * len(outs),
        scratch_shapes=scratch,
        compiler_params=pltpu.CompilerParams(vmem_limit_bytes=VMEM_BYTES),
        cost_estimate=pl.CostEstimate(
            flops=int(flops), bytes_accessed=int(moved), transcendentals=0
        ),
    )(*ins)


def place_kernel(tile_ref, cell_ref, obs_ref, pay_ref, place_ref, *, devices, cap, wide):
    rows, model = obs_ref.shape
    slots = devices * cap
    tile = tile_ref[...]
    member = tile == iota((rows, devices), 1)
    earlier = (iota((rows, rows), 1) < iota((rows, rows), 0)).astype(F32).astype(BF)
    before = dot(earlier, member.astype(F32).astype(BF))
    rank = jnp.sum(jnp.where(member, before, 0.0), -1, keepdims=True).astype(jnp.int32)
    slot = tile * cap + rank
    placing = (slot == iota((rows, slots), 1)).astype(F32).astype(BF)
    place_ref[...] = placing
    cell = cell_ref[...]
    shift = wide.bit_length() - 1
    lane = iota((rows, 128), 1)
    codes = jnp.where(
        lane == 0, (cell >> shift) + 1, jnp.where(lane == 1, (cell & (wide - 1)) + 1, 0)
    )
    pay_ref[:, model:] = dot(placing, codes.astype(F32).astype(BF), TN).astype(BF)
    for j in range(0, model, TILE):
        pay_ref[:, j : j + TILE] = dot(placing, obs_ref[:, j : j + TILE], TN).astype(BF)


def grid_kernel(
    grid_ref, cot_ref, gain_ref, wq_hbm, wp_hbm, wd_hbm, q_ref, own_ref, dh_ref,
    nrm, wq, wp, wd, sems,
):
    copies = fetch([wq_hbm, wp_hbm, wd_hbm], [wq, wp, wd], sems)
    cells, model = grid_ref.shape
    for rows in row_chunks(cells):
        normed, _ = unit(grid_ref[rows, :].astype(F32))
        nrm[rows, :] = (normed * gain_ref[0:1, :]).astype(BF)
    copies[0].wait()

    def query(j):
        q_ref[:, pl.ds(j, TILE)] = (
            dot(nrm[...], wq[:, pl.ds(j, TILE)]) * HALF ** (-0.5)
        ).astype(BF)

    tiles_of(model, query)
    copies[1].wait()

    def own(j):
        own_ref[:, pl.ds(j, TILE)] = dot(nrm[...], wp[:, pl.ds(j, TILE)]).astype(BF)

    tiles_of(2 * model, own)
    copies[2].wait()

    def hidden(j):
        dh_ref[:, pl.ds(j, TILE)] = dot(cot_ref[...], wd[pl.ds(j, TILE), :], NT).astype(BF)

    tiles_of(dh_ref.shape[1], hidden)


def cross_kernel(
    arr_ref, grid_ref, q_ref, own_ref, gain_ref, wp_hbm, wo_hbm,
    state_ref, nrm_ref, pairs_ref, wts_ref, mix_ref, ow_ref,
    wp, wo, scores, bias, sems, *, wide,
):
    copies = fetch([wp_hbm, wo_hbm], [wp, wo], sems)
    cells, model = grid_ref.shape
    slots = arr_ref.shape[0]
    pick = (iota((8, 128), 0) == iota((8, 128), 1)).astype(F32).astype(BF)
    codes = dot(pick, arr_ref[:, model:], NT)
    cell = iota((cells, slots), 0)
    shift = wide.bit_length() - 1
    row_gap = (cell >> shift).astype(F32) - (codes[0:1] - 1.0)
    col_gap = (cell & (wide - 1)).astype(F32) - (codes[1:2] - 1.0)
    near = -(row_gap * row_gap + col_gap * col_gap) * (1.0 / SPREAD)
    bias[...] = jnp.where(codes[0:1] > 0.5, near, LOW_SCORE)
    copies[0].wait()

    def project(j):
        pairs_ref[:, pl.ds(j, TILE)] = dot(
            arr_ref[:, :model], wp[:, pl.ds(j, TILE)]
        ).astype(BF)

    tiles_of(2 * model, project)

    @pl.loop(0, model // PAIR)
    def _(h):
        keys = pl.ds(pl.multiple_of(h * PAIR, PAIR), PAIR)
        vals = pl.ds(pl.multiple_of(model + h * PAIR, PAIR), PAIR)
        q = q_ref[:, keys]
        scores[...] = dot(stacked(q), pairs_ref[:, keys], NT)
        own_scores = lane_sums(q.astype(F32) * own_ref[:, keys].astype(F32))
        own_weights = []
        for side in range(2):
            parts = []
            for i in range(0, cells, CHUNK):
                own_score = own_scores[side][i : i + CHUNK]
                x = scores[pl.ds(side * cells + i, CHUNK), :] + bias[pl.ds(i, CHUNK), :]
                peak = jnp.maximum(jnp.max(x, -1, keepdims=True), own_score)
                x = jnp.exp(x - peak)
                own_weight = jnp.exp(own_score - peak)
                inverse = 1.0 / (jnp.sum(x, -1, keepdims=True) + own_weight)
                wts_ref[h, pl.ds(side * cells + i, CHUNK), :] = (x * inverse).astype(BF)
                parts.append(own_weight * inverse)
            own_weights.append(jnp.concatenate(parts, axis=0))
        lanes = iota((cells, PAIR), 1) < HALF
        weight = jnp.where(lanes, own_weights[0], own_weights[1]).astype(BF)
        ow_ref[:, keys] = weight
        mix = merged(dot(wts_ref[h], pairs_ref[:, vals]))
        mix_ref[:, keys] = (
            mix + weight.astype(F32) * own_ref[:, vals].astype(F32)
        ).astype(BF)

    copies[1].wait()

    def project_out(j):
        state_ref[:, pl.ds(j, TILE)] = grid_ref[:, pl.ds(j, TILE)].astype(F32) + dot(
            mix_ref[...], wo[:, pl.ds(j, TILE)]
        )

    tiles_of(model, project_out)
    for rows in row_chunks(cells):
        normed, _ = unit(state_ref[rows, :])
        nrm_ref[rows, :] = (normed * gain_ref[1:2, :]).astype(BF)


def near_own_kernel(nrm_ref, w_hbm, q_ref, kv_ref, w, sems):
    cells, model = nrm_ref.shape
    copies = fetch(
        [w_hbm.at[:, pl.ds(0, model)], w_hbm.at[:, pl.ds(model, 2 * model)]],
        [w.at[:, pl.ds(0, model)], w.at[:, pl.ds(model, 2 * model)]],
        sems,
    )
    copies[0].wait()

    def query(j):
        q_ref[:, pl.ds(j, TILE)] = (
            dot(nrm_ref[...], w[:, pl.ds(j, TILE)]) * HALF ** (-0.5)
        ).astype(BF)

    tiles_of(model, query)
    copies[1].wait()

    def pairs(j):
        kv_ref[:, pl.ds(j, TILE)] = dot(
            nrm_ref[...], w[:, pl.ds(pl.multiple_of(model + j, TILE), TILE)]
        ).astype(BF)

    tiles_of(2 * model, pairs)


def rim_kernel(own_ref, north_ref, south_ref, sel_ref, west_ref, east_ref, ext):
    cells, model = own_ref.shape
    rim = north_ref.shape[0]
    ext[pl.ds(0, cells), :] = own_ref[...]
    ext[pl.ds(cells, rim), :] = north_ref[...]
    ext[pl.ds(cells + rim, rim), :] = south_ref[...]
    side = west_ref.shape[0]

    def pick(j):
        both = dot(sel_ref[...], ext[:, pl.ds(j, TILE)]).astype(BF)
        west_ref[:, pl.ds(j, TILE)] = both[:side]
        east_ref[:, pl.ds(j, TILE)] = both[side:]

    tiles_of(model, pick)


def near_rows_kernel(north_ref, south_ref, w_hbm, kv_ref, x, w, sems):
    rim, model = north_ref.shape
    copies = fetch([w_hbm.at[:, pl.ds(model, 2 * model)]], [w], sems)
    x[pl.ds(0, rim), :] = north_ref[...]
    x[pl.ds(rim, rim), :] = south_ref[...]
    copies[0].wait()

    def pairs(j):
        kv_ref[:, pl.ds(j, TILE)] = dot(x[...], w[:, pl.ds(j, TILE)]).astype(BF)

    tiles_of(2 * model, pairs)


def near_kernel(
    q_ref, west_ref, east_ref, base_ref, inside_ref, state_ref, cot_ref, dh_ref, gain_ref,
    kvo_hbm, kvr_hbm, wn_hbm, wo_hbm, wu_hbm,
    after_ref, hid_ref, dwest_ref, deast_ref, dqkv_ref, drows_ref, dafter_ref,
    wkv, wo, wu, kv, dkv, x, wts, scores, ds, bias, mix, nrm, du, acc, dab, dmix, sems,
):
    cells, model = state_ref.shape
    keys_all = kv.shape[0]
    ext = 2 * cells
    side = west_ref.shape[0]
    ends = ext + 2 * side
    copies = fetch(
        [kvo_hbm, kvr_hbm, wn_hbm.at[:, pl.ds(model, 2 * model)], wo_hbm, wu_hbm],
        [kv.at[pl.ds(0, cells), :], kv.at[pl.ds(cells, cells), :], wkv, wo, wu],
        sems,
    )
    x[pl.ds(0, side), :] = west_ref[...]
    x[pl.ds(side, side), :] = east_ref[...]
    kv[pl.ds(ends, keys_all - ends), :] = jnp.zeros((keys_all - ends, 2 * model), BF)
    bias[...] = base_ref[...].astype(F32) + inside_ref[0:1, :]
    copies[0].wait()
    copies[1].wait()
    copies[2].wait()

    def project(j):
        kv[pl.ds(ext, 2 * side), pl.ds(j, TILE)] = dot(
            x[...], wkv[:, pl.ds(j, TILE)]
        ).astype(BF)

    tiles_of(2 * model, project)

    @pl.loop(0, model // PAIR)
    def _(h):
        keys = pl.ds(pl.multiple_of(h * PAIR, PAIR), PAIR)
        vals = pl.ds(pl.multiple_of(model + h * PAIR, PAIR), PAIR)
        scores[...] = dot(stacked(q_ref[:, keys]), kv[:, keys], NT)
        for start in range(0, 2 * cells, CHUNK):
            rows = pl.ds(start, CHUNK)
            v = scores[rows, :] + bias[pl.ds(start % cells, CHUNK), :]
            v = jnp.exp(v - jnp.max(v, -1, keepdims=True))
            inverse = 1.0 / jnp.sum(v, -1, keepdims=True)
            wts[h, rows, :] = (v * inverse).astype(BF)
        mix[:, keys] = merged(dot(wts[h], kv[:, vals])).astype(BF)

    copies[3].wait()

    def project_out(j):
        after_ref[:, pl.ds(j, TILE)] = state_ref[:, pl.ds(j, TILE)] + dot(
            mix[...], wo[:, pl.ds(j, TILE)]
        )

    tiles_of(model, project_out)
    for rows in row_chunks(cells):
        normed, _ = unit(after_ref[rows, :])
        nrm[rows, :] = (normed * gain_ref[2:3, :]).astype(BF)
    copies[4].wait()

    def feed(j):
        cols = pl.ds(j, TILE)
        u = dot(nrm[...], wu[:, cols])
        square = u * u
        t = jnp.tanh(GELU_C * (u + GELU_A * (square * u)))
        half = 0.5 * (1.0 + t)
        hid_ref[:, cols] = (u * half).astype(BF)
        slope = half + (0.5 * GELU_C) * u * (1.0 - t * t) * (1.0 + 3.0 * GELU_A * square)
        du[:, cols] = (dh_ref[:, cols].astype(F32) * slope).astype(BF)

    tiles_of(du.shape[1], feed)

    def feed_back(j):
        acc[:, pl.ds(j, TILE)] = dot(du[...], wu[pl.ds(j, TILE), :], NT)

    tiles_of(model, feed_back)
    for rows in row_chunks(cells):
        grad = acc[rows, :].astype(BF).astype(F32)
        total = cot_ref[rows, :].astype(F32) + norm_pull(
            after_ref[rows, :], gain_ref[2:3, :], grad
        )
        dafter_ref[rows, :] = total
        dab[rows, :] = total.astype(BF)

    def mix_back(j):
        dmix[:, pl.ds(j, TILE)] = dot(dab[...], wo[pl.ds(j, TILE), :], NT).astype(BF)

    tiles_of(model, mix_back)

    @pl.loop(0, model // PAIR)
    def _(h):
        keys = pl.ds(pl.multiple_of(h * PAIR, PAIR), PAIR)
        vals = pl.ds(pl.multiple_of(model + h * PAIR, PAIR), PAIR)
        grad = dmix[:, keys]
        grad_2 = stacked(grad)
        scores[...] = dot(grad_2, kv[:, vals], NT)
        deltas = lane_sums(grad.astype(F32) * mix[:, keys].astype(F32))
        for s in range(2):
            for i in range(0, cells, CHUNK):
                rows = pl.ds(s * cells + i, CHUNK)
                ds[rows, :] = (
                    wts[h, rows, :].astype(F32)
                    * (scores[rows, :] - deltas[s][i : i + CHUNK])
                ).astype(BF)
        dqkv_ref[:, keys] = (merged(dot(ds[...], kv[:, keys])) * HALF ** (-0.5)).astype(BF)
        dkv[:, keys] = dot(stacked(q_ref[:, keys]), ds[...], TN).T.astype(BF)
        dkv[:, vals] = dot(grad_2, wts[h], TN).T.astype(BF)

    def rim_back(j):
        both = dot(dkv[pl.ds(ext, 2 * side), :], wkv[pl.ds(j, TILE), :], NT).astype(BF)
        dwest_ref[:, pl.ds(j, TILE)] = both[:side]
        deast_ref[:, pl.ds(j, TILE)] = both[side:]

    tiles_of(model, rim_back)
    dqkv_ref[:, pl.ds(model, 2 * model)] = dkv[pl.ds(0, cells), :]
    drows_ref[...] = dkv[pl.ds(cells, cells), :]


def encode_kernel(after_ref, hid_ref, wd_hbm, enc_ref, wd, sems):
    copies = fetch([wd_hbm], [wd], sems)
    copies[0].wait()

    def down(j):
        enc_ref[:, pl.ds(j, TILE)] = (
            after_ref[:, pl.ds(j, TILE)] + dot(hid_ref[...], wd[:, pl.ds(j, TILE)])
        ).astype(BF)

    tiles_of(after_ref.shape[1], down)


def near_back_kernel(dqkv_ref, drows_ref, w_hbm, dn_ref, w, sems):
    copies = fetch([w_hbm], [w], sems)
    cells, wide = dqkv_ref.shape
    model = wide // 3
    copies[0].wait()

    def back(j):
        dn_ref[pl.ds(0, cells), pl.ds(j, TILE)] = dot(dqkv_ref[...], w[pl.ds(j, TILE), :], NT)
        dn_ref[pl.ds(cells, cells), pl.ds(j, TILE)] = dot(
            drows_ref[...], w[pl.ds(j, TILE), pl.ds(model, 2 * model)], NT
        )

    tiles_of(model, back)


def fold_kernel(dn_ref, from_east_ref, from_west_ref, sel_ref, own_ref, north_ref, south_ref, x):
    cells, model = own_ref.shape
    rim = north_ref.shape[0]
    side = from_east_ref.shape[0]
    x[pl.ds(0, side), :] = from_west_ref[...]
    x[pl.ds(side, side), :] = from_east_ref[...]

    def fold(j):
        cols = pl.ds(j, TILE)
        total = dn_ref[:, cols] + dot(sel_ref[...], x[:, cols], TN)
        own_ref[:, cols] = total[:cells]
        north_ref[:, cols] = total[cells : cells + rim].astype(BF)
        south_ref[:, cols] = total[cells + rim :].astype(BF)

    tiles_of(model, fold)


def cross_back_kernel(
    dn_ref, north_ref, south_ref, state_ref, dafter_ref, gain_ref, q_ref, own_ref, pairs_ref,
    wts_ref, mix_ref, ow_ref, wp_hbm, wo_hbm,
    dstate_ref, slot_ref, dq_ref, down_ref,
    wp, wo, dsb, dmix, dpairs, scores, ds, sems,
):
    copies = fetch([wo_hbm, wp_hbm], [wo, wp], sems)
    cells, model = state_ref.shape
    rim = north_ref.shape[0]
    for i in range(0, cells, CHUNK):
        rows = pl.ds(i, CHUNK)
        other = north_ref[rows, :] if i < rim else south_ref[pl.ds(i - rim, CHUNK), :]
        grad = (dn_ref[rows, :] + other.astype(F32)).astype(BF).astype(F32)
        total = dafter_ref[rows, :] + norm_pull(state_ref[rows, :], gain_ref[1:2, :], grad)
        dstate_ref[rows, :] = total
        dsb[rows, :] = total.astype(BF)
    copies[0].wait()

    def mix_back(j):
        dmix[:, pl.ds(j, TILE)] = dot(dsb[...], wo[pl.ds(j, TILE), :], NT).astype(BF)

    tiles_of(model, mix_back)

    @pl.loop(0, model // PAIR)
    def _(h):
        keys = pl.ds(pl.multiple_of(h * PAIR, PAIR), PAIR)
        vals = pl.ds(pl.multiple_of(model + h * PAIR, PAIR), PAIR)
        grad = dmix[:, keys]
        grad_2 = stacked(grad)
        grad_f = grad.astype(F32)
        scores[...] = dot(grad_2, pairs_ref[:, vals], NT)
        deltas = lane_sums(grad_f * mix_ref[:, keys].astype(F32))
        own_dots = lane_sums(grad_f * own_ref[:, vals].astype(F32))
        for s in range(2):
            for i in range(0, cells, CHUNK):
                rows = pl.ds(s * cells + i, CHUNK)
                ds[rows, :] = (
                    wts_ref[h, rows, :].astype(F32)
                    * (scores[rows, :] - deltas[s][i : i + CHUNK])
                ).astype(BF)
        lanes = iota((cells, PAIR), 1) < HALF
        weight = ow_ref[:, keys].astype(F32)
        own_grad = weight * jnp.where(
            lanes, own_dots[0] - deltas[0], own_dots[1] - deltas[1]
        )
        q = q_ref[:, keys]
        dq = merged(dot(ds[...], pairs_ref[:, keys])) + own_grad * own_ref[:, keys].astype(F32)
        dq_ref[:, keys] = (dq * HALF ** (-0.5)).astype(BF)
        down_ref[:, keys] = (own_grad * q.astype(F32)).astype(BF)
        down_ref[:, vals] = (weight * grad_f).astype(BF)
        dpairs[:, keys] = dot(stacked(q), ds[...], TN).T.astype(BF)
        dpairs[:, vals] = dot(grad_2, wts_ref[h], TN).T.astype(BF)

    copies[1].wait()

    def slot_back(j):
        slot_ref[:, pl.ds(j, TILE)] = dot(dpairs[...], wp[pl.ds(j, TILE), :], NT).astype(BF)

    tiles_of(model, slot_back)


def grid_back_kernel(
    grid_ref, dstate_ref, gain_ref, dq_ref, down_ref, wq_hbm, wp_hbm, out_ref, wq, wp, acc, sems
):
    copies = fetch([wq_hbm, wp_hbm], [wq, wp], sems)
    cells, model = grid_ref.shape
    for copy in copies:
        copy.wait()

    def back(j):
        acc[:, pl.ds(j, TILE)] = dot(dq_ref[...], wq[pl.ds(j, TILE), :], NT) + dot(
            down_ref[...], wp[pl.ds(j, TILE), :], NT
        )

    tiles_of(model, back)
    for rows in row_chunks(cells):
        grad = acc[rows, :].astype(BF).astype(F32)
        out_ref[rows, :] = (
            dstate_ref[rows, :]
            + norm_pull(grid_ref[rows, :].astype(F32), gain_ref[0:1, :], grad)
        ).astype(BF)


def ring(value, by):
    size = lax.axis_size("lon")
    return lax.ppermute(value, "lon", [(i, (i + by) % size) for i in range(size)])


def line(value, by):
    size = lax.axis_size("lat")
    pairs = [(i, i + by) for i in range(size) if 0 <= i + by < size]
    return lax.ppermute(value, "lat", pairs)


def key_places(rows_lat, rows_lon):
    places = [(r, c) for r in range(rows_lat) for c in range(rows_lon)]
    places += [(r, c) for r in range(-RADIUS, 0) for c in range(rows_lon)]
    places += [(rows_lat + r, c) for r in range(RADIUS) for c in range(rows_lon)]
    ext = list(places)
    tall = range(-RADIUS, rows_lat + RADIUS)
    places += [(r, c) for r in tall for c in range(-RADIUS, 0)]
    places += [(r, rows_lon + c) for r in tall for c in range(RADIUS)]
    return np.array(places), ext


def per_device(
    grid_state, observations, obs_tile, obs_cell, cotangent, norm_gains,
    w_cross_query, w_cross_pairs, w_cross_out, w_near_proj, w_near_out, w_up, w_down,
):
    rows_lat, rows_lon, model = grid_state.shape
    lat_count = lax.axis_size("lat")
    devices = lat_count * lax.axis_size("lon")
    rows_obs = observations.shape[0]
    cap = max(2, 2 * rows_obs // devices)
    slots = devices * cap
    cells = rows_lat * rows_lon
    ff = w_up.shape[1]
    pairs_n = model // PAIR
    rim = RADIUS * rows_lon
    side = RADIUS * (rows_lat + 2 * RADIUS)
    places, ext_places = key_places(rows_lat, rows_lon)
    keys_n = len(places)
    keys_all = -(-keys_n // 256) * 256
    spot = {place: i for i, place in enumerate(ext_places)}
    tall = range(-RADIUS, rows_lat + RADIUS)
    select = np.zeros((2 * side, len(ext_places)), np.float32)
    for i, r in enumerate(tall):
        for c in range(RADIUS):
            select[i * RADIUS + c, spot[(r, c)]] = 1.0
            select[side + i * RADIUS + c, spot[(r, rows_lon - RADIUS + c)]] = 1.0
    select = jnp.asarray(select.astype(jnp.bfloat16))
    base = np.full((cells, keys_all), LOW_SCORE, np.float32)
    own_rows, own_cols = places[:cells, 0], places[:cells, 1]
    allowed = (np.abs(places[None, :, 0] - own_rows[:, None]) <= RADIUS) & (
        np.abs(places[None, :, 1] - own_cols[:, None]) <= RADIUS
    )
    base[:, :keys_n][allowed] = 0.0
    base = jnp.asarray(base.astype(jnp.bfloat16))
    key_rows = np.zeros((8, keys_all), np.int32)
    key_rows[:, :keys_n] = places[None, :, 0]
    key_lat = jnp.asarray(key_rows) + lax.axis_index("lat") * rows_lat
    inside = jnp.where((key_lat >= 0) & (key_lat < rows_lat * lat_count), 0.0, LOW_SCORE)
    inside = inside.astype(F32)

    dma = pltpu.SemaphoreType.DMA
    vm = pltpu.VMEM
    flat = grid_state.reshape(cells, model)
    cot = cotangent.reshape(cells, model)

    payload, placing = call(
        functools.partial(place_kernel, devices=devices, cap=cap, wide=rows_lon),
        (obs_tile, obs_cell, observations), "vvv",
        [((slots, model + 128), BF), ((rows_obs, slots), BF)], [],
        2 * rows_obs * slots * model, "place",
    )
    arrived = lax.all_to_all(
        payload.reshape(devices, cap, model + 128), ("lat", "lon"), 0, 0, tiled=True
    ).reshape(slots, model + 128)
    q_c, own_pairs, dhid = call(
        grid_kernel,
        (flat, cot, norm_gains, w_cross_query, w_cross_pairs, w_down), "vvvhhh",
        [((cells, model), BF), ((cells, 2 * model), BF), ((cells, ff), BF)],
        [vm((cells, model), BF), vm((model, model), BF), vm((model, 2 * model), BF),
         vm((ff, model), BF), dma((3,))],
        2 * cells * model * (3 * model + ff), "grid_proj",
    )
    state, normal, slot_pairs, cross_w, cross_mix, own_w = call(
        functools.partial(cross_kernel, wide=rows_lon),
        (arrived, flat, q_c, own_pairs, norm_gains, w_cross_pairs, w_cross_out), "vvvvvhh",
        [((cells, model), F32), ((cells, model), BF), ((slots, 2 * model), BF),
         ((pairs_n, 2 * cells, slots), BF), ((cells, model), BF), ((cells, model), BF)],
        [vm((model, 2 * model), BF), vm((model, model), BF), vm((2 * cells, slots), F32),
         vm((cells, slots), F32), dma((2,))],
        2 * slots * model * 2 * model * 2, "cross",
    )
    south = line(normal[:rim], -1)
    north = line(normal[cells - rim :], 1)
    q_n, kv_own = call(
        near_own_kernel, (normal, w_near_proj), "vh",
        [((cells, model), BF), ((cells, 2 * model), BF)],
        [vm((model, 3 * model), BF), dma((2,))],
        2 * cells * model * 3 * model, "near_own",
    )
    west_send, east_send = call(
        rim_kernel, (normal, north, south, select), "vvvv",
        [((side, model), BF), ((side, model), BF)],
        [vm((cells + 2 * rim, model), BF)],
        2 * 2 * side * 2 * cells * model, "rim",
    )
    east = ring(west_send, -1)
    west = ring(east_send, 1)
    kv_rows = call(
        near_rows_kernel, (north, south, w_near_proj), "vvh",
        [((2 * rim, 2 * model), BF)],
        [vm((2 * rim, model), BF), vm((model, 2 * model), BF), dma((1,))],
        2 * 2 * rim * model * 2 * model, "near_rows",
    )
    after, hidden, dwest, deast, dqkv, drows, dafter = call(
        near_kernel,
        (q_n, west, east, base, inside, state, cot, dhid, norm_gains, kv_own, kv_rows,
         w_near_proj, w_near_out, w_up), "vvvvvvvvvhhhhh",
        [((cells, model), F32), ((cells, ff), BF), ((side, model), BF), ((side, model), BF),
         ((cells, 3 * model), BF), ((2 * rim, 2 * model), BF), ((cells, model), F32)],
        [vm((model, 2 * model), BF), vm((model, model), BF), vm((model, ff), BF),
         vm((keys_all, 2 * model), BF), vm((keys_all, 2 * model), BF),
         vm((2 * side, model), BF), vm((pairs_n, 2 * cells, keys_all), BF),
         vm((2 * cells, keys_all), F32), vm((2 * cells, keys_all), BF),
         vm((cells, keys_all), F32), vm((cells, model), BF), vm((cells, model), BF),
         vm((cells, ff), BF), vm((cells, model), F32), vm((cells, model), BF),
         vm((cells, model), BF), dma((5,))],
        2e10, "near",
    )
    from_east = ring(dwest, -1)
    from_west = ring(deast, 1)
    dn_ext = call(
        near_back_kernel, (dqkv, drows, w_near_proj), "vvh",
        [((cells + 2 * rim, model), F32)],
        [vm((model, 3 * model), BF), dma((1,))],
        2 * cells * model * 5 * model, "near_back",
    )
    dn_own, dnorth, dsouth = call(
        fold_kernel, (dn_ext, from_east, from_west, select), "vvvv",
        [((cells, model), F32), ((rim, model), BF), ((rim, model), BF)],
        [vm((2 * side, model), BF)],
        2 * 2 * side * 2 * cells * model, "fold",
    )
    from_south = line(dnorth, -1)
    from_north = line(dsouth, 1)
    encoded = call(
        encode_kernel, (after, hidden, w_down), "vvh", [((cells, model), BF)],
        [vm((ff, model), BF), dma((1,))], 2 * cells * model * ff, "encode",
    )
    dstate, slot_grads, dq, down = call(
        cross_back_kernel,
        (dn_own, from_north, from_south, state, dafter, norm_gains, q_c, own_pairs, slot_pairs,
         cross_w, cross_mix, own_w, w_cross_pairs, w_cross_out), "vvvvvvvvvvvvhh",
        [((cells, model), F32), ((slots, model), BF), ((cells, model), BF),
         ((cells, 2 * model), BF)],
        [vm((model, 2 * model), BF), vm((model, model), BF), vm((cells, model), BF),
         vm((cells, model), BF), vm((slots, 2 * model), BF), vm((2 * cells, slots), F32),
         vm((2 * cells, slots), BF), dma((2,))],
        2 * slots * model * 2 * model * 2, "cross_back",
    )
    returned = lax.all_to_all(
        slot_grads.reshape(devices, cap, model), ("lat", "lon"), 0, 0, tiled=True
    ).reshape(slots, model)
    grid_grad = call(
        grid_back_kernel,
        (flat, dstate, norm_gains, dq, down, w_cross_query, w_cross_pairs), "vvvvvhh",
        [((cells, model), BF)],
        [vm((model, model), BF), vm((model, 2 * model), BF), vm((cells, model), F32), dma((2,))],
        2 * cells * model * 3 * model, "grid_back",
    )
    obs_grad = dot(placing, returned).astype(BF)
    shape = (rows_lat, rows_lon, model)
    return encoded.reshape(shape), grid_grad.reshape(shape), obs_grad


def solution(mesh):
    return jax.shard_map(
        per_device,
        mesh=mesh,
        in_specs=(
            P("lat", "lon", None),
            P(("lat", "lon"), None),
            P(("lat", "lon"), None),
            P(("lat", "lon"), None),
            P("lat", "lon", None),
            P(), P(), P(), P(), P(), P(), P(), P(),
        ),
        out_specs=(P("lat", "lon", None), P("lat", "lon", None), P(("lat", "lon"), None)),
        check_vma=False,
    )
```

```python
import functools

import jax
import jax.numpy as jnp
import numpy as np
from jax import lax
from jax.experimental import pallas as pl
from jax.experimental.pallas import tpu as pltpu
from jax.sharding import PartitionSpec as P

HEADS = 16
RADIUS = 6
EPSILON = 1e-05
SPREAD = 32.0
LOW_SCORE = -1e30

BF = jnp.bfloat16
F32 = jnp.float32
NN = (((1,), (0,)), ((), ()))
NT = (((1,), (1,)), ((), ()))
TN = (((0,), (0,)), ((), ()))
CHUNK = 32
TILE = 1024
PAIR = 128
HALF = 64
SLACK_BYTES = 8 * 2**20
FEED_TILE = 512
GROUP = 2
GELU_C = 0.7978845608028654
GELU_A = 0.044715


def dot(left, right, dims=NN):
    return lax.dot_general(left, right, dims, preferred_element_type=F32)


def iota(shape, dim):
    return lax.broadcasted_iota(jnp.int32, shape, dim)


def tiles_of(count, body, tile=TILE):
    @pl.loop(0, count // tile)
    def _(i):
        body(pl.multiple_of(i * tile, tile))


def row_chunks(count):
    return [pl.ds(i, CHUNK) for i in range(0, count, CHUNK)]


def unit(values):
    center = values - jnp.mean(values, -1, keepdims=True)
    scale = lax.rsqrt(jnp.mean(center * center, -1, keepdims=True) + EPSILON)
    return center * scale, scale


def norm_pull(values, gain, grad):
    normed, scale = unit(values)
    inner = grad * gain
    return scale * (
        inner
        - jnp.mean(inner, -1, keepdims=True)
        - normed * jnp.mean(inner * normed, -1, keepdims=True)
    )


def head_masks():
    left = (iota((1, PAIR), 1) < HALF).astype(F32)
    return left.astype(BF), (1.0 - left).astype(BF)


def stacked(values):
    left, right = head_masks()
    return jnp.concatenate([values * left, values * right], axis=0)


def merged(values):
    count = values.shape[0] // 2
    lanes = iota((count, PAIR), 1) < HALF
    return jnp.where(lanes, values[:count], values[count:])


def lane_sums(values):
    lanes = iota(values.shape, 1) < HALF
    first = jnp.sum(jnp.where(lanes, values, 0.0), -1, keepdims=True)
    second = jnp.sum(jnp.where(lanes, 0.0, values), -1, keepdims=True)
    return first, second


def fetch(sources, targets, sems):
    copies = [
        pltpu.make_async_copy(source, target, sems.at[i])
        for i, (source, target) in enumerate(zip(sources, targets))
    ]
    for copy in copies:
        copy.start()
    return copies


def call(body, ins, kinds, outs, scratch, flops, name):
    any_spec = pl.BlockSpec(memory_space=pl.ANY)
    vmem_spec = pl.BlockSpec(memory_space=pltpu.VMEM)
    moved = sum(x.size * x.dtype.itemsize for x in ins)
    moved += sum(int(np.prod(s)) * jnp.dtype(t).itemsize for s, t in outs)
    held = sum(x.size * x.dtype.itemsize for x, k in zip(ins, kinds) if k == "v")
    held += sum(int(np.prod(s)) * jnp.dtype(t).itemsize for s, t in outs)
    for item in scratch:
        if jnp.issubdtype(item.dtype, jnp.floating):
            held += int(np.prod(item.shape)) * jnp.dtype(item.dtype).itemsize
    single = len(outs) == 1
    shapes = [jax.ShapeDtypeStruct(s, t) for s, t in outs]
    return pl.pallas_call(
        body,
        name=name,
        out_shape=shapes[0] if single else shapes,
        in_specs=[any_spec if k == "h" else vmem_spec for k in kinds],
        out_specs=vmem_spec if single else [vmem_spec] * len(outs),
        scratch_shapes=scratch,
        compiler_params=pltpu.CompilerParams(vmem_limit_bytes=held + SLACK_BYTES),
        cost_estimate=pl.CostEstimate(
            flops=int(flops), bytes_accessed=int(moved), transcendentals=0
        ),
    )(*ins)


def place_kernel(tile_ref, cell_ref, obs_ref, pay_ref, place_ref, *, devices, cap, wide):
    rows, model = obs_ref.shape
    slots = devices * cap
    tile = tile_ref[...]
    member = tile == iota((devices, rows), 0)
    earlier = (iota((rows, rows), 0) < iota((rows, rows), 1)).astype(F32).astype(BF)
    before = dot(member.astype(F32).astype(BF), earlier)
    rank = jnp.sum(jnp.where(member, before, 0.0), 0, keepdims=True).astype(jnp.int32)
    slot = tile * cap + rank
    placing = (slot == iota((slots, rows), 0)).astype(F32).astype(BF)
    place_ref[...] = placing
    cell = cell_ref[...]
    shift = wide.bit_length() - 1
    line_no = iota((128, rows), 0)
    codes = jnp.where(
        line_no == 0, (cell >> shift) + 1, jnp.where(line_no == 1, (cell & (wide - 1)) + 1, 0)
    )
    code_rows = dot(placing, codes.astype(F32).astype(BF), NT).astype(BF)
    pay_ref[:, :, model:] = code_rows.reshape(devices, cap, 128)
    moved = dot(placing, obs_ref[...]).astype(BF)
    pay_ref[:, :, :model] = moved.reshape(devices, cap, model)


def grid_kernel(
    grid_ref, cot_ref, gain_ref, wq_hbm, wp_hbm, wd_hbm, q_ref, own_ref, dh_ref,
    nrm, wq, wp, wd, sems,
):
    copies = fetch([wq_hbm, wp_hbm, wd_hbm], [wq, wp, wd], sems)
    cells, model = grid_ref.shape
    for rows in row_chunks(cells):
        normed, _ = unit(grid_ref[rows, :].astype(F32))
        nrm[rows, :] = (normed * gain_ref[0:1, :]).astype(BF)
    copies[0].wait()

    def query(j):
        q_ref[:, pl.ds(j, TILE)] = (
            dot(nrm[...], wq[:, pl.ds(j, TILE)]) * HALF ** (-0.5)
        ).astype(BF)

    tiles_of(model, query)
    copies[1].wait()

    def own(j):
        own_ref[:, pl.ds(j, TILE)] = dot(nrm[...], wp[:, pl.ds(j, TILE)]).astype(BF)

    tiles_of(2 * model, own)
    copies[2].wait()

    def hidden(j):
        dh_ref[:, pl.ds(j, TILE)] = dot(cot_ref[...], wd[pl.ds(j, TILE), :], NT).astype(BF)

    tiles_of(dh_ref.shape[1], hidden)


def cross_kernel(
    arr_ref, grid_ref, q_ref, own_ref, gain_ref, wp_hbm, wo_hbm,
    state_ref, top_ref, bottom_ref, pairs_ref, wts_ref, mix_ref, ow_ref,
    arr, wp, wo, scores, bias, sems, *, wide,
):
    copies = fetch([wp_hbm, wo_hbm], [wp, wo], sems)
    cells, model = grid_ref.shape
    rim = top_ref.shape[0]
    slots = arr.shape[0]
    arr[...] = arr_ref[...].reshape(arr.shape)
    pick = (iota((8, 128), 0) == iota((8, 128), 1)).astype(F32).astype(BF)
    codes = dot(pick, arr[:, model:], NT)
    cell = iota((cells, slots), 0)
    shift = wide.bit_length() - 1
    row_gap = (cell >> shift).astype(F32) - (codes[0:1] - 1.0)
    col_gap = (cell & (wide - 1)).astype(F32) - (codes[1:2] - 1.0)
    near = -(row_gap * row_gap + col_gap * col_gap) * (1.0 / SPREAD)
    bias[...] = jnp.where(codes[0:1] > 0.5, near, LOW_SCORE)
    copies[0].wait()

    def project(j):
        pairs_ref[:, pl.ds(j, TILE)] = dot(
            arr[:, :model], wp[:, pl.ds(j, TILE)]
        ).astype(BF)

    tiles_of(2 * model, project)

    def soften(h, k, own_scores):
        own_weights = []
        for side in range(2):
            parts = []
            for i in range(0, cells, CHUNK):
                own_score = own_scores[side][i : i + CHUNK]
                x = scores[k, pl.ds(side * cells + i, CHUNK), :] + bias[pl.ds(i, CHUNK), :]
                peak = jnp.maximum(jnp.max(x, -1, keepdims=True), own_score)
                x = jnp.exp(x - peak)
                own_weight = jnp.exp(own_score - peak)
                inverse = 1.0 / (jnp.sum(x, -1, keepdims=True) + own_weight)
                wts_ref[h, pl.ds(side * cells + i, CHUNK), :] = (x * inverse).astype(BF)
                parts.append(own_weight * inverse)
            own_weights.append(jnp.concatenate(parts, axis=0))
        lanes = iota((cells, PAIR), 1) < HALF
        return jnp.where(lanes, own_weights[0], own_weights[1]).astype(BF)

    @pl.loop(0, model // (PAIR * GROUP))
    def _(g):
        heads, own_scores, weights = [], [], []
        for k in range(GROUP):
            h = g * GROUP + k
            keys = pl.ds(pl.multiple_of(h * PAIR, PAIR), PAIR)
            vals = pl.ds(pl.multiple_of(model + h * PAIR, PAIR), PAIR)
            heads.append((h, keys, vals))
            q = q_ref[:, keys]
            scores[k] = dot(stacked(q), pairs_ref[:, keys], NT)
            own_scores.append(lane_sums(q.astype(F32) * own_ref[:, keys].astype(F32)))
        for k, (h, keys, vals) in enumerate(heads):
            weights.append(soften(h, k, own_scores[k]))
            ow_ref[:, keys] = weights[k]
        for k, (h, keys, vals) in enumerate(heads):
            mix = merged(dot(wts_ref[h], pairs_ref[:, vals]))
            mix_ref[:, keys] = (
                mix + weights[k].astype(F32) * own_ref[:, vals].astype(F32)
            ).astype(BF)

    copies[1].wait()

    def project_out(j):
        state_ref[:, pl.ds(j, TILE)] = grid_ref[:, pl.ds(j, TILE)].astype(F32) + dot(
            mix_ref[...], wo[:, pl.ds(j, TILE)]
        )

    tiles_of(model, project_out)
    for i in range(0, cells, CHUNK):
        normed, _ = unit(state_ref[pl.ds(i, CHUNK), :])
        normed = (normed * gain_ref[1:2, :]).astype(BF)
        if i < rim:
            top_ref[pl.ds(i, CHUNK), :] = normed
        else:
            bottom_ref[pl.ds(i - rim, CHUNK), :] = normed


def near_own_kernel(top_ref, bottom_ref, w_hbm, q_ref, kv_ref, nrm, w, sems):
    cells, model = nrm.shape
    rim = top_ref.shape[0]
    copies = fetch(
        [w_hbm.at[:, pl.ds(0, model)], w_hbm.at[:, pl.ds(model, 2 * model)]],
        [w.at[:, pl.ds(0, model)], w.at[:, pl.ds(model, 2 * model)]],
        sems,
    )
    nrm[pl.ds(0, rim), :] = top_ref[...]
    nrm[pl.ds(rim, rim), :] = bottom_ref[...]
    copies[0].wait()

    def query(j):
        q_ref[:, pl.ds(j, TILE)] = (
            dot(nrm[...], w[:, pl.ds(j, TILE)]) * HALF ** (-0.5)
        ).astype(BF)

    tiles_of(model, query)
    copies[1].wait()

    def pairs(j):
        kv_ref[:, pl.ds(j, TILE)] = dot(
            nrm[...], w[:, pl.ds(pl.multiple_of(model + j, TILE), TILE)]
        ).astype(BF)

    tiles_of(2 * model, pairs)


def rim_kernel(
    top_ref, bottom_ref, north_ref, south_ref, sel_ref, _, west_ref, east_ref, ext
):
    rim, model = north_ref.shape
    for i, part in enumerate((top_ref, bottom_ref, north_ref, south_ref)):
        ext[pl.ds(i * rim, rim), :] = part[...]
    side = west_ref.shape[0]

    def pick(j):
        both = dot(sel_ref[...], ext[:, pl.ds(j, TILE)]).astype(BF)
        west_ref[:, pl.ds(j, TILE)] = both[:side]
        east_ref[:, pl.ds(j, TILE)] = both[side:]

    tiles_of(model, pick)


def near_rows_kernel(north_ref, south_ref, w_hbm, kv_ref, x, w, sems):
    rim, model = north_ref.shape
    copies = fetch([w_hbm.at[:, pl.ds(model, 2 * model)]], [w], sems)
    x[pl.ds(0, rim), :] = north_ref[...]
    x[pl.ds(rim, rim), :] = south_ref[...]
    copies[0].wait()

    def pairs(j):
        kv_ref[:, pl.ds(j, TILE)] = dot(x[...], w[:, pl.ds(j, TILE)]).astype(BF)

    tiles_of(2 * model, pairs)


def near_kernel(
    q_ref, west_ref, east_ref, base_ref, inside_ref, state_ref, cot_ref, dh_ref, gain_ref,
    kvo_hbm, kvr_hbm, wn_hbm, wo_hbm, wu_hbm,
    after_ref, hid_ref, dwest_ref, deast_ref, dqkv_ref, drows_ref, dafter_ref,
    wkv, wo, wu, kv, dkv, x, wts, scores, ds, bias, mix, nrm, du, acc, dab, dmix, sems,
):
    cells, model = state_ref.shape
    keys_all = kv.shape[0]
    ext = 2 * cells
    side = west_ref.shape[0]
    ends = ext + 2 * side
    copies = fetch(
        [kvo_hbm, kvr_hbm, wn_hbm.at[:, pl.ds(model, 2 * model)], wo_hbm, wu_hbm],
        [kv.at[pl.ds(0, cells), :], kv.at[pl.ds(cells, cells), :], wkv, wo, wu],
        sems,
    )
    x[pl.ds(0, side), :] = west_ref[...]
    x[pl.ds(side, side), :] = east_ref[...]
    kv[pl.ds(ends, keys_all - ends), :] = jnp.zeros((keys_all - ends, 2 * model), BF)
    bias[...] = base_ref[...].astype(F32) + inside_ref[0:1, :]
    copies[0].wait()
    copies[1].wait()
    copies[2].wait()

    def project(j):
        kv[pl.ds(ext, 2 * side), pl.ds(j, TILE)] = dot(
            x[...], wkv[:, pl.ds(j, TILE)]
        ).astype(BF)

    tiles_of(2 * model, project)

    @pl.loop(0, model // (PAIR * GROUP))
    def _(g):
        heads = []
        for k in range(GROUP):
            h = g * GROUP + k
            keys = pl.ds(pl.multiple_of(h * PAIR, PAIR), PAIR)
            vals = pl.ds(pl.multiple_of(model + h * PAIR, PAIR), PAIR)
            heads.append((h, keys, vals))
            scores[k] = dot(stacked(q_ref[:, keys]), kv[:, keys], NT)
        for k, (h, keys, vals) in enumerate(heads):
            for start in range(0, 2 * cells, CHUNK):
                rows = pl.ds(start, CHUNK)
                v = scores[k, rows, :] + bias[pl.ds(start % cells, CHUNK), :]
                v = jnp.exp(v - jnp.max(v, -1, keepdims=True))
                inverse = 1.0 / jnp.sum(v, -1, keepdims=True)
                wts[h, rows, :] = (v * inverse).astype(BF)
        for k, (h, keys, vals) in enumerate(heads):
            mix[:, keys] = merged(dot(wts[h], kv[:, vals])).astype(BF)

    copies[3].wait()

    def project_out(j):
        after_ref[:, pl.ds(j, TILE)] = state_ref[:, pl.ds(j, TILE)] + dot(
            mix[...], wo[:, pl.ds(j, TILE)]
        )

    tiles_of(model, project_out)
    for rows in row_chunks(cells):
        normed, _ = unit(after_ref[rows, :])
        nrm[rows, :] = (normed * gain_ref[2:3, :]).astype(BF)
    copies[4].wait()

    def feed(j):
        cols = pl.ds(j, FEED_TILE)
        u = dot(nrm[...], wu[:, cols])
        square = u * u
        t = jnp.tanh(GELU_C * (u + GELU_A * (square * u)))
        half = 0.5 * (1.0 + t)
        hid_ref[:, cols] = (u * half).astype(BF)
        slope = half + (0.5 * GELU_C) * u * (1.0 - t * t) * (1.0 + 3.0 * GELU_A * square)
        du[:, cols] = (dh_ref[:, cols].astype(F32) * slope).astype(BF)

    tiles_of(du.shape[1], feed, FEED_TILE)

    def feed_back(j):
        acc[:, pl.ds(j, TILE)] = dot(du[...], wu[pl.ds(j, TILE), :], NT)

    tiles_of(model, feed_back)
    for rows in row_chunks(cells):
        grad = acc[rows, :].astype(BF).astype(F32)
        total = cot_ref[rows, :].astype(F32) + norm_pull(
            after_ref[rows, :], gain_ref[2:3, :], grad
        )
        dafter_ref[rows, :] = total
        dab[rows, :] = total.astype(BF)

    def mix_back(j):
        dmix[:, pl.ds(j, TILE)] = dot(dab[...], wo[pl.ds(j, TILE), :], NT).astype(BF)

    tiles_of(model, mix_back)

    @pl.loop(0, model // (PAIR * GROUP))
    def _(g):
        heads, deltas = [], []
        for k in range(GROUP):
            h = g * GROUP + k
            keys = pl.ds(pl.multiple_of(h * PAIR, PAIR), PAIR)
            vals = pl.ds(pl.multiple_of(model + h * PAIR, PAIR), PAIR)
            heads.append((h, keys, vals))
            grad = dmix[:, keys]
            scores[k] = dot(stacked(grad), kv[:, vals], NT)
            deltas.append(lane_sums(grad.astype(F32) * mix[:, keys].astype(F32)))
        for k, (h, keys, vals) in enumerate(heads):
            for s in range(2):
                for i in range(0, cells, CHUNK):
                    rows = pl.ds(s * cells + i, CHUNK)
                    ds[k, rows, :] = (
                        wts[h, rows, :].astype(F32)
                        * (scores[k, rows, :] - deltas[k][s][i : i + CHUNK])
                    ).astype(BF)
        for k, (h, keys, vals) in enumerate(heads):
            dq = merged(dot(ds[k], kv[:, keys])) * HALF ** (-0.5)
            dqkv_ref[:, keys] = dq.astype(BF)
            dkv[:, keys] = dot(stacked(q_ref[:, keys]), ds[k], TN).T.astype(BF)
            dkv[:, vals] = dot(stacked(dmix[:, keys]), wts[h], TN).T.astype(BF)

    def rim_back(j):
        both = dot(dkv[pl.ds(ext, 2 * side), :], wkv[pl.ds(j, TILE), :], NT).astype(BF)
        dwest_ref[:, pl.ds(j, TILE)] = both[:side]
        deast_ref[:, pl.ds(j, TILE)] = both[side:]

    tiles_of(model, rim_back)
    dqkv_ref[:, pl.ds(model, 2 * model)] = dkv[pl.ds(0, cells), :]
    drows_ref[...] = dkv[pl.ds(cells, cells), :]


def encode_kernel(after_ref, hid_ref, wd_hbm, _, enc_ref, wd, sems):
    copies = fetch([wd_hbm], [wd], sems)
    copies[0].wait()

    def down(j):
        enc_ref[:, pl.ds(j, TILE)] = (
            after_ref[:, pl.ds(j, TILE)] + dot(hid_ref[...], wd[:, pl.ds(j, TILE)])
        ).astype(BF)

    tiles_of(after_ref.shape[1], down)


def rows_back_kernel(drows_ref, w_hbm, dn_ref, w, sems):
    model = dn_ref.shape[1]
    copies = fetch([w_hbm.at[:, pl.ds(model, 2 * model)]], [w], sems)
    copies[0].wait()

    def back(j):
        dn_ref[:, pl.ds(j, TILE)] = dot(drows_ref[...], w[pl.ds(j, TILE), :], NT)

    tiles_of(model, back)


def fold_kernel(dn_ref, from_east_ref, from_west_ref, sel_ref, north_ref, south_ref, x):
    rim, model = north_ref.shape
    side = from_east_ref.shape[0]
    x[pl.ds(0, side), :] = from_west_ref[...]
    x[pl.ds(side, side), :] = from_east_ref[...]

    def fold(j):
        cols = pl.ds(j, TILE)
        total = (dn_ref[:, cols] + dot(sel_ref[...], x[:, cols], TN)).astype(BF)
        north_ref[:, cols] = total[:rim]
        south_ref[:, cols] = total[rim:]

    tiles_of(model, fold)


def own_back_kernel(
    dqkv_ref, from_east_ref, from_west_ref, sel_ref, w_hbm, _, dn_ref, x, w, sems
):
    copies = fetch([w_hbm], [w], sems)
    side = from_east_ref.shape[0]
    x[pl.ds(0, side), :] = from_west_ref[...]
    x[pl.ds(side, side), :] = from_east_ref[...]
    copies[0].wait()

    def back(j):
        cols = pl.ds(j, TILE)
        dn_ref[:, cols] = dot(dqkv_ref[...], w[cols, :], NT) + dot(
            sel_ref[...], x[:, cols], TN
        )

    tiles_of(dn_ref.shape[1], back)


def cross_back_kernel(
    dn_ref, north_ref, south_ref, state_ref, dafter_ref, gain_ref, q_ref, own_ref, pairs_ref,
    wts_ref, mix_ref, ow_ref, wp_hbm, wo_hbm, _,
    dstate_ref, slot_ref, dq_ref, down_ref,
    wp, wo, dsb, dmix, dpairs, scores, ds, sems,
):
    copies = fetch([wo_hbm, wp_hbm], [wo, wp], sems)
    cells, model = state_ref.shape
    rim = north_ref.shape[0]
    for i in range(0, cells, CHUNK):
        rows = pl.ds(i, CHUNK)
        other = north_ref[rows, :] if i < rim else south_ref[pl.ds(i - rim, CHUNK), :]
        grad = (dn_ref[rows, :] + other.astype(F32)).astype(BF).astype(F32)
        total = dafter_ref[rows, :] + norm_pull(state_ref[rows, :], gain_ref[1:2, :], grad)
        dstate_ref[rows, :] = total
        dsb[rows, :] = total.astype(BF)
    copies[0].wait()

    def mix_back(j):
        dmix[:, pl.ds(j, TILE)] = dot(dsb[...], wo[pl.ds(j, TILE), :], NT).astype(BF)

    tiles_of(model, mix_back)

    @pl.loop(0, model // (PAIR * GROUP))
    def _(g):
        heads, deltas, own_dots = [], [], []
        for k in range(GROUP):
            h = g * GROUP + k
            keys = pl.ds(pl.multiple_of(h * PAIR, PAIR), PAIR)
            vals = pl.ds(pl.multiple_of(model + h * PAIR, PAIR), PAIR)
            heads.append((h, keys, vals))
            grad = dmix[:, keys]
            grad_f = grad.astype(F32)
            scores[k] = dot(stacked(grad), pairs_ref[:, vals], NT)
            deltas.append(lane_sums(grad_f * mix_ref[:, keys].astype(F32)))
            own_dots.append(lane_sums(grad_f * own_ref[:, vals].astype(F32)))
        for k, (h, keys, vals) in enumerate(heads):
            for s in range(2):
                for i in range(0, cells, CHUNK):
                    rows = pl.ds(s * cells + i, CHUNK)
                    ds[k, rows, :] = (
                        wts_ref[h, rows, :].astype(F32)
                        * (scores[k, rows, :] - deltas[k][s][i : i + CHUNK])
                    ).astype(BF)
        for k, (h, keys, vals) in enumerate(heads):
            lanes = iota((cells, PAIR), 1) < HALF
            weight = ow_ref[:, keys].astype(F32)
            own_grad = weight * jnp.where(
                lanes, own_dots[k][0] - deltas[k][0], own_dots[k][1] - deltas[k][1]
            )
            q = q_ref[:, keys]
            grad = dmix[:, keys]
            dq = merged(dot(ds[k], pairs_ref[:, keys]))
            dq = dq + own_grad * own_ref[:, keys].astype(F32)
            dq_ref[:, keys] = (dq * HALF ** (-0.5)).astype(BF)
            down_ref[:, keys] = (own_grad * q.astype(F32)).astype(BF)
            down_ref[:, vals] = (weight * grad.astype(F32)).astype(BF)
            dpairs[:, keys] = dot(stacked(q), ds[k], TN).T.astype(BF)
            dpairs[:, vals] = dot(stacked(grad), wts_ref[h], TN).T.astype(BF)

    copies[1].wait()

    def slot_back(j):
        grads = dot(dpairs[...], wp[pl.ds(j, TILE), :], NT).astype(BF)
        slot_ref[:, :, pl.ds(j, TILE)] = grads.reshape(slot_ref.shape[:2] + (TILE,))

    tiles_of(model, slot_back)


def grid_back_kernel(
    grid_ref, dstate_ref, gain_ref, dq_ref, down_ref, wq_hbm, wp_hbm, out_ref, wq, wp, acc, sems
):
    copies = fetch([wq_hbm, wp_hbm], [wq, wp], sems)
    cells, model = grid_ref.shape
    for copy in copies:
        copy.wait()

    def back(j):
        acc[:, pl.ds(j, TILE)] = dot(dq_ref[...], wq[pl.ds(j, TILE), :], NT) + dot(
            down_ref[...], wp[pl.ds(j, TILE), :], NT
        )

    tiles_of(model, back)
    for rows in row_chunks(cells):
        grad = acc[rows, :].astype(BF).astype(F32)
        out_ref[rows, :] = (
            dstate_ref[rows, :]
            + norm_pull(grid_ref[rows, :].astype(F32), gain_ref[0:1, :], grad)
        ).astype(BF)


def ring(value, by):
    size = lax.axis_size("lon")
    return lax.ppermute(value, "lon", [(i, (i + by) % size) for i in range(size)])


def line(value, by):
    size = lax.axis_size("lat")
    pairs = [(i, i + by) for i in range(size) if 0 <= i + by < size]
    return lax.ppermute(value, "lat", pairs)


def key_places(rows_lat, rows_lon):
    places = [(r, c) for r in range(rows_lat) for c in range(rows_lon)]
    places += [(r, c) for r in range(-RADIUS, 0) for c in range(rows_lon)]
    places += [(rows_lat + r, c) for r in range(RADIUS) for c in range(rows_lon)]
    ext = list(places)
    tall = range(-RADIUS, rows_lat + RADIUS)
    places += [(r, c) for r in tall for c in range(-RADIUS, 0)]
    places += [(r, rows_lon + c) for r in tall for c in range(RADIUS)]
    return np.array(places), ext


def per_device(
    grid_state, observations, obs_tile, obs_cell, cotangent, norm_gains,
    w_cross_query, w_cross_pairs, w_cross_out, w_near_proj, w_near_out, w_up, w_down,
):
    rows_lat, rows_lon, model = grid_state.shape
    lat_count = lax.axis_size("lat")
    devices = lat_count * lax.axis_size("lon")
    rows_obs = observations.shape[0]
    cap = max(2, 2 * rows_obs // devices)
    slots = devices * cap
    cells = rows_lat * rows_lon
    ff = w_up.shape[1]
    pairs_n = model // PAIR
    rim = RADIUS * rows_lon
    side = RADIUS * (rows_lat + 2 * RADIUS)
    places, ext_places = key_places(rows_lat, rows_lon)
    keys_n = len(places)
    keys_all = -(-keys_n // 256) * 256
    spot = {place: i for i, place in enumerate(ext_places)}
    tall = range(-RADIUS, rows_lat + RADIUS)
    select = np.zeros((2 * side, len(ext_places)), np.float32)
    for i, r in enumerate(tall):
        for c in range(RADIUS):
            select[i * RADIUS + c, spot[(r, c)]] = 1.0
            select[side + i * RADIUS + c, spot[(r, rows_lon - RADIUS + c)]] = 1.0
    select = select.astype(jnp.bfloat16)
    base = np.full((cells, keys_all), LOW_SCORE, np.float32)
    own_rows, own_cols = places[:cells, 0], places[:cells, 1]
    allowed = (np.abs(places[None, :, 0] - own_rows[:, None]) <= RADIUS) & (
        np.abs(places[None, :, 1] - own_cols[:, None]) <= RADIUS
    )
    base[:, :keys_n][allowed] = 0.0
    base = jnp.asarray(base.astype(jnp.bfloat16))
    key_rows = np.zeros((8, keys_all), np.int32)
    key_rows[:, :keys_n] = places[None, :, 0]
    key_lat = jnp.asarray(key_rows) + lax.axis_index("lat") * rows_lat
    inside = jnp.where((key_lat >= 0) & (key_lat < rows_lat * lat_count), 0.0, LOW_SCORE)
    inside = inside.astype(F32)

    dma = pltpu.SemaphoreType.DMA
    vm = pltpu.VMEM
    flat = grid_state.reshape(cells, model)
    cot = cotangent.reshape(cells, model)

    payload, placing = call(
        functools.partial(place_kernel, devices=devices, cap=cap, wide=rows_lon),
        (obs_tile.reshape(1, rows_obs), obs_cell.reshape(1, rows_obs), observations), "vvv",
        [((devices, cap, model + 128), BF), ((slots, rows_obs), BF)], [],
        2 * rows_obs * slots * model, "place",
    )
    arrived = lax.all_to_all(payload, ("lat", "lon"), 0, 0, tiled=True)
    q_c, own_pairs, dhid = call(
        grid_kernel,
        (flat, cot, norm_gains, w_cross_query, w_cross_pairs, w_down), "vvvhhh",
        [((cells, model), BF), ((cells, 2 * model), BF), ((cells, ff), BF)],
        [vm((cells, model), BF), vm((model, model), BF), vm((model, 2 * model), BF),
         vm((ff, model), BF), dma((3,))],
        2 * cells * model * (3 * model + ff), "grid_proj",
    )
    state, top, bottom, slot_pairs, cross_w, cross_mix, own_w = call(
        functools.partial(cross_kernel, wide=rows_lon),
        (arrived, flat, q_c, own_pairs, norm_gains, w_cross_pairs, w_cross_out), "vvvvvhh",
        [((cells, model), F32), ((rim, model), BF), ((rim, model), BF), ((slots, 2 * model), BF),
         ((pairs_n, 2 * cells, slots), BF), ((cells, model), BF), ((cells, model), BF)],
        [vm((slots, model + 128), BF), vm((model, 2 * model), BF), vm((model, model), BF),
         vm((GROUP, 2 * cells, slots), F32), vm((cells, slots), F32), dma((2,))],
        2 * slots * model * 2 * model * 2, "cross",
    )
    south = line(top, -1)
    north = line(bottom, 1)
    q_n, kv_own = call(
        near_own_kernel, (top, bottom, w_near_proj), "vvh",
        [((cells, model), BF), ((cells, 2 * model), BF)],
        [vm((cells, model), BF), vm((model, 3 * model), BF), dma((2,))],
        2 * cells * model * 3 * model, "near_own",
    )
    west_send, east_send = call(
        rim_kernel, (top, bottom, north, south, jnp.asarray(select), kv_own), "vvvvvh",
        [((side, model), BF), ((side, model), BF)],
        [vm((cells + 2 * rim, model), BF)],
        2 * 2 * side * 2 * cells * model, "rim",
    )
    east = ring(west_send, -1)
    west = ring(east_send, 1)
    kv_rows = call(
        near_rows_kernel, (north, south, w_near_proj), "vvh",
        [((2 * rim, 2 * model), BF)],
        [vm((2 * rim, model), BF), vm((model, 2 * model), BF), dma((1,))],
        2 * 2 * rim * model * 2 * model, "near_rows",
    )
    after, hidden, dwest, deast, dqkv, drows, dafter = call(
        near_kernel,
        (q_n, west, east, base, inside, state, cot, dhid, norm_gains, kv_own, kv_rows,
         w_near_proj, w_near_out, w_up), "vvvvvvvvvhhhhh",
        [((cells, model), F32), ((cells, ff), BF), ((side, model), BF), ((side, model), BF),
         ((cells, 3 * model), BF), ((2 * rim, 2 * model), BF), ((cells, model), F32)],
        [vm((model, 2 * model), BF), vm((model, model), BF), vm((model, ff), BF),
         vm((keys_all, 2 * model), BF), vm((keys_all, 2 * model), BF),
         vm((2 * side, model), BF), vm((pairs_n, 2 * cells, keys_all), BF),
         vm((GROUP, 2 * cells, keys_all), F32), vm((GROUP, 2 * cells, keys_all), BF),
         vm((cells, keys_all), F32), vm((cells, model), BF), vm((cells, model), BF),
         vm((cells, ff), BF), vm((cells, model), F32), vm((cells, model), BF),
         vm((cells, model), BF), dma((5,))],
        2e10, "near",
    )
    from_east = ring(dwest, -1)
    from_west = ring(deast, 1)
    dn_rows = call(
        rows_back_kernel, (drows, w_near_proj), "vh", [((2 * rim, model), F32)],
        [vm((model, 2 * model), BF), dma((1,))],
        2 * 2 * rim * model * 2 * model, "rows_back",
    )
    dnorth, dsouth = call(
        fold_kernel, (dn_rows, from_east, from_west, jnp.asarray(select[:, cells:])), "vvvv",
        [((rim, model), BF), ((rim, model), BF)],
        [vm((2 * side, model), BF)],
        2 * 2 * side * 2 * rim * model, "fold",
    )
    from_south = line(dnorth, -1)
    from_north = line(dsouth, 1)
    dn_own = call(
        own_back_kernel,
        (dqkv, from_east, from_west, jnp.asarray(select[:, :cells]), w_near_proj, dnorth), "vvvvhh",
        [((cells, model), F32)],
        [vm((2 * side, model), BF), vm((model, 3 * model), BF), dma((1,))],
        2 * cells * model * 3 * model, "own_back",
    )
    encoded = call(
        encode_kernel, (after, hidden, w_down, dsouth), "vvhh", [((cells, model), BF)],
        [vm((ff, model), BF), dma((1,))], 2 * cells * model * ff, "encode",
    )
    dstate, slot_grads, dq, down = call(
        cross_back_kernel,
        (dn_own, from_north, from_south, state, dafter, norm_gains, q_c, own_pairs, slot_pairs,
         cross_w, cross_mix, own_w, w_cross_pairs, w_cross_out, encoded), "vvvvvvvvvvvvhhh",
        [((cells, model), F32), ((devices, cap, model), BF), ((cells, model), BF),
         ((cells, 2 * model), BF)],
        [vm((model, 2 * model), BF), vm((model, model), BF), vm((cells, model), BF),
         vm((cells, model), BF), vm((slots, 2 * model), BF), vm((GROUP, 2 * cells, slots), F32),
         vm((GROUP, 2 * cells, slots), BF), dma((2,))],
        2 * slots * model * 2 * model * 2, "cross_back",
    )
    returned = lax.all_to_all(
        slot_grads, ("lat", "lon"), 0, 0, tiled=True
    ).reshape(slots, model)
    grid_grad = call(
        grid_back_kernel,
        (flat, dstate, norm_gains, dq, down, w_cross_query, w_cross_pairs), "vvvvvhh",
        [((cells, model), BF)],
        [vm((model, model), BF), vm((model, 2 * model), BF), vm((cells, model), F32), dma((2,))],
        2 * cells * model * 3 * model, "grid_back",
    )
    obs_grad = dot(placing, returned, TN).astype(BF)
    shape = (rows_lat, rows_lon, model)
    return encoded.reshape(shape), grid_grad.reshape(shape), obs_grad


def solution(mesh):
    return jax.shard_map(
        per_device,
        mesh=mesh,
        in_specs=(
            P("lat", "lon", None),
            P(("lat", "lon"), None),
            P(("lat", "lon"), None),
            P(("lat", "lon"), None),
            P("lat", "lon", None),
            P(), P(), P(), P(), P(), P(), P(), P(),
        ),
        out_specs=(P("lat", "lon", None), P("lat", "lon", None), P(("lat", "lon"), None)),
        check_vma=False,
    )
```

```python
import functools

import jax
import jax.numpy as jnp
import numpy as np
from jax import lax
from jax.experimental import pallas as pl
from jax.experimental.pallas import tpu as pltpu
from jax.sharding import PartitionSpec as P

HEADS = 16
RADIUS = 6
EPSILON = 1e-05
SPREAD = 32.0
LOW_SCORE = -1e30

BF = jnp.bfloat16
F32 = jnp.float32
NN = (((1,), (0,)), ((), ()))
NT = (((1,), (1,)), ((), ()))
TN = (((0,), (0,)), ((), ()))
CHUNK = 32
TILE = 1024
PAIR = 128
HALF = 64
SLACK_BYTES = 8 * 2**20
FEED_TILE = 512
GROUP = 2
GELU_C = 0.7978845608028654
GELU_A = 0.044715


def dot(left, right, dims=NN):
    return lax.dot_general(left, right, dims, preferred_element_type=F32)


def iota(shape, dim):
    return lax.broadcasted_iota(jnp.int32, shape, dim)


def tiles_of(count, body, tile=TILE):
    @pl.loop(0, count // tile)
    def _(i):
        body(pl.multiple_of(i * tile, tile))


def row_chunks(count):
    return [pl.ds(i, CHUNK) for i in range(0, count, CHUNK)]


def unit(values):
    center = values - jnp.mean(values, -1, keepdims=True)
    scale = lax.rsqrt(jnp.mean(center * center, -1, keepdims=True) + EPSILON)
    return center * scale, scale


def norm_pull(values, gain, grad):
    normed, scale = unit(values)
    inner = grad * gain
    return scale * (
        inner
        - jnp.mean(inner, -1, keepdims=True)
        - normed * jnp.mean(inner * normed, -1, keepdims=True)
    )


def head_masks():
    left = (iota((1, PAIR), 1) < HALF).astype(F32)
    return left.astype(BF), (1.0 - left).astype(BF)


def stacked(values):
    left, right = head_masks()
    return jnp.concatenate([values * left, values * right], axis=0)


def merged(values):
    count = values.shape[0] // 2
    lanes = iota((count, PAIR), 1) < HALF
    return jnp.where(lanes, values[:count], values[count:])


def lane_sums(values):
    lanes = iota(values.shape, 1) < HALF
    first = jnp.sum(jnp.where(lanes, values, 0.0), -1, keepdims=True)
    second = jnp.sum(jnp.where(lanes, 0.0, values), -1, keepdims=True)
    return first, second


def fetch(sources, targets, sems):
    copies = [
        pltpu.make_async_copy(source, target, sems.at[i])
        for i, (source, target) in enumerate(zip(sources, targets))
    ]
    for copy in copies:
        copy.start()
    return copies


def call(body, ins, kinds, outs, scratch, flops, name):
    any_spec = pl.BlockSpec(memory_space=pl.ANY)
    vmem_spec = pl.BlockSpec(memory_space=pltpu.VMEM)
    moved = sum(x.size * x.dtype.itemsize for x in ins)
    moved += sum(int(np.prod(o[0])) * jnp.dtype(o[1]).itemsize for o in outs)
    held = sum(x.size * x.dtype.itemsize for x, k in zip(ins, kinds) if k == "v")
    held += sum(int(np.prod(o[0])) * jnp.dtype(o[1]).itemsize for o in outs if len(o) == 2)
    for item in scratch:
        if jnp.issubdtype(item.dtype, jnp.floating):
            held += int(np.prod(item.shape)) * jnp.dtype(item.dtype).itemsize
    single = len(outs) == 1
    shapes = [
        jax.ShapeDtypeStruct(*o) if len(o) == 2 else pltpu.HBM(o[0], o[1]) for o in outs
    ]
    specs = [vmem_spec if len(o) == 2 else any_spec for o in outs]
    ins = [
        pltpu.with_memory_space_constraint(x, pltpu.HBM) if k == "h" else x
        for x, k in zip(ins, kinds)
    ]
    return pl.pallas_call(
        body,
        name=name,
        out_shape=shapes[0] if single else shapes,
        in_specs=[vmem_spec if k == "v" else any_spec for k in kinds],
        out_specs=specs[0] if single else specs,
        scratch_shapes=scratch,
        compiler_params=pltpu.CompilerParams(vmem_limit_bytes=held + SLACK_BYTES),
        cost_estimate=pl.CostEstimate(
            flops=int(flops), bytes_accessed=int(moved), transcendentals=0
        ),
    )(*ins)


def place_kernel(
    tile_hbm, cell_hbm, obs_hbm, pay_hbm, place_hbm,
    tile_ref, cell_ref, obs_ref, pay_ref, place_ref, sems, *, devices, cap, wide,
):
    copies = fetch([tile_hbm, cell_hbm, obs_hbm], [tile_ref, cell_ref, obs_ref], sems)
    copies[0].wait()
    rows, model = obs_ref.shape
    slots = devices * cap
    tile = tile_ref[...]
    member = tile == iota((devices, rows), 0)
    earlier = (iota((rows, rows), 0) < iota((rows, rows), 1)).astype(F32).astype(BF)
    before = dot(member.astype(F32).astype(BF), earlier)
    rank = jnp.sum(jnp.where(member, before, 0.0), 0, keepdims=True).astype(jnp.int32)
    slot = tile * cap + rank
    placing = (slot == iota((slots, rows), 0)).astype(F32).astype(BF)
    place_ref[...] = placing
    copies[1].wait()
    copies[2].wait()
    cell = cell_ref[...]
    shift = wide.bit_length() - 1
    line_no = iota((128, rows), 0)
    codes = jnp.where(
        line_no == 0, (cell >> shift) + 1, jnp.where(line_no == 1, (cell & (wide - 1)) + 1, 0)
    )
    code_rows = dot(placing, codes.astype(F32).astype(BF), NT).astype(BF)
    pay_ref[:, :, model:] = code_rows.reshape(devices, cap, 128)
    moved = dot(placing, obs_ref[...]).astype(BF)
    pay_ref[:, :, :model] = moved.reshape(devices, cap, model)
    for copy in fetch([pay_ref, place_ref], [pay_hbm, place_hbm], sems):
        copy.wait()


def grid_kernel(
    grid_hbm, cot_hbm, gain_ref, wq_hbm, wp_hbm, wd_hbm, q_hbm, own_hbm, dh_hbm,
    grid_ref, cot_ref, q_ref, own_ref, dh_ref, nrm, wq, wp, wd, sems, out_sems,
):
    first, *copies = fetch(
        [grid_hbm, wq_hbm, wp_hbm, wd_hbm, cot_hbm], [grid_ref, wq, wp, wd, cot_ref], sems
    )
    cells, model = grid_ref.shape
    first.wait()
    for rows in row_chunks(cells):
        normed, _ = unit(grid_ref[rows, :].astype(F32))
        nrm[rows, :] = (normed * gain_ref[0:1, :]).astype(BF)
    copies[0].wait()

    def query(j):
        q_ref[:, pl.ds(j, TILE)] = (
            dot(nrm[...], wq[:, pl.ds(j, TILE)]) * HALF ** (-0.5)
        ).astype(BF)

    tiles_of(model, query)
    copies[1].wait()

    def own(j):
        own_ref[:, pl.ds(j, TILE)] = dot(nrm[...], wp[:, pl.ds(j, TILE)]).astype(BF)

    tiles_of(2 * model, own)
    copies[2].wait()
    copies[3].wait()

    def hidden(j):
        dh_ref[:, pl.ds(j, TILE)] = dot(cot_ref[...], wd[pl.ds(j, TILE), :], NT).astype(BF)

    tiles_of(dh_ref.shape[1], hidden)
    for copy in fetch([q_ref, own_ref, dh_ref], [q_hbm, own_hbm, dh_hbm], out_sems):
        copy.wait()


def cross_kernel(
    arr_ref, grid_hbm, q_hbm, own_hbm, gain_ref, wp_hbm, wo_hbm,
    state_hbm, top_ref, bottom_ref, pairs_hbm, wts_hbm, mix_hbm, ow_hbm,
    arr, wp, wo, scores, bias, grid_ref, q_ref, own_ref, state_ref, pairs_ref, wts_ref,
    mix_ref, ow_ref, sems, out_sems, *, wide,
):
    copies = fetch(
        [wp_hbm, wo_hbm, q_hbm, own_hbm, grid_hbm], [wp, wo, q_ref, own_ref, grid_ref], sems
    )
    cells, model = grid_ref.shape
    rim = top_ref.shape[0]
    slots = arr.shape[0]
    arr[...] = arr_ref[...].reshape(arr.shape)
    pick = (iota((8, 128), 0) == iota((8, 128), 1)).astype(F32).astype(BF)
    codes = dot(pick, arr[:, model:], NT)
    cell = iota((cells, slots), 0)
    shift = wide.bit_length() - 1
    row_gap = (cell >> shift).astype(F32) - (codes[0:1] - 1.0)
    col_gap = (cell & (wide - 1)).astype(F32) - (codes[1:2] - 1.0)
    near = -(row_gap * row_gap + col_gap * col_gap) * (1.0 / SPREAD)
    bias[...] = jnp.where(codes[0:1] > 0.5, near, LOW_SCORE)
    copies[0].wait()

    def project(j):
        pairs_ref[:, pl.ds(j, TILE)] = dot(
            arr[:, :model], wp[:, pl.ds(j, TILE)]
        ).astype(BF)

    tiles_of(2 * model, project)
    leaving = fetch([pairs_ref], [pairs_hbm], out_sems.at[pl.ds(0, 1)])
    copies[2].wait()
    copies[3].wait()

    def soften(h, k, own_scores):
        own_weights = []
        for side in range(2):
            parts = []
            for i in range(0, cells, CHUNK):
                own_score = own_scores[side][i : i + CHUNK]
                x = scores[k, pl.ds(side * cells + i, CHUNK), :] + bias[pl.ds(i, CHUNK), :]
                peak = jnp.maximum(jnp.max(x, -1, keepdims=True), own_score)
                x = jnp.exp(x - peak)
                own_weight = jnp.exp(own_score - peak)
                inverse = 1.0 / (jnp.sum(x, -1, keepdims=True) + own_weight)
                wts_ref[h, pl.ds(side * cells + i, CHUNK), :] = (x * inverse).astype(BF)
                parts.append(own_weight * inverse)
            own_weights.append(jnp.concatenate(parts, axis=0))
        lanes = iota((cells, PAIR), 1) < HALF
        return jnp.where(lanes, own_weights[0], own_weights[1]).astype(BF)

    @pl.loop(0, model // (PAIR * GROUP))
    def _(g):
        heads, own_scores, weights = [], [], []
        for k in range(GROUP):
            h = g * GROUP + k
            keys = pl.ds(pl.multiple_of(h * PAIR, PAIR), PAIR)
            vals = pl.ds(pl.multiple_of(model + h * PAIR, PAIR), PAIR)
            heads.append((h, keys, vals))
            q = q_ref[:, keys]
            scores[k] = dot(stacked(q), pairs_ref[:, keys], NT)
            own_scores.append(lane_sums(q.astype(F32) * own_ref[:, keys].astype(F32)))
        for k, (h, keys, vals) in enumerate(heads):
            weights.append(soften(h, k, own_scores[k]))
            ow_ref[:, keys] = weights[k]
        for k, (h, keys, vals) in enumerate(heads):
            mix = merged(dot(wts_ref[h], pairs_ref[:, vals]))
            mix_ref[:, keys] = (
                mix + weights[k].astype(F32) * own_ref[:, vals].astype(F32)
            ).astype(BF)

    leaving += fetch(
        [wts_ref, mix_ref, ow_ref], [wts_hbm, mix_hbm, ow_hbm], out_sems.at[pl.ds(1, 3)]
    )
    copies[1].wait()
    copies[4].wait()

    def project_out(j):
        state_ref[:, pl.ds(j, TILE)] = grid_ref[:, pl.ds(j, TILE)].astype(F32) + dot(
            mix_ref[...], wo[:, pl.ds(j, TILE)]
        )

    tiles_of(model, project_out)
    leaving += fetch([state_ref], [state_hbm], out_sems.at[pl.ds(4, 1)])
    for i in range(0, cells, CHUNK):
        normed, _ = unit(state_ref[pl.ds(i, CHUNK), :])
        normed = (normed * gain_ref[1:2, :]).astype(BF)
        if i < rim:
            top_ref[pl.ds(i, CHUNK), :] = normed
        else:
            bottom_ref[pl.ds(i - rim, CHUNK), :] = normed
    for copy in leaving:
        copy.wait()


def near_own_kernel(top_ref, bottom_ref, w_hbm, q_ref, kv_ref, nrm, w, sems):
    cells, model = nrm.shape
    rim = top_ref.shape[0]
    copies = fetch(
        [w_hbm.at[:, pl.ds(0, model)], w_hbm.at[:, pl.ds(model, 2 * model)]],
        [w.at[:, pl.ds(0, model)], w.at[:, pl.ds(model, 2 * model)]],
        sems,
    )
    nrm[pl.ds(0, rim), :] = top_ref[...]
    nrm[pl.ds(rim, rim), :] = bottom_ref[...]
    copies[0].wait()

    def query(j):
        q_ref[:, pl.ds(j, TILE)] = (
            dot(nrm[...], w[:, pl.ds(j, TILE)]) * HALF ** (-0.5)
        ).astype(BF)

    tiles_of(model, query)
    copies[1].wait()

    def pairs(j):
        kv_ref[:, pl.ds(j, TILE)] = dot(
            nrm[...], w[:, pl.ds(pl.multiple_of(model + j, TILE), TILE)]
        ).astype(BF)

    tiles_of(2 * model, pairs)


def rim_kernel(
    top_ref, bottom_ref, north_ref, south_ref, sel_ref, _, west_ref, east_ref, ext
):
    rim, model = north_ref.shape
    for i, part in enumerate((top_ref, bottom_ref, north_ref, south_ref)):
        ext[pl.ds(i * rim, rim), :] = part[...]
    side = west_ref.shape[0]

    def pick(j):
        both = dot(sel_ref[...], ext[:, pl.ds(j, TILE)]).astype(BF)
        west_ref[:, pl.ds(j, TILE)] = both[:side]
        east_ref[:, pl.ds(j, TILE)] = both[side:]

    tiles_of(model, pick)


def near_rows_kernel(north_ref, south_ref, w_hbm, kv_ref, x, w, sems):
    rim, model = north_ref.shape
    copies = fetch([w_hbm.at[:, pl.ds(model, 2 * model)]], [w], sems)
    x[pl.ds(0, rim), :] = north_ref[...]
    x[pl.ds(rim, rim), :] = south_ref[...]
    copies[0].wait()

    def pairs(j):
        kv_ref[:, pl.ds(j, TILE)] = dot(x[...], w[:, pl.ds(j, TILE)]).astype(BF)

    tiles_of(2 * model, pairs)


def near_kernel(
    q_ref, west_ref, east_ref, base_ref, inside_ref, state_ref, cot_ref, dh_ref, gain_ref,
    kvo_hbm, kvr_hbm, wn_hbm, wo_hbm, wu_hbm,
    after_ref, hid_ref, dwest_ref, deast_ref, dqkv_ref, drows_ref, dafter_ref,
    wkv, wo, wu, kv, dkv, x, wts, scores, ds, bias, mix, nrm, du, acc, dab, dmix, sems,
):
    cells, model = state_ref.shape
    keys_all = kv.shape[0]
    ext = 2 * cells
    side = west_ref.shape[0]
    ends = ext + 2 * side
    copies = fetch(
        [kvo_hbm, kvr_hbm, wn_hbm.at[:, pl.ds(model, 2 * model)], wo_hbm, wu_hbm],
        [kv.at[pl.ds(0, cells), :], kv.at[pl.ds(cells, cells), :], wkv, wo, wu],
        sems,
    )
    x[pl.ds(0, side), :] = west_ref[...]
    x[pl.ds(side, side), :] = east_ref[...]
    kv[pl.ds(ends, keys_all - ends), :] = jnp.zeros((keys_all - ends, 2 * model), BF)
    bias[...] = base_ref[...].astype(F32) + inside_ref[0:1, :]
    copies[0].wait()
    copies[1].wait()
    copies[2].wait()

    def project(j):
        kv[pl.ds(ext, 2 * side), pl.ds(j, TILE)] = dot(
            x[...], wkv[:, pl.ds(j, TILE)]
        ).astype(BF)

    tiles_of(2 * model, project)

    @pl.loop(0, model // (PAIR * GROUP))
    def _(g):
        heads = []
        for k in range(GROUP):
            h = g * GROUP + k
            keys = pl.ds(pl.multiple_of(h * PAIR, PAIR), PAIR)
            vals = pl.ds(pl.multiple_of(model + h * PAIR, PAIR), PAIR)
            heads.append((h, keys, vals))
            scores[k] = dot(stacked(q_ref[:, keys]), kv[:, keys], NT)
        for k, (h, keys, vals) in enumerate(heads):
            for start in range(0, 2 * cells, CHUNK):
                rows = pl.ds(start, CHUNK)
                v = scores[k, rows, :] + bias[pl.ds(start % cells, CHUNK), :]
                v = jnp.exp(v - jnp.max(v, -1, keepdims=True))
                inverse = 1.0 / jnp.sum(v, -1, keepdims=True)
                wts[h, rows, :] = (v * inverse).astype(BF)
        for k, (h, keys, vals) in enumerate(heads):
            mix[:, keys] = merged(dot(wts[h], kv[:, vals])).astype(BF)

    copies[3].wait()

    def project_out(j):
        after_ref[:, pl.ds(j, TILE)] = state_ref[:, pl.ds(j, TILE)] + dot(
            mix[...], wo[:, pl.ds(j, TILE)]
        )

    tiles_of(model, project_out)
    for rows in row_chunks(cells):
        normed, _ = unit(after_ref[rows, :])
        nrm[rows, :] = (normed * gain_ref[2:3, :]).astype(BF)
    copies[4].wait()

    def feed(j):
        cols = pl.ds(j, FEED_TILE)
        u = dot(nrm[...], wu[:, cols])
        square = u * u
        t = jnp.tanh(GELU_C * (u + GELU_A * (square * u)))
        half = 0.5 * (1.0 + t)
        hid_ref[:, cols] = (u * half).astype(BF)
        slope = half + (0.5 * GELU_C) * u * (1.0 - t * t) * (1.0 + 3.0 * GELU_A * square)
        du[:, cols] = (dh_ref[:, cols].astype(F32) * slope).astype(BF)

    tiles_of(du.shape[1], feed, FEED_TILE)

    def feed_back(j):
        acc[:, pl.ds(j, TILE)] = dot(du[...], wu[pl.ds(j, TILE), :], NT)

    tiles_of(model, feed_back)
    for rows in row_chunks(cells):
        grad = acc[rows, :].astype(BF).astype(F32)
        total = cot_ref[rows, :].astype(F32) + norm_pull(
            after_ref[rows, :], gain_ref[2:3, :], grad
        )
        dafter_ref[rows, :] = total
        dab[rows, :] = total.astype(BF)

    def mix_back(j):
        dmix[:, pl.ds(j, TILE)] = dot(dab[...], wo[pl.ds(j, TILE), :], NT).astype(BF)

    tiles_of(model, mix_back)

    @pl.loop(0, model // (PAIR * GROUP))
    def _(g):
        heads, deltas = [], []
        for k in range(GROUP):
            h = g * GROUP + k
            keys = pl.ds(pl.multiple_of(h * PAIR, PAIR), PAIR)
            vals = pl.ds(pl.multiple_of(model + h * PAIR, PAIR), PAIR)
            heads.append((h, keys, vals))
            grad = dmix[:, keys]
            scores[k] = dot(stacked(grad), kv[:, vals], NT)
            deltas.append(lane_sums(grad.astype(F32) * mix[:, keys].astype(F32)))
        for k, (h, keys, vals) in enumerate(heads):
            for s in range(2):
                for i in range(0, cells, CHUNK):
                    rows = pl.ds(s * cells + i, CHUNK)
                    ds[k, rows, :] = (
                        wts[h, rows, :].astype(F32)
                        * (scores[k, rows, :] - deltas[k][s][i : i + CHUNK])
                    ).astype(BF)
        for k, (h, keys, vals) in enumerate(heads):
            dq = merged(dot(ds[k], kv[:, keys])) * HALF ** (-0.5)
            dqkv_ref[:, keys] = dq.astype(BF)
            dkv[:, keys] = dot(stacked(q_ref[:, keys]), ds[k], TN).T.astype(BF)
            dkv[:, vals] = dot(stacked(dmix[:, keys]), wts[h], TN).T.astype(BF)

    def rim_back(j):
        both = dot(dkv[pl.ds(ext, 2 * side), :], wkv[pl.ds(j, TILE), :], NT).astype(BF)
        dwest_ref[:, pl.ds(j, TILE)] = both[:side]
        deast_ref[:, pl.ds(j, TILE)] = both[side:]

    tiles_of(model, rim_back)
    dqkv_ref[:, pl.ds(model, 2 * model)] = dkv[pl.ds(0, cells), :]
    drows_ref[...] = dkv[pl.ds(cells, cells), :]


def encode_kernel(after_ref, hid_ref, wd_hbm, _, enc_ref, wd, sems):
    copies = fetch([wd_hbm], [wd], sems)
    copies[0].wait()

    def down(j):
        enc_ref[:, pl.ds(j, TILE)] = (
            after_ref[:, pl.ds(j, TILE)] + dot(hid_ref[...], wd[:, pl.ds(j, TILE)])
        ).astype(BF)

    tiles_of(after_ref.shape[1], down)


def rows_back_kernel(drows_ref, w_hbm, dn_ref, w, sems):
    model = dn_ref.shape[1]
    copies = fetch([w_hbm.at[:, pl.ds(model, 2 * model)]], [w], sems)
    copies[0].wait()

    def back(j):
        dn_ref[:, pl.ds(j, TILE)] = dot(drows_ref[...], w[pl.ds(j, TILE), :], NT)

    tiles_of(model, back)


def fold_kernel(dn_ref, from_east_ref, from_west_ref, sel_ref, north_ref, south_ref, x):
    rim, model = north_ref.shape
    side = from_east_ref.shape[0]
    x[pl.ds(0, side), :] = from_west_ref[...]
    x[pl.ds(side, side), :] = from_east_ref[...]

    def fold(j):
        cols = pl.ds(j, TILE)
        total = (dn_ref[:, cols] + dot(sel_ref[...], x[:, cols], TN)).astype(BF)
        north_ref[:, cols] = total[:rim]
        south_ref[:, cols] = total[rim:]

    tiles_of(model, fold)


def own_back_kernel(
    dqkv_ref, from_east_ref, from_west_ref, sel_ref, w_hbm, _, dn_ref, x, w, sems
):
    copies = fetch([w_hbm], [w], sems)
    side = from_east_ref.shape[0]
    x[pl.ds(0, side), :] = from_west_ref[...]
    x[pl.ds(side, side), :] = from_east_ref[...]
    copies[0].wait()

    def back(j):
        cols = pl.ds(j, TILE)
        dn_ref[:, cols] = dot(dqkv_ref[...], w[cols, :], NT) + dot(
            sel_ref[...], x[:, cols], TN
        )

    tiles_of(dn_ref.shape[1], back)


def cross_back_kernel(
    dn_ref, north_ref, south_ref, state_ref, dafter_ref, gain_ref, q_ref, own_ref, pairs_ref,
    wts_ref, mix_ref, ow_ref, wp_hbm, wo_hbm, _,
    dstate_hbm, slot_ref, dq_hbm, down_hbm,
    wp, wo, dsb, dmix, dpairs, scores, ds, dstate_ref, dq_ref, down_ref, sems, out_sems,
):
    copies = fetch([wo_hbm, wp_hbm], [wo, wp], sems)
    cells, model = state_ref.shape
    rim = north_ref.shape[0]
    for i in range(0, cells, CHUNK):
        rows = pl.ds(i, CHUNK)
        other = north_ref[rows, :] if i < rim else south_ref[pl.ds(i - rim, CHUNK), :]
        grad = (dn_ref[rows, :] + other.astype(F32)).astype(BF).astype(F32)
        total = dafter_ref[rows, :] + norm_pull(state_ref[rows, :], gain_ref[1:2, :], grad)
        dstate_ref[rows, :] = total
        dsb[rows, :] = total.astype(BF)
    copies[0].wait()

    def mix_back(j):
        dmix[:, pl.ds(j, TILE)] = dot(dsb[...], wo[pl.ds(j, TILE), :], NT).astype(BF)

    tiles_of(model, mix_back)

    @pl.loop(0, model // (PAIR * GROUP))
    def _(g):
        heads, deltas, own_dots = [], [], []
        for k in range(GROUP):
            h = g * GROUP + k
            keys = pl.ds(pl.multiple_of(h * PAIR, PAIR), PAIR)
            vals = pl.ds(pl.multiple_of(model + h * PAIR, PAIR), PAIR)
            heads.append((h, keys, vals))
            grad = dmix[:, keys]
            grad_f = grad.astype(F32)
            scores[k] = dot(stacked(grad), pairs_ref[:, vals], NT)
            deltas.append(lane_sums(grad_f * mix_ref[:, keys].astype(F32)))
            own_dots.append(lane_sums(grad_f * own_ref[:, vals].astype(F32)))
        for k, (h, keys, vals) in enumerate(heads):
            for s in range(2):
                for i in range(0, cells, CHUNK):
                    rows = pl.ds(s * cells + i, CHUNK)
                    ds[k, rows, :] = (
                        wts_ref[h, rows, :].astype(F32)
                        * (scores[k, rows, :] - deltas[k][s][i : i + CHUNK])
                    ).astype(BF)
        for k, (h, keys, vals) in enumerate(heads):
            lanes = iota((cells, PAIR), 1) < HALF
            weight = ow_ref[:, keys].astype(F32)
            own_grad = weight * jnp.where(
                lanes, own_dots[k][0] - deltas[k][0], own_dots[k][1] - deltas[k][1]
            )
            q = q_ref[:, keys]
            grad = dmix[:, keys]
            dq = merged(dot(ds[k], pairs_ref[:, keys]))
            dq = dq + own_grad * own_ref[:, keys].astype(F32)
            dq_ref[:, keys] = (dq * HALF ** (-0.5)).astype(BF)
            down_ref[:, keys] = (own_grad * q.astype(F32)).astype(BF)
            down_ref[:, vals] = (weight * grad.astype(F32)).astype(BF)
            dpairs[:, keys] = dot(stacked(q), ds[k], TN).T.astype(BF)
            dpairs[:, vals] = dot(stacked(grad), wts_ref[h], TN).T.astype(BF)

    leaving = fetch(
        [dstate_ref, dq_ref, down_ref], [dstate_hbm, dq_hbm, down_hbm], out_sems
    )
    copies[1].wait()

    def slot_back(j):
        grads = dot(dpairs[...], wp[pl.ds(j, TILE), :], NT).astype(BF)
        slot_ref[:, :, pl.ds(j, TILE)] = grads.reshape(slot_ref.shape[:2] + (TILE,))

    tiles_of(model, slot_back)
    for copy in leaving:
        copy.wait()


def gather_kernel(place_ref, ret_ref, out_ref, ret):
    ret[...] = ret_ref[...].reshape(ret.shape)
    out_ref[...] = dot(place_ref[...], ret[...], TN).astype(BF)


def grid_back_kernel(
    grid_ref, dstate_ref, gain_ref, dq_ref, down_ref, wq_hbm, wp_hbm, out_ref, wq, wp, acc, sems
):
    copies = fetch([wq_hbm, wp_hbm], [wq, wp], sems)
    cells, model = grid_ref.shape
    for copy in copies:
        copy.wait()

    def back(j):
        acc[:, pl.ds(j, TILE)] = dot(dq_ref[...], wq[pl.ds(j, TILE), :], NT) + dot(
            down_ref[...], wp[pl.ds(j, TILE), :], NT
        )

    tiles_of(model, back)
    for rows in row_chunks(cells):
        grad = acc[rows, :].astype(BF).astype(F32)
        out_ref[rows, :] = (
            dstate_ref[rows, :]
            + norm_pull(grid_ref[rows, :].astype(F32), gain_ref[0:1, :], grad)
        ).astype(BF)


def ring(value, by):
    size = lax.axis_size("lon")
    return lax.ppermute(value, "lon", [(i, (i + by) % size) for i in range(size)])


def line(value, by):
    size = lax.axis_size("lat")
    pairs = [(i, i + by) for i in range(size) if 0 <= i + by < size]
    return lax.ppermute(value, "lat", pairs)


def key_places(rows_lat, rows_lon):
    places = [(r, c) for r in range(rows_lat) for c in range(rows_lon)]
    places += [(r, c) for r in range(-RADIUS, 0) for c in range(rows_lon)]
    places += [(rows_lat + r, c) for r in range(RADIUS) for c in range(rows_lon)]
    ext = list(places)
    tall = range(-RADIUS, rows_lat + RADIUS)
    places += [(r, c) for r in tall for c in range(-RADIUS, 0)]
    places += [(r, rows_lon + c) for r in tall for c in range(RADIUS)]
    return np.array(places), ext


def per_device(
    grid_state, observations, obs_tile, obs_cell, cotangent, norm_gains,
    w_cross_query, w_cross_pairs, w_cross_out, w_near_proj, w_near_out, w_up, w_down,
):
    rows_lat, rows_lon, model = grid_state.shape
    lat_count = lax.axis_size("lat")
    devices = lat_count * lax.axis_size("lon")
    rows_obs = observations.shape[0]
    cap = max(2, 2 * rows_obs // devices)
    slots = devices * cap
    cells = rows_lat * rows_lon
    ff = w_up.shape[1]
    pairs_n = model // PAIR
    rim = RADIUS * rows_lon
    side = RADIUS * (rows_lat + 2 * RADIUS)
    places, ext_places = key_places(rows_lat, rows_lon)
    keys_n = len(places)
    keys_all = -(-keys_n // 256) * 256
    spot = {place: i for i, place in enumerate(ext_places)}
    tall = range(-RADIUS, rows_lat + RADIUS)
    select = np.zeros((2 * side, len(ext_places)), np.float32)
    for i, r in enumerate(tall):
        for c in range(RADIUS):
            select[i * RADIUS + c, spot[(r, c)]] = 1.0
            select[side + i * RADIUS + c, spot[(r, rows_lon - RADIUS + c)]] = 1.0
    select = select.astype(jnp.bfloat16)
    base = np.full((cells, keys_all), LOW_SCORE, np.float32)
    own_rows, own_cols = places[:cells, 0], places[:cells, 1]
    allowed = (np.abs(places[None, :, 0] - own_rows[:, None]) <= RADIUS) & (
        np.abs(places[None, :, 1] - own_cols[:, None]) <= RADIUS
    )
    base[:, :keys_n][allowed] = 0.0
    base = jnp.asarray(base.astype(jnp.bfloat16))
    key_rows = np.zeros((8, keys_all), np.int32)
    key_rows[:, :keys_n] = places[None, :, 0]
    key_lat = jnp.asarray(key_rows) + lax.axis_index("lat") * rows_lat
    inside = jnp.where((key_lat >= 0) & (key_lat < rows_lat * lat_count), 0.0, LOW_SCORE)
    inside = inside.astype(F32)

    dma = pltpu.SemaphoreType.DMA
    vm = pltpu.VMEM
    flat = grid_state.reshape(cells, model)
    cot = cotangent.reshape(cells, model)

    payload, placing = call(
        functools.partial(place_kernel, devices=devices, cap=cap, wide=rows_lon),
        (obs_tile.reshape(1, rows_obs), obs_cell.reshape(1, rows_obs), observations), "hhh",
        [((devices, cap, model + 128), BF, "h"), ((slots, rows_obs), BF, "h")],
        [vm((1, rows_obs), jnp.int32), vm((1, rows_obs), jnp.int32), vm((rows_obs, model), BF),
         vm((devices, cap, model + 128), BF), vm((slots, rows_obs), BF), dma((3,))],
        2 * rows_obs * slots * model, "place",
    )
    arrived = lax.all_to_all(payload, ("lat", "lon"), 0, 0, tiled=True)
    q_c, own_pairs, dhid = call(
        grid_kernel,
        (flat, cot, norm_gains, w_cross_query, w_cross_pairs, w_down), "hhvhhh",
        [((cells, model), BF, "h"), ((cells, 2 * model), BF, "h"), ((cells, ff), BF, "h")],
        [vm((cells, model), BF), vm((cells, model), BF), vm((cells, model), BF),
         vm((cells, 2 * model), BF), vm((cells, ff), BF),
         vm((cells, model), BF), vm((model, model), BF), vm((model, 2 * model), BF),
         vm((ff, model), BF), dma((5,)), dma((3,))],
        2 * cells * model * (3 * model + ff), "grid_proj",
    )
    state, top, bottom, slot_pairs, cross_w, cross_mix, own_w = call(
        functools.partial(cross_kernel, wide=rows_lon),
        (arrived, flat, q_c, own_pairs, norm_gains, w_cross_pairs, w_cross_out), "vhhhvhh",
        [((cells, model), F32, "h"), ((rim, model), BF), ((rim, model), BF),
         ((slots, 2 * model), BF, "h"), ((pairs_n, 2 * cells, slots), BF, "h"),
         ((cells, model), BF, "h"), ((cells, model), BF, "h")],
        [vm((slots, model + 128), BF), vm((model, 2 * model), BF), vm((model, model), BF),
         vm((GROUP, 2 * cells, slots), F32), vm((cells, slots), F32), vm((cells, model), BF),
         vm((cells, model), BF), vm((cells, 2 * model), BF), vm((cells, model), F32),
         vm((slots, 2 * model), BF), vm((pairs_n, 2 * cells, slots), BF), vm((cells, model), BF),
         vm((cells, model), BF), dma((5,)), dma((5,))],
        2 * slots * model * 2 * model * 2, "cross",
    )
    south = line(top, -1)
    north = line(bottom, 1)
    q_n, kv_own = call(
        near_own_kernel, (top, bottom, w_near_proj), "vva",
        [((cells, model), BF), ((cells, 2 * model), BF)],
        [vm((cells, model), BF), vm((model, 3 * model), BF), dma((2,))],
        2 * cells * model * 3 * model, "near_own",
    )
    west_send, east_send = call(
        rim_kernel, (top, bottom, north, south, jnp.asarray(select), kv_own), "vvvvva",
        [((side, model), BF), ((side, model), BF)],
        [vm((cells + 2 * rim, model), BF)],
        2 * 2 * side * 2 * cells * model, "rim",
    )
    east = ring(west_send, -1)
    west = ring(east_send, 1)
    kv_rows = call(
        near_rows_kernel, (north, south, w_near_proj), "vva",
        [((2 * rim, 2 * model), BF)],
        [vm((2 * rim, model), BF), vm((model, 2 * model), BF), dma((1,))],
        2 * 2 * rim * model * 2 * model, "near_rows",
    )
    after, hidden, dwest, deast, dqkv, drows, dafter = call(
        near_kernel,
        (q_n, west, east, base, inside, state, cot, dhid, norm_gains, kv_own, kv_rows,
         w_near_proj, w_near_out, w_up), "vvvvvvvvvaaaaa",
        [((cells, model), F32), ((cells, ff), BF), ((side, model), BF), ((side, model), BF),
         ((cells, 3 * model), BF), ((2 * rim, 2 * model), BF), ((cells, model), F32)],
        [vm((model, 2 * model), BF), vm((model, model), BF), vm((model, ff), BF),
         vm((keys_all, 2 * model), BF), vm((keys_all, 2 * model), BF),
         vm((2 * side, model), BF), vm((pairs_n, 2 * cells, keys_all), BF),
         vm((GROUP, 2 * cells, keys_all), F32), vm((GROUP, 2 * cells, keys_all), BF),
         vm((cells, keys_all), F32), vm((cells, model), BF), vm((cells, model), BF),
         vm((cells, ff), BF), vm((cells, model), F32), vm((cells, model), BF),
         vm((cells, model), BF), dma((5,))],
        2e10, "near",
    )
    from_east = ring(dwest, -1)
    from_west = ring(deast, 1)
    dn_rows = call(
        rows_back_kernel, (drows, w_near_proj), "va", [((2 * rim, model), F32)],
        [vm((model, 2 * model), BF), dma((1,))],
        2 * 2 * rim * model * 2 * model, "rows_back",
    )
    dnorth, dsouth = call(
        fold_kernel, (dn_rows, from_east, from_west, jnp.asarray(select[:, cells:])), "vvvv",
        [((rim, model), BF), ((rim, model), BF)],
        [vm((2 * side, model), BF)],
        2 * 2 * side * 2 * rim * model, "fold",
    )
    from_south = line(dnorth, -1)
    from_north = line(dsouth, 1)
    dn_own = call(
        own_back_kernel,
        (dqkv, from_east, from_west, jnp.asarray(select[:, :cells]), w_near_proj, dnorth), "vvvvaa",
        [((cells, model), F32)],
        [vm((2 * side, model), BF), vm((model, 3 * model), BF), dma((1,))],
        2 * cells * model * 3 * model, "own_back",
    )
    encoded = call(
        encode_kernel, (after, hidden, w_down, dsouth), "vvaa", [((cells, model), BF)],
        [vm((ff, model), BF), dma((1,))], 2 * cells * model * ff, "encode",
    )
    dstate, slot_grads, dq, down = call(
        cross_back_kernel,
        (dn_own, from_north, from_south, state, dafter, norm_gains, q_c, own_pairs, slot_pairs,
         cross_w, cross_mix, own_w, w_cross_pairs, w_cross_out, encoded), "vvvvvvvvvvvvaaa",
        [((cells, model), F32, "h"), ((devices, cap, model), BF), ((cells, model), BF, "h"),
         ((cells, 2 * model), BF, "h")],
        [vm((model, 2 * model), BF), vm((model, model), BF), vm((cells, model), BF),
         vm((cells, model), BF), vm((slots, 2 * model), BF), vm((GROUP, 2 * cells, slots), F32),
         vm((GROUP, 2 * cells, slots), BF), vm((cells, model), F32), vm((cells, model), BF),
         vm((cells, 2 * model), BF), dma((2,)), dma((3,))],
        2 * slots * model * 2 * model * 2, "cross_back",
    )
    returned = lax.all_to_all(slot_grads, ("lat", "lon"), 0, 0, tiled=True)
    grid_grad = call(
        grid_back_kernel,
        (flat, dstate, norm_gains, dq, down, w_cross_query, w_cross_pairs), "vvvvvaa",
        [((cells, model), BF)],
        [vm((model, model), BF), vm((model, 2 * model), BF), vm((cells, model), F32), dma((2,))],
        2 * cells * model * 3 * model, "grid_back",
    )
    obs_grad = call(
        gather_kernel, (placing, returned), "vv", [((rows_obs, model), BF)],
        [vm((slots, model), BF)], 2 * rows_obs * slots * model, "gather",
    )
    shape = (rows_lat, rows_lon, model)
    return encoded.reshape(shape), grid_grad.reshape(shape), obs_grad


def solution(mesh):
    return jax.shard_map(
        per_device,
        mesh=mesh,
        in_specs=(
            P("lat", "lon", None),
            P(("lat", "lon"), None),
            P(("lat", "lon"), None),
            P(("lat", "lon"), None),
            P("lat", "lon", None),
            P(), P(), P(), P(), P(), P(), P(), P(),
        ),
        out_specs=(P("lat", "lon", None), P("lat", "lon", None), P(("lat", "lon"), None)),
        check_vma=False,
    )
```

```python
import functools

import jax
import jax.numpy as jnp
import numpy as np
from jax import lax
from jax.experimental import pallas as pl
from jax.experimental.pallas import tpu as pltpu
from jax.sharding import PartitionSpec as P

HEADS = 16
RADIUS = 6
EPSILON = 1e-05
SPREAD = 32.0
LOW_SCORE = -1e30

BF = jnp.bfloat16
F32 = jnp.float32
NN = (((1,), (0,)), ((), ()))
NT = (((1,), (1,)), ((), ()))
TN = (((0,), (0,)), ((), ()))
CHUNK = 32
TILE = 1024
PAIR = 128
HALF = 64
SLACK_BYTES = 8 * 2**20
FEED_TILE = 512
GROUP = 2
GELU_C = 0.7978845608028654
GELU_A = 0.044715


def dot(left, right, dims=NN):
    return lax.dot_general(left, right, dims, preferred_element_type=F32)


def iota(shape, dim):
    return lax.broadcasted_iota(jnp.int32, shape, dim)


def tiles_of(count, body, tile=TILE):
    @pl.loop(0, count // tile)
    def _(i):
        body(pl.multiple_of(i * tile, tile))


def row_chunks(count):
    return [pl.ds(i, CHUNK) for i in range(0, count, CHUNK)]


def unit(values):
    center = values - jnp.mean(values, -1, keepdims=True)
    scale = lax.rsqrt(jnp.mean(center * center, -1, keepdims=True) + EPSILON)
    return center * scale, scale


def norm_pull(values, gain, grad):
    normed, scale = unit(values)
    inner = grad * gain
    return scale * (
        inner
        - jnp.mean(inner, -1, keepdims=True)
        - normed * jnp.mean(inner * normed, -1, keepdims=True)
    )


def head_masks():
    left = (iota((1, PAIR), 1) < HALF).astype(F32)
    return left.astype(BF), (1.0 - left).astype(BF)


def stacked(values):
    left, right = head_masks()
    return jnp.concatenate([values * left, values * right], axis=0)


def merged(values):
    count = values.shape[0] // 2
    lanes = iota((count, PAIR), 1) < HALF
    return jnp.where(lanes, values[:count], values[count:])


def lane_sums(values):
    lanes = iota(values.shape, 1) < HALF
    first = jnp.sum(jnp.where(lanes, values, 0.0), -1, keepdims=True)
    second = jnp.sum(jnp.where(lanes, 0.0, values), -1, keepdims=True)
    return first, second


def fetch(sources, targets, sems):
    copies = [
        pltpu.make_async_copy(source, target, sems.at[i])
        for i, (source, target) in enumerate(zip(sources, targets))
    ]
    for copy in copies:
        copy.start()
    return copies


def call(body, ins, kinds, outs, scratch, flops, name):
    any_spec = pl.BlockSpec(memory_space=pl.ANY)
    vmem_spec = pl.BlockSpec(memory_space=pltpu.VMEM)
    moved = sum(x.size * x.dtype.itemsize for x in ins)
    moved += sum(int(np.prod(o[0])) * jnp.dtype(o[1]).itemsize for o in outs)
    held = sum(x.size * x.dtype.itemsize for x, k in zip(ins, kinds) if k == "v")
    held += sum(int(np.prod(o[0])) * jnp.dtype(o[1]).itemsize for o in outs if len(o) == 2)
    for item in scratch:
        if jnp.issubdtype(item.dtype, jnp.floating):
            held += int(np.prod(item.shape)) * jnp.dtype(item.dtype).itemsize
    single = len(outs) == 1
    shapes = [
        jax.ShapeDtypeStruct(*o) if len(o) == 2 else pltpu.HBM(o[0], o[1]) for o in outs
    ]
    specs = [vmem_spec if len(o) == 2 else any_spec for o in outs]
    ins = [
        pltpu.with_memory_space_constraint(x, pltpu.HBM) if k == "h" else x
        for x, k in zip(ins, kinds)
    ]
    return pl.pallas_call(
        body,
        name=name,
        out_shape=shapes[0] if single else shapes,
        in_specs=[vmem_spec if k == "v" else any_spec for k in kinds],
        out_specs=specs[0] if single else specs,
        scratch_shapes=scratch,
        compiler_params=pltpu.CompilerParams(vmem_limit_bytes=held + SLACK_BYTES),
        cost_estimate=pl.CostEstimate(
            flops=int(flops), bytes_accessed=int(moved), transcendentals=0
        ),
    )(*ins)


def place_kernel(
    tile_hbm, cell_hbm, obs_hbm, pay_hbm, place_hbm,
    tile_ref, cell_ref, obs_ref, pay_ref, place_ref, sems, *, devices, cap, wide,
):
    copies = fetch([tile_hbm, cell_hbm, obs_hbm], [tile_ref, cell_ref, obs_ref], sems)
    copies[0].wait()
    rows, model = obs_ref.shape
    slots = devices * cap
    tile = tile_ref[...]
    member = tile == iota((devices, rows), 0)
    earlier = (iota((rows, rows), 0) < iota((rows, rows), 1)).astype(F32).astype(BF)
    before = dot(member.astype(F32).astype(BF), earlier)
    rank = jnp.sum(jnp.where(member, before, 0.0), 0, keepdims=True).astype(jnp.int32)
    slot = tile * cap + rank
    placing = (slot == iota((slots, rows), 0)).astype(F32).astype(BF)
    place_ref[...] = placing
    copies[1].wait()
    copies[2].wait()
    cell = cell_ref[...]
    shift = wide.bit_length() - 1
    line_no = iota((128, rows), 0)
    codes = jnp.where(
        line_no == 0, (cell >> shift) + 1, jnp.where(line_no == 1, (cell & (wide - 1)) + 1, 0)
    )
    code_rows = dot(placing, codes.astype(F32).astype(BF), NT).astype(BF)
    pay_ref[:, :, model:] = code_rows.reshape(devices, cap, 128)
    moved = dot(placing, obs_ref[...]).astype(BF)
    pay_ref[:, :, :model] = moved.reshape(devices, cap, model)
    for copy in fetch([pay_ref, place_ref], [pay_hbm, place_hbm], sems):
        copy.wait()


def grid_kernel(
    grid_hbm, cot_hbm, gain_ref, wq_hbm, wp_hbm, wd_hbm, q_hbm, own_hbm, dh_hbm,
    grid_ref, cot_ref, q_ref, own_ref, dh_ref, nrm, wq, wp, wd, sems, out_sems,
):
    first, *copies = fetch(
        [grid_hbm, wq_hbm, wp_hbm, wd_hbm, cot_hbm], [grid_ref, wq, wp, wd, cot_ref], sems
    )
    cells, model = grid_ref.shape
    first.wait()
    for rows in row_chunks(cells):
        normed, _ = unit(grid_ref[rows, :].astype(F32))
        nrm[rows, :] = (normed * gain_ref[0:1, :]).astype(BF)
    copies[0].wait()

    def query(j):
        q_ref[:, pl.ds(j, TILE)] = (
            dot(nrm[...], wq[:, pl.ds(j, TILE)]) * HALF ** (-0.5)
        ).astype(BF)

    tiles_of(model, query)
    copies[1].wait()

    def own(j):
        own_ref[:, pl.ds(j, TILE)] = dot(nrm[...], wp[:, pl.ds(j, TILE)]).astype(BF)

    tiles_of(2 * model, own)
    copies[2].wait()
    copies[3].wait()

    def hidden(j):
        dh_ref[:, pl.ds(j, TILE)] = dot(cot_ref[...], wd[pl.ds(j, TILE), :], NT).astype(BF)

    tiles_of(dh_ref.shape[1], hidden)
    for copy in fetch([q_ref, own_ref, dh_ref], [q_hbm, own_hbm, dh_hbm], out_sems):
        copy.wait()


def cross_kernel(
    arr_ref, grid_hbm, q_hbm, own_hbm, gain_ref, wp_hbm, wo_hbm,
    state_hbm, top_ref, bottom_ref, pairs_hbm, wts_hbm, mix_hbm, ow_hbm,
    arr, wp, wo, scores, bias, grid_ref, q_ref, own_ref, state_ref, pairs_ref, wts_ref,
    mix_ref, ow_ref, sems, out_sems, *, wide,
):
    cells, model = grid_ref.shape
    parts = [pl.ds(j, TILE) for j in range(0, 2 * model, TILE)]
    copies = fetch([wp_hbm.at[:, c] for c in parts], [wp.at[:, c] for c in parts], sems)
    lates = out_sems.at[pl.ds(5, 4)]
    rim = top_ref.shape[0]
    slots = arr.shape[0]
    arr[...] = arr_ref[...].reshape(arr.shape)
    pick = (iota((8, 128), 0) == iota((8, 128), 1)).astype(F32).astype(BF)
    codes = dot(pick, arr[:, model:], NT)
    cell = iota((cells, slots), 0)
    shift = wide.bit_length() - 1
    row_gap = (cell >> shift).astype(F32) - (codes[0:1] - 1.0)
    col_gap = (cell & (wide - 1)).astype(F32) - (codes[1:2] - 1.0)
    near = -(row_gap * row_gap + col_gap * col_gap) * (1.0 / SPREAD)
    bias[...] = jnp.where(codes[0:1] > 0.5, near, LOW_SCORE)
    for i, cols in enumerate(parts):
        copies[i].wait()
        if i == 0:
            late = fetch(
                [q_hbm, own_hbm, wo_hbm, grid_hbm], [q_ref, own_ref, wo, grid_ref], lates
            )
        pairs_ref[:, cols] = dot(arr[:, :model], wp[:, cols]).astype(BF)
    leaving = fetch([pairs_ref], [pairs_hbm], out_sems.at[pl.ds(0, 1)])
    late[0].wait()
    late[1].wait()

    def soften(h, k, own_scores):
        own_weights = []
        for side in range(2):
            parts = []
            for i in range(0, cells, CHUNK):
                own_score = own_scores[side][i : i + CHUNK]
                x = scores[k, pl.ds(side * cells + i, CHUNK), :] + bias[pl.ds(i, CHUNK), :]
                peak = jnp.maximum(jnp.max(x, -1, keepdims=True), own_score)
                x = jnp.exp(x - peak)
                own_weight = jnp.exp(own_score - peak)
                inverse = 1.0 / (jnp.sum(x, -1, keepdims=True) + own_weight)
                wts_ref[h, pl.ds(side * cells + i, CHUNK), :] = (x * inverse).astype(BF)
                parts.append(own_weight * inverse)
            own_weights.append(jnp.concatenate(parts, axis=0))
        lanes = iota((cells, PAIR), 1) < HALF
        return jnp.where(lanes, own_weights[0], own_weights[1]).astype(BF)

    @pl.loop(0, model // (PAIR * GROUP))
    def _(g):
        heads, own_scores, weights = [], [], []
        for k in range(GROUP):
            h = g * GROUP + k
            keys = pl.ds(pl.multiple_of(h * PAIR, PAIR), PAIR)
            vals = pl.ds(pl.multiple_of(model + h * PAIR, PAIR), PAIR)
            heads.append((h, keys, vals))
            q = q_ref[:, keys]
            scores[k] = dot(stacked(q), pairs_ref[:, keys], NT)
            own_scores.append(lane_sums(q.astype(F32) * own_ref[:, keys].astype(F32)))
        for k, (h, keys, vals) in enumerate(heads):
            weights.append(soften(h, k, own_scores[k]))
            ow_ref[:, keys] = weights[k]
        for k, (h, keys, vals) in enumerate(heads):
            mix = merged(dot(wts_ref[h], pairs_ref[:, vals]))
            mix_ref[:, keys] = (
                mix + weights[k].astype(F32) * own_ref[:, vals].astype(F32)
            ).astype(BF)

    leaving += fetch(
        [wts_ref, mix_ref, ow_ref], [wts_hbm, mix_hbm, ow_hbm], out_sems.at[pl.ds(1, 3)]
    )
    late[2].wait()
    late[3].wait()

    def project_out(j):
        state_ref[:, pl.ds(j, TILE)] = grid_ref[:, pl.ds(j, TILE)].astype(F32) + dot(
            mix_ref[...], wo[:, pl.ds(j, TILE)]
        )

    tiles_of(model, project_out)
    leaving += fetch([state_ref], [state_hbm], out_sems.at[pl.ds(4, 1)])
    for i in range(0, cells, CHUNK):
        normed, _ = unit(state_ref[pl.ds(i, CHUNK), :])
        normed = (normed * gain_ref[1:2, :]).astype(BF)
        if i < rim:
            top_ref[pl.ds(i, CHUNK), :] = normed
        else:
            bottom_ref[pl.ds(i - rim, CHUNK), :] = normed
    for copy in leaving:
        copy.wait()


def near_own_kernel(top_ref, bottom_ref, w_hbm, q_ref, kv_ref, nrm, w, sems):
    cells, model = nrm.shape
    rim = top_ref.shape[0]
    copies = fetch(
        [w_hbm.at[:, pl.ds(0, model)], w_hbm.at[:, pl.ds(model, 2 * model)]],
        [w.at[:, pl.ds(0, model)], w.at[:, pl.ds(model, 2 * model)]],
        sems,
    )
    nrm[pl.ds(0, rim), :] = top_ref[...]
    nrm[pl.ds(rim, rim), :] = bottom_ref[...]
    copies[0].wait()

    def query(j):
        q_ref[:, pl.ds(j, TILE)] = (
            dot(nrm[...], w[:, pl.ds(j, TILE)]) * HALF ** (-0.5)
        ).astype(BF)

    tiles_of(model, query)
    copies[1].wait()

    def pairs(j):
        kv_ref[:, pl.ds(j, TILE)] = dot(
            nrm[...], w[:, pl.ds(pl.multiple_of(model + j, TILE), TILE)]
        ).astype(BF)

    tiles_of(2 * model, pairs)


def rim_kernel(
    top_ref, bottom_ref, north_ref, south_ref, sel_ref, _, west_ref, east_ref, ext
):
    rim, model = north_ref.shape
    for i, part in enumerate((top_ref, bottom_ref, north_ref, south_ref)):
        ext[pl.ds(i * rim, rim), :] = part[...]
    side = west_ref.shape[0]

    def pick(j):
        both = dot(sel_ref[...], ext[:, pl.ds(j, TILE)]).astype(BF)
        west_ref[:, pl.ds(j, TILE)] = both[:side]
        east_ref[:, pl.ds(j, TILE)] = both[side:]

    tiles_of(model, pick)


def near_rows_kernel(north_ref, south_ref, w_hbm, kv_ref, x, w, sems):
    rim, model = north_ref.shape
    copies = fetch([w_hbm.at[:, pl.ds(model, 2 * model)]], [w], sems)
    x[pl.ds(0, rim), :] = north_ref[...]
    x[pl.ds(rim, rim), :] = south_ref[...]
    copies[0].wait()

    def pairs(j):
        kv_ref[:, pl.ds(j, TILE)] = dot(x[...], w[:, pl.ds(j, TILE)]).astype(BF)

    tiles_of(2 * model, pairs)


def near_back_loop(q_ref, kv, kv_rows, wts, cols, mix, dmix, dkv, scores, ds, put):
    cells, model = q_ref.shape

    @pl.loop(0, model // (PAIR * GROUP))
    def _(g):
        heads, deltas = [], []
        for k in range(GROUP):
            h = g * GROUP + k
            keys = pl.ds(pl.multiple_of(h * PAIR, PAIR), PAIR)
            vals = pl.ds(pl.multiple_of(model + h * PAIR, PAIR), PAIR)
            heads.append((h, keys, vals))
            grad = dmix[:, keys]
            scores[k, :, pl.ds(0, cols.size)] = dot(stacked(grad), kv[kv_rows, vals], NT)
            deltas.append(lane_sums(grad.astype(F32) * mix[:, keys].astype(F32)))
        for k, (h, keys, vals) in enumerate(heads):
            for s in range(2):
                for i in range(0, cells, CHUNK):
                    rows = pl.ds(s * cells + i, CHUNK)
                    ds[k, rows, :] = (
                        wts[h, rows, cols].astype(F32)
                        * (scores[k, rows, pl.ds(0, cols.size)] - deltas[k][s][i : i + CHUNK])
                    ).astype(BF)
        for k, (h, keys, vals) in enumerate(heads):
            put(keys, merged(dot(ds[k], kv[kv_rows, keys])))
            dkv[:, keys] = dot(stacked(q_ref[:, keys]), ds[k], TN).T.astype(BF)
            dkv[:, vals] = dot(stacked(dmix[:, keys]), wts[h, :, cols], TN).T.astype(BF)


def near_kernel(
    q_ref, west_ref, east_ref, base_ref, inside_ref, state_ref, cot_ref, dh_ref, gain_ref,
    kvo_hbm, kvr_hbm, wn_hbm, wo_hbm, wu_hbm,
    after_ref, hid_ref, dwest_ref, deast_ref, dq_ref, wts_hbm, mix, dmix, dafter_ref,
    wkv, wo, wu, kv, dkv, x, wts, scores, ds, bias, nrm, du, acc, dab, sems, out_sems,
):
    cells, model = state_ref.shape
    keys_all = kv.shape[0]
    ext = 2 * cells
    side = west_ref.shape[0]
    ends = ext + 2 * side
    copies = fetch(
        [kvo_hbm, kvr_hbm, wn_hbm.at[:, pl.ds(model, 2 * model)], wo_hbm, wu_hbm],
        [kv.at[pl.ds(0, cells), :], kv.at[pl.ds(cells, cells), :], wkv, wo, wu],
        sems,
    )
    x[pl.ds(0, side), :] = west_ref[...]
    x[pl.ds(side, side), :] = east_ref[...]
    kv[pl.ds(ends, keys_all - ends), :] = jnp.zeros((keys_all - ends, 2 * model), BF)
    bias[...] = base_ref[...].astype(F32) + inside_ref[0:1, :]
    copies[0].wait()
    copies[1].wait()
    copies[2].wait()

    def project(j):
        kv[pl.ds(ext, 2 * side), pl.ds(j, TILE)] = dot(
            x[...], wkv[:, pl.ds(j, TILE)]
        ).astype(BF)

    tiles_of(2 * model, project)

    @pl.loop(0, model // (PAIR * GROUP))
    def _(g):
        heads = []
        for k in range(GROUP):
            h = g * GROUP + k
            keys = pl.ds(pl.multiple_of(h * PAIR, PAIR), PAIR)
            vals = pl.ds(pl.multiple_of(model + h * PAIR, PAIR), PAIR)
            heads.append((h, keys, vals))
            scores[k] = dot(stacked(q_ref[:, keys]), kv[:, keys], NT)
        for k, (h, keys, vals) in enumerate(heads):
            for start in range(0, 2 * cells, CHUNK):
                rows = pl.ds(start, CHUNK)
                v = scores[k, rows, :] + bias[pl.ds(start % cells, CHUNK), :]
                v = jnp.exp(v - jnp.max(v, -1, keepdims=True))
                inverse = 1.0 / jnp.sum(v, -1, keepdims=True)
                wts[h, rows, :] = (v * inverse).astype(BF)
        for k, (h, keys, vals) in enumerate(heads):
            mix[:, keys] = merged(dot(wts[h], kv[:, vals])).astype(BF)

    leaving = fetch([wts.at[:, :, pl.ds(0, ext)]], [wts_hbm], out_sems)
    copies[3].wait()

    def project_out(j):
        after_ref[:, pl.ds(j, TILE)] = state_ref[:, pl.ds(j, TILE)] + dot(
            mix[...], wo[:, pl.ds(j, TILE)]
        )

    tiles_of(model, project_out)
    for rows in row_chunks(cells):
        normed, _ = unit(after_ref[rows, :])
        nrm[rows, :] = (normed * gain_ref[2:3, :]).astype(BF)
    copies[4].wait()

    def feed(j):
        cols = pl.ds(j, FEED_TILE)
        u = dot(nrm[...], wu[:, cols])
        square = u * u
        t = jnp.tanh(GELU_C * (u + GELU_A * (square * u)))
        half = 0.5 * (1.0 + t)
        hid_ref[:, cols] = (u * half).astype(BF)
        slope = half + (0.5 * GELU_C) * u * (1.0 - t * t) * (1.0 + 3.0 * GELU_A * square)
        du[:, cols] = (dh_ref[:, cols].astype(F32) * slope).astype(BF)

    tiles_of(du.shape[1], feed, FEED_TILE)

    def feed_back(j):
        acc[:, pl.ds(j, TILE)] = dot(du[...], wu[pl.ds(j, TILE), :], NT)

    tiles_of(model, feed_back)
    for rows in row_chunks(cells):
        grad = acc[rows, :].astype(BF).astype(F32)
        total = cot_ref[rows, :].astype(F32) + norm_pull(
            after_ref[rows, :], gain_ref[2:3, :], grad
        )
        dafter_ref[rows, :] = total
        dab[rows, :] = total.astype(BF)

    def mix_back(j):
        dmix[:, pl.ds(j, TILE)] = dot(dab[...], wo[pl.ds(j, TILE), :], NT).astype(BF)

    tiles_of(model, mix_back)

    outer = pl.ds(ext, keys_all - ext)

    def put(keys, dq):
        dq_ref[:, keys] = dq

    near_back_loop(q_ref, kv, outer, wts, outer, mix, dmix, dkv, scores, ds, put)

    def rim_back(j):
        both = dot(dkv[pl.ds(0, 2 * side), :], wkv[pl.ds(j, TILE), :], NT).astype(BF)
        dwest_ref[:, pl.ds(j, TILE)] = both[:side]
        deast_ref[:, pl.ds(j, TILE)] = both[side:]

    tiles_of(model, rim_back)
    for copy in leaving:
        copy.wait()


def middle_back_kernel(
    q_ref, kvo_ref, kvr_ref, mix, dmix, dq_in_ref, wts_hbm, wn_hbm,
    dq_ref, down_ref, dn_ref, wkv, kv, dkv, wts, scores, ds, sems,
):
    cells, model = q_ref.shape
    part = cells - PAIR
    copies = fetch(
        [wts_hbm.at[:, :, pl.ds(PAIR, kv.shape[0])], wn_hbm.at[:, pl.ds(model, 2 * model)]],
        [wts, wkv],
        sems,
    )
    kv[pl.ds(0, part), :] = kvo_ref[pl.ds(PAIR, part), :]
    kv[pl.ds(part, cells), :] = kvr_ref[...]
    copies[0].wait()

    def put(keys, dq):
        dq_ref[:, keys] = dq + dq_in_ref[:, keys]

    whole = pl.ds(0, kv.shape[0])
    near_back_loop(q_ref, kv, whole, wts, whole, mix, dmix, dkv, scores, ds, put)
    down_ref[...] = dkv[pl.ds(0, part), :]
    copies[1].wait()

    def back(j):
        dn_ref[:, pl.ds(j, TILE)] = dot(
            dkv[pl.ds(part, cells), :], wkv[pl.ds(j, TILE), :], NT
        )

    tiles_of(model, back)


def encode_kernel(after_ref, hid_ref, wd_hbm, _, enc_ref, wd, sems):
    copies = fetch([wd_hbm], [wd], sems)
    copies[0].wait()

    def down(j):
        enc_ref[:, pl.ds(j, TILE)] = (
            after_ref[:, pl.ds(j, TILE)] + dot(hid_ref[...], wd[:, pl.ds(j, TILE)])
        ).astype(BF)

    tiles_of(after_ref.shape[1], down)


def fold_kernel(dn_ref, from_east_ref, from_west_ref, sel_ref, north_ref, south_ref, x):
    rim, model = north_ref.shape
    side = from_east_ref.shape[0]
    x[pl.ds(0, side), :] = from_west_ref[...]
    x[pl.ds(side, side), :] = from_east_ref[...]

    def fold(j):
        cols = pl.ds(j, TILE)
        total = (dn_ref[:, cols] + dot(sel_ref[...], x[:, cols], TN)).astype(BF)
        north_ref[:, cols] = total[:rim]
        south_ref[:, cols] = total[rim:]

    tiles_of(model, fold)


def own_back_kernel(
    q_ref, kvo_ref, mix, dmix, dq_in_ref, down_ref, from_east_ref, from_west_ref, sel_ref,
    wts_hbm, w_hbm, _, dn_ref, dqkv, dkv, wts, scores, ds, x, w, sems,
):
    copies = fetch([wts_hbm.at[:, :, pl.ds(0, PAIR)], w_hbm], [wts, w], sems)
    cells, model = q_ref.shape
    side = from_east_ref.shape[0]
    x[pl.ds(0, side), :] = from_west_ref[...]
    x[pl.ds(side, side), :] = from_east_ref[...]
    copies[0].wait()

    def put(keys, dq):
        dqkv[:, keys] = ((dq + dq_in_ref[:, keys]) * HALF ** (-0.5)).astype(BF)

    whole = pl.ds(0, PAIR)
    near_back_loop(q_ref, kvo_ref, whole, wts, whole, mix, dmix, dkv, scores, ds, put)
    dqkv[pl.ds(0, PAIR), pl.ds(model, 2 * model)] = dkv[...]
    dqkv[pl.ds(PAIR, cells - PAIR), pl.ds(model, 2 * model)] = down_ref[...]
    copies[1].wait()

    def back(j):
        cols = pl.ds(j, TILE)
        dn_ref[:, cols] = dot(dqkv[...], w[cols, :], NT) + dot(
            sel_ref[...], x[:, cols], TN
        )

    tiles_of(model, back)


def cross_back_kernel(
    dn_ref, north_ref, south_ref, state_ref, dafter_ref, gain_ref, q_ref, own_ref, pairs_ref,
    wts_ref, mix_ref, ow_ref, wp_hbm, wo_hbm,
    dstate_hbm, slot_hbm, dq_hbm, down_hbm,
    wp, wo, dsb, dmix, dpairs, scores, ds, dstate_ref, dq_ref, down_ref, slot_ref, sems, out_sems,
):
    copies = fetch([wo_hbm, wp_hbm], [wo, wp], sems)
    cells, model = state_ref.shape
    rim = north_ref.shape[0]
    for i in range(0, cells, CHUNK):
        rows = pl.ds(i, CHUNK)
        other = north_ref[rows, :] if i < rim else south_ref[pl.ds(i - rim, CHUNK), :]
        grad = (dn_ref[rows, :] + other.astype(F32)).astype(BF).astype(F32)
        total = dafter_ref[rows, :] + norm_pull(state_ref[rows, :], gain_ref[1:2, :], grad)
        dstate_ref[rows, :] = total
        dsb[rows, :] = total.astype(BF)
    copies[0].wait()

    def mix_back(j):
        dmix[:, pl.ds(j, TILE)] = dot(dsb[...], wo[pl.ds(j, TILE), :], NT).astype(BF)

    tiles_of(model, mix_back)

    @pl.loop(0, model // (PAIR * GROUP))
    def _(g):
        heads, deltas, own_dots = [], [], []
        for k in range(GROUP):
            h = g * GROUP + k
            keys = pl.ds(pl.multiple_of(h * PAIR, PAIR), PAIR)
            vals = pl.ds(pl.multiple_of(model + h * PAIR, PAIR), PAIR)
            heads.append((h, keys, vals))
            grad = dmix[:, keys]
            grad_f = grad.astype(F32)
            scores[k] = dot(stacked(grad), pairs_ref[:, vals], NT)
            deltas.append(lane_sums(grad_f * mix_ref[:, keys].astype(F32)))
            own_dots.append(lane_sums(grad_f * own_ref[:, vals].astype(F32)))
        for k, (h, keys, vals) in enumerate(heads):
            for s in range(2):
                for i in range(0, cells, CHUNK):
                    rows = pl.ds(s * cells + i, CHUNK)
                    ds[k, rows, :] = (
                        wts_ref[h, rows, :].astype(F32)
                        * (scores[k, rows, :] - deltas[k][s][i : i + CHUNK])
                    ).astype(BF)
        for k, (h, keys, vals) in enumerate(heads):
            lanes = iota((cells, PAIR), 1) < HALF
            weight = ow_ref[:, keys].astype(F32)
            own_grad = weight * jnp.where(
                lanes, own_dots[k][0] - deltas[k][0], own_dots[k][1] - deltas[k][1]
            )
            q = q_ref[:, keys]
            grad = dmix[:, keys]
            dq = merged(dot(ds[k], pairs_ref[:, keys]))
            dq = dq + own_grad * own_ref[:, keys].astype(F32)
            dq_ref[:, keys] = (dq * HALF ** (-0.5)).astype(BF)
            down_ref[:, keys] = (own_grad * q.astype(F32)).astype(BF)
            down_ref[:, vals] = (weight * grad.astype(F32)).astype(BF)
            dpairs[:, keys] = dot(stacked(q), ds[k], TN).T.astype(BF)
            dpairs[:, vals] = dot(stacked(grad), wts_ref[h], TN).T.astype(BF)

    leaving = fetch(
        [dstate_ref, dq_ref, down_ref], [dstate_hbm, dq_hbm, down_hbm],
        out_sems.at[pl.ds(0, 3)],
    )
    copies[1].wait()
    half = model // 2
    for i in range(2):
        cols = pl.ds(i * half, half)
        grads = dot(dpairs[...], wp[cols, :], NT).astype(BF)
        slot_ref[:, :, cols] = grads.reshape(slot_ref.shape[:2] + (half,))
        leaving += fetch(
            [slot_ref.at[:, :, cols]], [slot_hbm.at[:, :, cols]], out_sems.at[pl.ds(3 + i, 1)]
        )
    for copy in leaving:
        copy.wait()


def gather_kernel(place_hbm, ret_ref, out_ref, place_ref, ret, sems):
    copies = fetch([place_hbm], [place_ref], sems)
    ret[...] = ret_ref[...].reshape(ret.shape)
    copies[0].wait()
    out_ref[...] = dot(place_ref[...], ret[...], TN).astype(BF)


def grid_back_kernel(
    grid_ref, dstate_ref, gain_ref, dq_ref, down_ref, wq_hbm, wp_hbm, out_ref, wq, wp, acc, sems
):
    copies = fetch([wq_hbm, wp_hbm], [wq, wp], sems)
    cells, model = grid_ref.shape
    for copy in copies:
        copy.wait()

    def back(j):
        acc[:, pl.ds(j, TILE)] = dot(dq_ref[...], wq[pl.ds(j, TILE), :], NT) + dot(
            down_ref[...], wp[pl.ds(j, TILE), :], NT
        )

    tiles_of(model, back)
    for rows in row_chunks(cells):
        grad = acc[rows, :].astype(BF).astype(F32)
        out_ref[rows, :] = (
            dstate_ref[rows, :]
            + norm_pull(grid_ref[rows, :].astype(F32), gain_ref[0:1, :], grad)
        ).astype(BF)


def ring(value, by):
    size = lax.axis_size("lon")
    return lax.ppermute(value, "lon", [(i, (i + by) % size) for i in range(size)])


def line(value, by):
    size = lax.axis_size("lat")
    pairs = [(i, i + by) for i in range(size) if 0 <= i + by < size]
    return lax.ppermute(value, "lat", pairs)


def key_places(rows_lat, rows_lon):
    places = [(r, c) for r in range(rows_lat) for c in range(rows_lon)]
    places += [(r, c) for r in range(-RADIUS, 0) for c in range(rows_lon)]
    places += [(rows_lat + r, c) for r in range(RADIUS) for c in range(rows_lon)]
    ext = list(places)
    tall = range(-RADIUS, rows_lat + RADIUS)
    places += [(r, c) for r in tall for c in range(-RADIUS, 0)]
    places += [(r, rows_lon + c) for r in tall for c in range(RADIUS)]
    return np.array(places), ext


def per_device(
    grid_state, observations, obs_tile, obs_cell, cotangent, norm_gains,
    w_cross_query, w_cross_pairs, w_cross_out, w_near_proj, w_near_out, w_up, w_down,
):
    rows_lat, rows_lon, model = grid_state.shape
    lat_count = lax.axis_size("lat")
    devices = lat_count * lax.axis_size("lon")
    rows_obs = observations.shape[0]
    cap = max(2, 2 * rows_obs // devices)
    slots = devices * cap
    cells = rows_lat * rows_lon
    ff = w_up.shape[1]
    pairs_n = model // PAIR
    rim = RADIUS * rows_lon
    side = RADIUS * (rows_lat + 2 * RADIUS)
    places, ext_places = key_places(rows_lat, rows_lon)
    keys_n = len(places)
    keys_all = -(-keys_n // 256) * 256
    spot = {place: i for i, place in enumerate(ext_places)}
    tall = range(-RADIUS, rows_lat + RADIUS)
    select = np.zeros((2 * side, len(ext_places)), np.float32)
    for i, r in enumerate(tall):
        for c in range(RADIUS):
            select[i * RADIUS + c, spot[(r, c)]] = 1.0
            select[side + i * RADIUS + c, spot[(r, rows_lon - RADIUS + c)]] = 1.0
    select = select.astype(jnp.bfloat16)
    base = np.full((cells, keys_all), LOW_SCORE, np.float32)
    own_rows, own_cols = places[:cells, 0], places[:cells, 1]
    allowed = (np.abs(places[None, :, 0] - own_rows[:, None]) <= RADIUS) & (
        np.abs(places[None, :, 1] - own_cols[:, None]) <= RADIUS
    )
    base[:, :keys_n][allowed] = 0.0
    base = jnp.asarray(base.astype(jnp.bfloat16))
    key_rows = np.zeros((8, keys_all), np.int32)
    key_rows[:, :keys_n] = places[None, :, 0]
    key_lat = jnp.asarray(key_rows) + lax.axis_index("lat") * rows_lat
    inside = jnp.where((key_lat >= 0) & (key_lat < rows_lat * lat_count), 0.0, LOW_SCORE)
    inside = inside.astype(F32)

    dma = pltpu.SemaphoreType.DMA
    vm = pltpu.VMEM
    flat = grid_state.reshape(cells, model)
    cot = cotangent.reshape(cells, model)

    payload, placing = call(
        functools.partial(place_kernel, devices=devices, cap=cap, wide=rows_lon),
        (obs_tile.reshape(1, rows_obs), obs_cell.reshape(1, rows_obs), observations), "hhh",
        [((devices, cap, model + 128), BF, "h"), ((slots, rows_obs), BF, "h")],
        [vm((1, rows_obs), jnp.int32), vm((1, rows_obs), jnp.int32), vm((rows_obs, model), BF),
         vm((devices, cap, model + 128), BF), vm((slots, rows_obs), BF), dma((3,))],
        2 * rows_obs * slots * model, "place",
    )
    arrived = lax.all_to_all(payload, ("lat", "lon"), 0, 0, tiled=True)
    q_c, own_pairs, dhid = call(
        grid_kernel,
        (flat, cot, norm_gains, w_cross_query, w_cross_pairs, w_down), "hhvhhh",
        [((cells, model), BF, "h"), ((cells, 2 * model), BF, "h"), ((cells, ff), BF, "h")],
        [vm((cells, model), BF), vm((cells, model), BF), vm((cells, model), BF),
         vm((cells, 2 * model), BF), vm((cells, ff), BF),
         vm((cells, model), BF), vm((model, model), BF), vm((model, 2 * model), BF),
         vm((ff, model), BF), dma((5,)), dma((3,))],
        2 * cells * model * (3 * model + ff), "grid_proj",
    )
    state, top, bottom, slot_pairs, cross_w, cross_mix, own_w = call(
        functools.partial(cross_kernel, wide=rows_lon),
        (arrived, flat, q_c, own_pairs, norm_gains, w_cross_pairs, w_cross_out), "vhhhvhh",
        [((cells, model), F32, "h"), ((rim, model), BF), ((rim, model), BF),
         ((slots, 2 * model), BF, "h"), ((pairs_n, 2 * cells, slots), BF, "h"),
         ((cells, model), BF, "h"), ((cells, model), BF, "h")],
        [vm((slots, model + 128), BF), vm((model, 2 * model), BF), vm((model, model), BF),
         vm((GROUP, 2 * cells, slots), F32), vm((cells, slots), F32), vm((cells, model), BF),
         vm((cells, model), BF), vm((cells, 2 * model), BF), vm((cells, model), F32),
         vm((slots, 2 * model), BF), vm((pairs_n, 2 * cells, slots), BF), vm((cells, model), BF),
         vm((cells, model), BF), dma((2 * model // TILE,)), dma((9,))],
        2 * slots * model * 2 * model * 2, "cross",
    )
    south = line(top, -1)
    north = line(bottom, 1)
    q_n, kv_own = call(
        near_own_kernel, (top, bottom, w_near_proj), "vva",
        [((cells, model), BF), ((cells, 2 * model), BF)],
        [vm((cells, model), BF), vm((model, 3 * model), BF), dma((2,))],
        2 * cells * model * 3 * model, "near_own",
    )
    west_send, east_send = call(
        rim_kernel, (top, bottom, north, south, jnp.asarray(select), kv_own), "vvvvva",
        [((side, model), BF), ((side, model), BF)],
        [vm((cells + 2 * rim, model), BF)],
        2 * 2 * side * 2 * cells * model, "rim",
    )
    east = ring(west_send, -1)
    west = ring(east_send, 1)
    kv_rows = call(
        near_rows_kernel, (north, south, w_near_proj), "vva",
        [((2 * rim, 2 * model), BF)],
        [vm((2 * rim, model), BF), vm((model, 2 * model), BF), dma((1,))],
        2 * 2 * rim * model * 2 * model, "near_rows",
    )
    after, hidden, dwest, deast, dq_rim, near_w, near_mix, dmix, dafter = call(
        near_kernel,
        (q_n, west, east, base, inside, state, cot, dhid, norm_gains, kv_own, kv_rows,
         w_near_proj, w_near_out, w_up), "vvvvvvvvvaaaaa",
        [((cells, model), F32), ((cells, ff), BF), ((side, model), BF), ((side, model), BF),
         ((cells, model), F32), ((pairs_n, 2 * cells, 2 * cells), BF, "h"), ((cells, model), BF),
         ((cells, model), BF), ((cells, model), F32)],
        [vm((model, 2 * model), BF), vm((model, model), BF), vm((model, ff), BF),
         vm((keys_all, 2 * model), BF), vm((keys_all - 2 * cells, 2 * model), BF),
         vm((2 * side, model), BF), vm((pairs_n, 2 * cells, keys_all), BF),
         vm((GROUP, 2 * cells, keys_all), F32),
         vm((GROUP, 2 * cells, keys_all - 2 * cells), BF),
         vm((cells, keys_all), F32), vm((cells, model), BF),
         vm((cells, ff), BF), vm((cells, model), F32), vm((cells, model), BF),
         dma((5,)), dma((1,))],
        2e10, "near",
    )
    from_east = ring(dwest, -1)
    from_west = ring(deast, 1)
    middle = 2 * cells - PAIR
    dq_most, down_part, dn_rows = call(
        middle_back_kernel,
        (q_n, kv_own, kv_rows, near_mix, dmix, dq_rim, near_w, w_near_proj), "vvvvvvha",
        [((cells, model), F32), ((cells - PAIR, 2 * model), BF), ((2 * rim, model), F32)],
        [vm((model, 2 * model), BF), vm((middle, 2 * model), BF), vm((middle, 2 * model), BF),
         vm((pairs_n, 2 * cells, middle), BF), vm((GROUP, 2 * cells, middle), F32),
         vm((GROUP, 2 * cells, middle), BF), dma((2,))],
        4 * cells * model * 2 * model, "middle_back",
    )
    dnorth, dsouth = call(
        fold_kernel, (dn_rows, from_east, from_west, jnp.asarray(select[:, cells:])), "vvvv",
        [((rim, model), BF), ((rim, model), BF)],
        [vm((2 * side, model), BF)],
        2 * 2 * side * 2 * rim * model, "fold",
    )
    from_south = line(dnorth, -1)
    from_north = line(dsouth, 1)
    dn_own = call(
        own_back_kernel,
        (q_n, kv_own, near_mix, dmix, dq_most, down_part, from_east, from_west,
         jnp.asarray(select[:, :cells]), near_w, w_near_proj, dnorth), "vvvvvvvvvhaa",
        [((cells, model), F32)],
        [vm((cells, 3 * model), BF), vm((PAIR, 2 * model), BF),
         vm((pairs_n, 2 * cells, PAIR), BF), vm((GROUP, 2 * cells, PAIR), F32),
         vm((GROUP, 2 * cells, PAIR), BF), vm((2 * side, model), BF),
         vm((model, 3 * model), BF), dma((2,))],
        2 * cells * model * 4 * model, "own_back",
    )
    dstate, slot_grads, dq, down = call(
        cross_back_kernel,
        (dn_own, from_north, from_south, state, dafter, norm_gains, q_c, own_pairs, slot_pairs,
         cross_w, cross_mix, own_w, w_cross_pairs, w_cross_out), "vvvvvvvvvvvvaa",
        [((cells, model), F32, "h"), ((devices, cap, model), BF, "h"),
         ((cells, model), BF, "h"), ((cells, 2 * model), BF, "h")],
        [vm((model, 2 * model), BF), vm((model, model), BF), vm((cells, model), BF),
         vm((cells, model), BF), vm((slots, 2 * model), BF), vm((GROUP, 2 * cells, slots), F32),
         vm((GROUP, 2 * cells, slots), BF), vm((cells, model), F32), vm((cells, model), BF),
         vm((cells, 2 * model), BF), vm((devices, cap, model), BF), dma((2,)), dma((5,))],
        2 * slots * model * 2 * model * 2, "cross_back",
    )
    returned = lax.all_to_all(slot_grads, ("lat", "lon"), 0, 0, tiled=True)
    encoded = call(
        encode_kernel, (after, hidden, w_down, dq), "vvaa", [((cells, model), BF)],
        [vm((ff, model), BF), dma((1,))], 2 * cells * model * ff, "encode",
    )
    grid_grad = call(
        grid_back_kernel,
        (flat, dstate, norm_gains, dq, down, w_cross_query, w_cross_pairs), "vvvvvaa",
        [((cells, model), BF)],
        [vm((model, model), BF), vm((model, 2 * model), BF), vm((cells, model), F32), dma((2,))],
        2 * cells * model * 3 * model, "grid_back",
    )
    obs_grad = call(
        gather_kernel, (placing, returned), "hv", [((rows_obs, model), BF)],
        [vm((slots, rows_obs), BF), vm((slots, model), BF), dma((1,))], 2 * rows_obs * slots * model, "gather",
    )
    shape = (rows_lat, rows_lon, model)
    return encoded.reshape(shape), grid_grad.reshape(shape), obs_grad


def solution(mesh):
    return jax.shard_map(
        per_device,
        mesh=mesh,
        in_specs=(
            P("lat", "lon", None),
            P(("lat", "lon"), None),
            P(("lat", "lon"), None),
            P(("lat", "lon"), None),
            P("lat", "lon", None),
            P(), P(), P(), P(), P(), P(), P(), P(),
        ),
        out_specs=(P("lat", "lon", None), P("lat", "lon", None), P(("lat", "lon"), None)),
        check_vma=False,
    )
```

```python
import functools

import jax
import jax.numpy as jnp
import numpy as np
from jax import lax
from jax.experimental import pallas as pl
from jax.experimental.pallas import tpu as pltpu
from jax.sharding import PartitionSpec as P

HEADS = 16
RADIUS = 6
EPSILON = 1e-05
SPREAD = 32.0
LOW_SCORE = -1e30

BF = jnp.bfloat16
F32 = jnp.float32
NN = (((1,), (0,)), ((), ()))
NT = (((1,), (1,)), ((), ()))
TN = (((0,), (0,)), ((), ()))
CHUNK = 32
SOFT = 32
TILE = 1024
PAIR = 128
HALF = 64
SLACK_BYTES = 8 * 2**20
FEED_TILE = 1024
GROUP = 2
GELU_C = 0.7978845608028654
GELU_A = 0.044715


def dot(left, right, dims=NN):
    return lax.dot_general(left, right, dims, preferred_element_type=F32)


def iota(shape, dim):
    return lax.broadcasted_iota(jnp.int32, shape, dim)


def tiles_of(count, body, tile=TILE):
    @pl.loop(0, count // tile)
    def _(i):
        body(pl.multiple_of(i * tile, tile))


def row_chunks(count):
    return [pl.ds(i, CHUNK) for i in range(0, count, CHUNK)]


def unit(values):
    center = values - jnp.mean(values, -1, keepdims=True)
    scale = lax.rsqrt(jnp.mean(center * center, -1, keepdims=True) + EPSILON)
    return center * scale, scale


def norm_pull(values, gain, grad):
    normed, scale = unit(values)
    inner = grad * gain
    return scale * (
        inner
        - jnp.mean(inner, -1, keepdims=True)
        - normed * jnp.mean(inner * normed, -1, keepdims=True)
    )


def head_masks():
    left = (iota((1, PAIR), 1) < HALF).astype(F32)
    return left.astype(BF), (1.0 - left).astype(BF)


def stacked(values):
    left, right = head_masks()
    return jnp.concatenate([values * left, values * right], axis=0)


def merged(values):
    count = values.shape[0] // 2
    lanes = iota((count, PAIR), 1) < HALF
    return jnp.where(lanes, values[:count], values[count:])


def lane_sums(values):
    lanes = iota(values.shape, 1) < HALF
    first = jnp.sum(jnp.where(lanes, values, 0.0), -1, keepdims=True)
    second = jnp.sum(jnp.where(lanes, 0.0, values), -1, keepdims=True)
    return first, second


def fetch(sources, targets, sems):
    copies = [
        pltpu.make_async_copy(source, target, sems.at[i])
        for i, (source, target) in enumerate(zip(sources, targets))
    ]
    for copy in copies:
        copy.start()
    return copies


def call(body, ins, kinds, outs, scratch, flops, name):
    any_spec = pl.BlockSpec(memory_space=pl.ANY)
    vmem_spec = pl.BlockSpec(memory_space=pltpu.VMEM)
    moved = sum(x.size * x.dtype.itemsize for x in ins)
    moved += sum(int(np.prod(o[0])) * jnp.dtype(o[1]).itemsize for o in outs)
    held = sum(x.size * x.dtype.itemsize for x, k in zip(ins, kinds) if k == "v")
    held += sum(int(np.prod(o[0])) * jnp.dtype(o[1]).itemsize for o in outs if len(o) == 2)
    for item in scratch:
        if jnp.issubdtype(item.dtype, jnp.floating):
            held += int(np.prod(item.shape)) * jnp.dtype(item.dtype).itemsize
    single = len(outs) == 1
    shapes = [
        jax.ShapeDtypeStruct(*o) if len(o) == 2 else pltpu.HBM(o[0], o[1]) for o in outs
    ]
    specs = [vmem_spec if len(o) == 2 else any_spec for o in outs]
    ins = [
        pltpu.with_memory_space_constraint(x, pltpu.HBM) if k == "h" else x
        for x, k in zip(ins, kinds)
    ]
    return pl.pallas_call(
        body,
        name=name,
        out_shape=shapes[0] if single else shapes,
        in_specs=[vmem_spec if k == "v" else any_spec for k in kinds],
        out_specs=specs[0] if single else specs,
        scratch_shapes=scratch,
        compiler_params=pltpu.CompilerParams(vmem_limit_bytes=held + SLACK_BYTES),
        cost_estimate=pl.CostEstimate(
            flops=int(flops), bytes_accessed=int(moved), transcendentals=0
        ),
    )(*ins)


def place_kernel(
    tile_hbm, cell_hbm, obs_hbm, pay_hbm, place_hbm,
    tile_ref, cell_ref, obs_ref, pay_ref, place_ref, sems, *, devices, cap, wide,
):
    copies = fetch([tile_hbm, cell_hbm, obs_hbm], [tile_ref, cell_ref, obs_ref], sems)
    copies[0].wait()
    rows, model = obs_ref.shape
    slots = devices * cap
    tile = tile_ref[...]
    member = tile == iota((devices, rows), 0)
    earlier = (iota((rows, rows), 0) < iota((rows, rows), 1)).astype(F32).astype(BF)
    before = dot(member.astype(F32).astype(BF), earlier)
    rank = jnp.sum(jnp.where(member, before, 0.0), 0, keepdims=True).astype(jnp.int32)
    slot = tile * cap + rank
    placing = (slot == iota((slots, rows), 0)).astype(F32).astype(BF)
    place_ref[...] = placing
    copies[1].wait()
    copies[2].wait()
    cell = cell_ref[...]
    shift = wide.bit_length() - 1
    line_no = iota((128, rows), 0)
    codes = jnp.where(
        line_no == 0, (cell >> shift) + 1, jnp.where(line_no == 1, (cell & (wide - 1)) + 1, 0)
    )
    code_rows = dot(placing, codes.astype(F32).astype(BF), NT).astype(BF)
    pay_ref[:, :, model:] = code_rows.reshape(devices, cap, 128)
    moved = dot(placing, obs_ref[...]).astype(BF)
    pay_ref[:, :, :model] = moved.reshape(devices, cap, model)
    for copy in fetch([pay_ref, place_ref], [pay_hbm, place_hbm], sems):
        copy.wait()


def grid_kernel(
    grid_hbm, cot_hbm, gain_ref, wq_hbm, wp_hbm, wd_hbm, q_hbm, own_hbm, dh_hbm,
    grid_ref, cot_ref, q_ref, own_ref, dh_ref, nrm, wq, wp, wd, sems, out_sems,
):
    first, *copies = fetch(
        [grid_hbm, wq_hbm, wp_hbm, wd_hbm, cot_hbm], [grid_ref, wq, wp, wd, cot_ref], sems
    )
    cells, model = grid_ref.shape
    first.wait()
    for rows in row_chunks(cells):
        normed, _ = unit(grid_ref[rows, :].astype(F32))
        nrm[rows, :] = (normed * gain_ref[0:1, :]).astype(BF)
    copies[0].wait()

    def query(j):
        q_ref[:, pl.ds(j, TILE)] = (
            dot(nrm[...], wq[:, pl.ds(j, TILE)]) * HALF ** (-0.5)
        ).astype(BF)

    tiles_of(model, query)
    copies[1].wait()

    def own(j):
        own_ref[:, pl.ds(j, TILE)] = dot(nrm[...], wp[:, pl.ds(j, TILE)]).astype(BF)

    tiles_of(2 * model, own)
    copies[2].wait()
    copies[3].wait()

    def hidden(j):
        dh_ref[:, pl.ds(j, TILE)] = dot(cot_ref[...], wd[pl.ds(j, TILE), :], NT).astype(BF)

    tiles_of(dh_ref.shape[1], hidden)
    for copy in fetch([q_ref, own_ref, dh_ref], [q_hbm, own_hbm, dh_hbm], out_sems):
        copy.wait()


def cross_kernel(
    arr_ref, grid_hbm, q_hbm, own_hbm, gain_ref, wp_hbm, wo_hbm,
    state_hbm, top_ref, bottom_ref, pairs_hbm, wts_hbm, mix_hbm, ow_hbm,
    arr, wp, wo, scores, bias, grid_ref, q_ref, own_ref, state_ref, pairs_ref, wts_ref,
    mix_ref, ow_ref, sems, out_sems, *, wide,
):
    cells, model = grid_ref.shape
    parts = [pl.ds(j, TILE) for j in range(0, 2 * model, TILE)]
    copies = fetch([wp_hbm.at[:, c] for c in parts], [wp.at[:, c] for c in parts], sems)
    lates = out_sems.at[pl.ds(5, 4)]
    rim = top_ref.shape[0]
    slots = arr.shape[0]
    arr[...] = arr_ref[...].reshape(arr.shape)
    pick = (iota((8, 128), 0) == iota((8, 128), 1)).astype(F32).astype(BF)
    codes = dot(pick, arr[:, model:], NT)
    cell = iota((cells, slots), 0)
    shift = wide.bit_length() - 1
    row_gap = (cell >> shift).astype(F32) - (codes[0:1] - 1.0)
    col_gap = (cell & (wide - 1)).astype(F32) - (codes[1:2] - 1.0)
    near = -(row_gap * row_gap + col_gap * col_gap) * (1.0 / SPREAD)
    bias[...] = jnp.where(codes[0:1] > 0.5, near, LOW_SCORE)
    for i, cols in enumerate(parts):
        copies[i].wait()
        if i == 0:
            late = fetch(
                [q_hbm, own_hbm, wo_hbm, grid_hbm], [q_ref, own_ref, wo, grid_ref], lates
            )
        pairs_ref[:, cols] = dot(arr[:, :model], wp[:, cols]).astype(BF)
    leaving = fetch([pairs_ref], [pairs_hbm], out_sems.at[pl.ds(0, 1)])
    late[0].wait()
    late[1].wait()

    def soften(h, k, own_scores):
        own_weights = []
        for side in range(2):
            parts = []
            for i in range(0, cells, SOFT):
                own_score = own_scores[side][i : i + SOFT]
                x = scores[k, pl.ds(side * cells + i, SOFT), :] + bias[pl.ds(i, SOFT), :]
                peak = jnp.maximum(jnp.max(x, -1, keepdims=True), own_score)
                x = jnp.exp(x - peak)
                own_weight = jnp.exp(own_score - peak)
                inverse = 1.0 / (jnp.sum(x, -1, keepdims=True) + own_weight)
                wts_ref[h, pl.ds(side * cells + i, SOFT), :] = (x * inverse).astype(BF)
                parts.append(own_weight * inverse)
            own_weights.append(jnp.concatenate(parts, axis=0))
        lanes = iota((cells, PAIR), 1) < HALF
        return jnp.where(lanes, own_weights[0], own_weights[1]).astype(BF)

    @pl.loop(0, model // (PAIR * GROUP))
    def _(g):
        heads, own_scores, weights = [], [], []
        for k in range(GROUP):
            h = g * GROUP + k
            keys = pl.ds(pl.multiple_of(h * PAIR, PAIR), PAIR)
            vals = pl.ds(pl.multiple_of(model + h * PAIR, PAIR), PAIR)
            heads.append((h, keys, vals))
            q = q_ref[:, keys]
            scores[k] = dot(stacked(q), pairs_ref[:, keys], NT)
            own_scores.append(lane_sums(q.astype(F32) * own_ref[:, keys].astype(F32)))
        for k, (h, keys, vals) in enumerate(heads):
            weights.append(soften(h, k, own_scores[k]))
            ow_ref[:, keys] = weights[k]
        for k, (h, keys, vals) in enumerate(heads):
            mix = merged(dot(wts_ref[h], pairs_ref[:, vals]))
            mix_ref[:, keys] = (
                mix + weights[k].astype(F32) * own_ref[:, vals].astype(F32)
            ).astype(BF)

    leaving += fetch(
        [wts_ref, mix_ref, ow_ref], [wts_hbm, mix_hbm, ow_hbm], out_sems.at[pl.ds(1, 3)]
    )
    late[2].wait()
    late[3].wait()

    def project_out(j):
        state_ref[:, pl.ds(j, TILE)] = grid_ref[:, pl.ds(j, TILE)].astype(F32) + dot(
            mix_ref[...], wo[:, pl.ds(j, TILE)]
        )

    tiles_of(model, project_out)
    leaving += fetch([state_ref], [state_hbm], out_sems.at[pl.ds(4, 1)])
    for i in range(0, cells, CHUNK):
        normed, _ = unit(state_ref[pl.ds(i, CHUNK), :])
        normed = (normed * gain_ref[1:2, :]).astype(BF)
        if i < rim:
            top_ref[pl.ds(i, CHUNK), :] = normed
        else:
            bottom_ref[pl.ds(i - rim, CHUNK), :] = normed
    for copy in leaving:
        copy.wait()


def near_own_kernel(top_ref, bottom_ref, w_hbm, q_ref, kv_ref, nrm, w, sems):
    cells, model = nrm.shape
    rim = top_ref.shape[0]
    copies = fetch(
        [w_hbm.at[:, pl.ds(0, model)], w_hbm.at[:, pl.ds(model, 2 * model)]],
        [w.at[:, pl.ds(0, model)], w.at[:, pl.ds(model, 2 * model)]],
        sems,
    )
    nrm[pl.ds(0, rim), :] = top_ref[...]
    nrm[pl.ds(rim, rim), :] = bottom_ref[...]
    copies[0].wait()

    def query(j):
        q_ref[:, pl.ds(j, TILE)] = (
            dot(nrm[...], w[:, pl.ds(j, TILE)]) * HALF ** (-0.5)
        ).astype(BF)

    tiles_of(model, query)
    copies[1].wait()

    def pairs(j):
        kv_ref[:, pl.ds(j, TILE)] = dot(
            nrm[...], w[:, pl.ds(pl.multiple_of(model + j, TILE), TILE)]
        ).astype(BF)

    tiles_of(2 * model, pairs)


def rim_kernel(
    top_ref, bottom_ref, north_ref, south_ref, sel_ref, _, west_ref, east_ref, ext
):
    rim, model = north_ref.shape
    for i, part in enumerate((top_ref, bottom_ref, north_ref, south_ref)):
        ext[pl.ds(i * rim, rim), :] = part[...]
    side = west_ref.shape[0]

    def pick(j):
        both = dot(sel_ref[...], ext[:, pl.ds(j, TILE)]).astype(BF)
        west_ref[:, pl.ds(j, TILE)] = both[:side]
        east_ref[:, pl.ds(j, TILE)] = both[side:]

    tiles_of(model, pick)


def spread(first, second):
    lanes = iota((first.shape[0], PAIR), 1) < HALF
    return jnp.where(lanes, first, second)


def inner_kernel(
    north_ref, south_ref, q_ref, kvo_ref, base_ref, inside_ref, w_hbm,
    kvr_ref, wts_hbm, mix_ref, peak_ref, sum_ref,
    x, w, kv, bias, scores, wts, sems, out_sems,
):
    rim, model = north_ref.shape
    cells = q_ref.shape[0]
    copies = fetch([w_hbm.at[:, pl.ds(model, 2 * model)]], [w], sems)
    x[pl.ds(0, rim), :] = north_ref[...]
    x[pl.ds(rim, rim), :] = south_ref[...]
    kv[pl.ds(0, cells), :] = kvo_ref[...]
    bias[...] = base_ref[...].astype(F32) + inside_ref[0:1, :]
    copies[0].wait()

    def pairs(j):
        part = dot(x[...], w[:, pl.ds(j, TILE)]).astype(BF)
        kvr_ref[:, pl.ds(j, TILE)] = part
        kv[pl.ds(cells, cells), pl.ds(j, TILE)] = part

    tiles_of(2 * model, pairs)

    @pl.loop(0, model // (PAIR * GROUP))
    def _(g):
        heads = []
        for k in range(GROUP):
            h = g * GROUP + k
            keys = pl.ds(pl.multiple_of(h * PAIR, PAIR), PAIR)
            vals = pl.ds(pl.multiple_of(model + h * PAIR, PAIR), PAIR)
            heads.append((h, keys, vals))
            scores[k] = dot(stacked(q_ref[:, keys]), kv[:, keys], NT)
        for k, (h, keys, vals) in enumerate(heads):
            for i in range(0, cells, SOFT):
                peaks, sums = [], []
                for side in range(2):
                    rows = pl.ds(side * cells + i, SOFT)
                    v = scores[k, rows, :] + bias[pl.ds(i, SOFT), :]
                    peak = jnp.max(v, -1, keepdims=True)
                    v = jnp.exp(v - peak)
                    wts[h, rows, :] = v.astype(BF)
                    peaks.append(peak)
                    sums.append(jnp.sum(v, -1, keepdims=True))
                peak_ref[pl.ds(i, SOFT), keys] = spread(*peaks)
                sum_ref[pl.ds(i, SOFT), keys] = spread(*sums)
        for k, (h, keys, vals) in enumerate(heads):
            mix_ref[:, keys] = merged(dot(wts[h], kv[:, vals]))

    for copy in fetch([wts], [wts_hbm], out_sems):
        copy.wait()


def near_back_loop(q_ref, kv, kv_rows, wts, cols, mix, dmix, dkv, scores, ds, put):
    cells, model = q_ref.shape

    @pl.loop(0, model // (PAIR * GROUP))
    def _(g):
        heads, deltas = [], []
        for k in range(GROUP):
            h = g * GROUP + k
            keys = pl.ds(pl.multiple_of(h * PAIR, PAIR), PAIR)
            vals = pl.ds(pl.multiple_of(model + h * PAIR, PAIR), PAIR)
            heads.append((h, keys, vals))
            grad = dmix[:, keys]
            scores[k, :, pl.ds(0, cols.size)] = dot(stacked(grad), kv[kv_rows, vals], NT)
            deltas.append(lane_sums(grad.astype(F32) * mix[:, keys].astype(F32)))
        for k, (h, keys, vals) in enumerate(heads):
            for s in range(2):
                for i in range(0, cells, SOFT):
                    rows = pl.ds(s * cells + i, SOFT)
                    ds[k, rows, :] = (
                        wts[h, rows, cols].astype(F32)
                        * (scores[k, rows, pl.ds(0, cols.size)] - deltas[k][s][i : i + SOFT])
                    ).astype(BF)
        for k, (h, keys, vals) in enumerate(heads):
            put(keys, merged(dot(ds[k], kv[kv_rows, keys])))
            dkv[:, keys] = dot(stacked(q_ref[:, keys]), ds[k], TN).T.astype(BF)
            dkv[:, vals] = dot(stacked(dmix[:, keys]), wts[h, :, cols], TN).T.astype(BF)


def near_kernel(
    q_ref, west_ref, east_ref, base_ref, inside_ref, state_ref, cot_ref, dh_ref, gain_ref,
    mix_in_ref, peak_ref, sum_ref, wn_hbm, wo_hbm, wu_hbm,
    after_ref, hid_ref, dwest_ref, deast_ref, dq_ref, mix, dscaled_ref, dafter_ref,
    wkv, wo, wu, kv, dkv, x, wts, scores, ds, bias, share, nrm, du, acc, dab, dmix, sems,
):
    cells, model = state_ref.shape
    keys_all = kv.shape[0]
    side = west_ref.shape[0]
    ends = 2 * side
    copies = fetch(
        [wn_hbm.at[:, pl.ds(model, 2 * model)], wo_hbm, wu_hbm], [wkv, wo, wu], sems
    )
    x[pl.ds(0, side), :] = west_ref[...]
    x[pl.ds(side, side), :] = east_ref[...]
    kv[pl.ds(ends, keys_all - ends), :] = jnp.zeros((keys_all - ends, 2 * model), BF)
    bias[...] = base_ref[...].astype(F32) + inside_ref[0:1, :]
    copies[0].wait()

    def project(j):
        kv[pl.ds(0, ends), pl.ds(j, TILE)] = dot(x[...], wkv[:, pl.ds(j, TILE)]).astype(BF)

    tiles_of(2 * model, project)

    @pl.loop(0, model // (PAIR * GROUP))
    def _(g):
        heads = []
        for k in range(GROUP):
            h = g * GROUP + k
            keys = pl.ds(pl.multiple_of(h * PAIR, PAIR), PAIR)
            vals = pl.ds(pl.multiple_of(model + h * PAIR, PAIR), PAIR)
            heads.append((h, keys, vals))
            scores[k] = dot(stacked(q_ref[:, keys]), kv[:, keys], NT)
        for k, (h, keys, vals) in enumerate(heads):
            for i in range(0, cells, SOFT):
                here = pl.ds(i, SOFT)
                peaks, sums = peak_ref[here, keys], sum_ref[here, keys]
                shares = []
                for s in range(2):
                    rows = pl.ds(s * cells + i, SOFT)
                    before = peaks[:, s * HALF : s * HALF + 1]
                    v = scores[k, rows, :] + bias[here, :]
                    peak = jnp.maximum(jnp.max(v, -1, keepdims=True), before)
                    v = jnp.exp(v - peak)
                    part = jnp.exp(before - peak)
                    total = jnp.sum(v, -1, keepdims=True)
                    total = total + part * sums[:, s * HALF : s * HALF + 1]
                    inverse = 1.0 / total
                    wts[h, rows, :] = (v * inverse).astype(BF)
                    shares.append(part * inverse)
                share[here, keys] = spread(*shares)
        for k, (h, keys, vals) in enumerate(heads):
            rims = merged(dot(wts[h], kv[:, vals]))
            mix[:, keys] = (rims + mix_in_ref[:, keys] * share[:, keys]).astype(BF)

    copies[1].wait()

    def project_out(j):
        after_ref[:, pl.ds(j, TILE)] = state_ref[:, pl.ds(j, TILE)] + dot(
            mix[...], wo[:, pl.ds(j, TILE)]
        )

    tiles_of(model, project_out)
    for rows in row_chunks(cells):
        normed, _ = unit(after_ref[rows, :])
        nrm[rows, :] = (normed * gain_ref[2:3, :]).astype(BF)
    copies[2].wait()

    def feed(j):
        cols = pl.ds(j, FEED_TILE)
        u = dot(nrm[...], wu[:, cols])
        square = u * u
        t = jnp.tanh(GELU_C * (u + GELU_A * (square * u)))
        half = 0.5 * (1.0 + t)
        hid_ref[:, cols] = (u * half).astype(BF)
        slope = half + (0.5 * GELU_C) * u * (1.0 - t * t) * (1.0 + 3.0 * GELU_A * square)
        du[:, cols] = (dh_ref[:, cols].astype(F32) * slope).astype(BF)

    tiles_of(du.shape[1], feed, FEED_TILE)

    def feed_back(j):
        acc[:, pl.ds(j, TILE)] = dot(du[...], wu[pl.ds(j, TILE), :], NT)

    tiles_of(model, feed_back)
    for rows in row_chunks(cells):
        grad = acc[rows, :].astype(BF).astype(F32)
        total = cot_ref[rows, :].astype(F32) + norm_pull(
            after_ref[rows, :], gain_ref[2:3, :], grad
        )
        dafter_ref[rows, :] = total
        dab[rows, :] = total.astype(BF)

    def mix_back(j):
        cols = pl.ds(j, TILE)
        grad = dot(dab[...], wo[cols, :], NT)
        dmix[:, cols] = grad.astype(BF)
        dscaled_ref[:, cols] = (grad * share[:, cols]).astype(BF)

    tiles_of(model, mix_back)
    outer = pl.ds(0, keys_all)

    def put(keys, dq):
        dq_ref[:, keys] = dq

    near_back_loop(q_ref, kv, outer, wts, outer, mix, dmix, dkv, scores, ds, put)

    def rim_back(j):
        both = dot(dkv[pl.ds(0, 2 * side), :], wkv[pl.ds(j, TILE), :], NT).astype(BF)
        dwest_ref[:, pl.ds(j, TILE)] = both[:side]
        deast_ref[:, pl.ds(j, TILE)] = both[side:]

    tiles_of(model, rim_back)


def middle_back_kernel(
    q_ref, kvo_ref, kvr_ref, mix, dmix, dq_in_ref, wts_hbm, wn_hbm,
    dq_ref, down_ref, dn_ref, wkv, kv, dkv, wts, scores, ds, sems,
):
    cells, model = q_ref.shape
    part = cells - PAIR
    copies = fetch(
        [wts_hbm.at[:, :, pl.ds(PAIR, kv.shape[0])], wn_hbm.at[:, pl.ds(model, 2 * model)]],
        [wts, wkv],
        sems,
    )
    kv[pl.ds(0, part), :] = kvo_ref[pl.ds(PAIR, part), :]
    kv[pl.ds(part, cells), :] = kvr_ref[...]
    copies[0].wait()

    def put(keys, dq):
        dq_ref[:, keys] = dq + dq_in_ref[:, keys]

    whole = pl.ds(0, kv.shape[0])
    near_back_loop(q_ref, kv, whole, wts, whole, mix, dmix, dkv, scores, ds, put)
    down_ref[...] = dkv[pl.ds(0, part), :]
    copies[1].wait()

    def back(j):
        dn_ref[:, pl.ds(j, TILE)] = dot(
            dkv[pl.ds(part, cells), :], wkv[pl.ds(j, TILE), :], NT
        )

    tiles_of(model, back)


def encode_kernel(after_ref, hid_ref, wd_hbm, _, enc_ref, wd, sems):
    copies = fetch([wd_hbm], [wd], sems)
    copies[0].wait()

    def down(j):
        enc_ref[:, pl.ds(j, TILE)] = (
            after_ref[:, pl.ds(j, TILE)] + dot(hid_ref[...], wd[:, pl.ds(j, TILE)])
        ).astype(BF)

    tiles_of(after_ref.shape[1], down)


def fold_kernel(dn_ref, from_east_ref, from_west_ref, sel_ref, north_ref, south_ref, x):
    rim, model = north_ref.shape
    side = from_east_ref.shape[0]
    x[pl.ds(0, side), :] = from_west_ref[...]
    x[pl.ds(side, side), :] = from_east_ref[...]

    def fold(j):
        cols = pl.ds(j, TILE)
        total = (dn_ref[:, cols] + dot(sel_ref[...], x[:, cols], TN)).astype(BF)
        north_ref[:, cols] = total[:rim]
        south_ref[:, cols] = total[rim:]

    tiles_of(model, fold)


def own_back_kernel(
    q_ref, kvo_ref, mix, dmix, dq_in_ref, down_ref, from_east_ref, from_west_ref, sel_ref,
    wts_hbm, w_hbm, _, dn_ref, dqkv, dkv, wts, scores, ds, x, w, sems,
):
    copies = fetch([wts_hbm.at[:, :, pl.ds(0, PAIR)], w_hbm], [wts, w], sems)
    cells, model = q_ref.shape
    side = from_east_ref.shape[0]
    x[pl.ds(0, side), :] = from_west_ref[...]
    x[pl.ds(side, side), :] = from_east_ref[...]
    copies[0].wait()

    def put(keys, dq):
        dqkv[:, keys] = ((dq + dq_in_ref[:, keys]) * HALF ** (-0.5)).astype(BF)

    whole = pl.ds(0, PAIR)
    near_back_loop(q_ref, kvo_ref, whole, wts, whole, mix, dmix, dkv, scores, ds, put)
    dqkv[pl.ds(0, PAIR), pl.ds(model, 2 * model)] = dkv[...]
    dqkv[pl.ds(PAIR, cells - PAIR), pl.ds(model, 2 * model)] = down_ref[...]
    copies[1].wait()

    def back(j):
        cols = pl.ds(j, TILE)
        dn_ref[:, cols] = dot(dqkv[...], w[cols, :], NT) + dot(
            sel_ref[...], x[:, cols], TN
        )

    tiles_of(model, back)


def cross_back_kernel(
    dn_ref, north_ref, south_ref, state_ref, dafter_ref, gain_ref, q_ref, own_ref, pairs_ref,
    wts_ref, mix_ref, ow_ref, wp_hbm, wo_hbm,
    dstate_hbm, slot_hbm, dq_hbm, down_hbm,
    wp, wo, dsb, dmix, dpairs, scores, ds, dstate_ref, dq_ref, down_ref, slot_ref, sems, out_sems,
):
    copies = fetch([wo_hbm, wp_hbm], [wo, wp], sems)
    cells, model = state_ref.shape
    rim = north_ref.shape[0]
    for i in range(0, cells, CHUNK):
        rows = pl.ds(i, CHUNK)
        other = north_ref[rows, :] if i < rim else south_ref[pl.ds(i - rim, CHUNK), :]
        grad = (dn_ref[rows, :] + other.astype(F32)).astype(BF).astype(F32)
        total = dafter_ref[rows, :] + norm_pull(state_ref[rows, :], gain_ref[1:2, :], grad)
        dstate_ref[rows, :] = total
        dsb[rows, :] = total.astype(BF)
    copies[0].wait()

    def mix_back(j):
        dmix[:, pl.ds(j, TILE)] = dot(dsb[...], wo[pl.ds(j, TILE), :], NT).astype(BF)

    tiles_of(model, mix_back)

    @pl.loop(0, model // (PAIR * GROUP))
    def _(g):
        heads, deltas, own_dots = [], [], []
        for k in range(GROUP):
            h = g * GROUP + k
            keys = pl.ds(pl.multiple_of(h * PAIR, PAIR), PAIR)
            vals = pl.ds(pl.multiple_of(model + h * PAIR, PAIR), PAIR)
            heads.append((h, keys, vals))
            grad = dmix[:, keys]
            grad_f = grad.astype(F32)
            scores[k] = dot(stacked(grad), pairs_ref[:, vals], NT)
            deltas.append(lane_sums(grad_f * mix_ref[:, keys].astype(F32)))
            own_dots.append(lane_sums(grad_f * own_ref[:, vals].astype(F32)))
        for k, (h, keys, vals) in enumerate(heads):
            for s in range(2):
                for i in range(0, cells, SOFT):
                    rows = pl.ds(s * cells + i, SOFT)
                    ds[k, rows, :] = (
                        wts_ref[h, rows, :].astype(F32)
                        * (scores[k, rows, :] - deltas[k][s][i : i + SOFT])
                    ).astype(BF)
        for k, (h, keys, vals) in enumerate(heads):
            lanes = iota((cells, PAIR), 1) < HALF
            weight = ow_ref[:, keys].astype(F32)
            own_grad = weight * jnp.where(
                lanes, own_dots[k][0] - deltas[k][0], own_dots[k][1] - deltas[k][1]
            )
            q = q_ref[:, keys]
            grad = dmix[:, keys]
            dq = merged(dot(ds[k], pairs_ref[:, keys]))
            dq = dq + own_grad * own_ref[:, keys].astype(F32)
            dq_ref[:, keys] = (dq * HALF ** (-0.5)).astype(BF)
            down_ref[:, keys] = (own_grad * q.astype(F32)).astype(BF)
            down_ref[:, vals] = (weight * grad.astype(F32)).astype(BF)
            dpairs[:, keys] = dot(stacked(q), ds[k], TN).T.astype(BF)
            dpairs[:, vals] = dot(stacked(grad), wts_ref[h], TN).T.astype(BF)

    leaving = fetch(
        [dstate_ref, dq_ref, down_ref], [dstate_hbm, dq_hbm, down_hbm],
        out_sems.at[pl.ds(0, 3)],
    )
    copies[1].wait()
    half = model // 2
    for i in range(2):
        cols = pl.ds(i * half, half)
        grads = dot(dpairs[...], wp[cols, :], NT).astype(BF)
        slot_ref[:, :, cols] = grads.reshape(slot_ref.shape[:2] + (half,))
        leaving += fetch(
            [slot_ref.at[:, :, cols]], [slot_hbm.at[:, :, cols]], out_sems.at[pl.ds(3 + i, 1)]
        )
    for copy in leaving:
        copy.wait()


def gather_kernel(place_hbm, ret_ref, out_ref, place_ref, ret, sems):
    copies = fetch([place_hbm], [place_ref], sems)
    ret[...] = ret_ref[...].reshape(ret.shape)
    copies[0].wait()
    out_ref[...] = dot(place_ref[...], ret[...], TN).astype(BF)


def grid_back_kernel(
    grid_ref, dstate_ref, gain_ref, dq_ref, down_ref, wq_hbm, wp_hbm, out_ref, wq, wp, acc, sems
):
    copies = fetch([wq_hbm, wp_hbm], [wq, wp], sems)
    cells, model = grid_ref.shape
    for copy in copies:
        copy.wait()

    def back(j):
        acc[:, pl.ds(j, TILE)] = dot(dq_ref[...], wq[pl.ds(j, TILE), :], NT) + dot(
            down_ref[...], wp[pl.ds(j, TILE), :], NT
        )

    tiles_of(model, back)
    for rows in row_chunks(cells):
        grad = acc[rows, :].astype(BF).astype(F32)
        out_ref[rows, :] = (
            dstate_ref[rows, :]
            + norm_pull(grid_ref[rows, :].astype(F32), gain_ref[0:1, :], grad)
        ).astype(BF)


def ring(value, by):
    size = lax.axis_size("lon")
    return lax.ppermute(value, "lon", [(i, (i + by) % size) for i in range(size)])


def line(value, by):
    size = lax.axis_size("lat")
    pairs = [(i, i + by) for i in range(size) if 0 <= i + by < size]
    return lax.ppermute(value, "lat", pairs)


def key_places(rows_lat, rows_lon):
    places = [(r, c) for r in range(rows_lat) for c in range(rows_lon)]
    places += [(r, c) for r in range(-RADIUS, 0) for c in range(rows_lon)]
    places += [(rows_lat + r, c) for r in range(RADIUS) for c in range(rows_lon)]
    ext = list(places)
    tall = range(-RADIUS, rows_lat + RADIUS)
    places += [(r, c) for r in tall for c in range(-RADIUS, 0)]
    places += [(r, rows_lon + c) for r in tall for c in range(RADIUS)]
    return np.array(places), ext


def per_device(
    grid_state, observations, obs_tile, obs_cell, cotangent, norm_gains,
    w_cross_query, w_cross_pairs, w_cross_out, w_near_proj, w_near_out, w_up, w_down,
):
    rows_lat, rows_lon, model = grid_state.shape
    lat_count = lax.axis_size("lat")
    devices = lat_count * lax.axis_size("lon")
    rows_obs = observations.shape[0]
    cap = max(2, 2 * rows_obs // devices)
    slots = devices * cap
    cells = rows_lat * rows_lon
    ff = w_up.shape[1]
    pairs_n = model // PAIR
    rim = RADIUS * rows_lon
    side = RADIUS * (rows_lat + 2 * RADIUS)
    places, ext_places = key_places(rows_lat, rows_lon)
    keys_n = len(places)
    keys_all = -(-keys_n // 256) * 256
    spot = {place: i for i, place in enumerate(ext_places)}
    tall = range(-RADIUS, rows_lat + RADIUS)
    select = np.zeros((2 * side, len(ext_places)), np.float32)
    for i, r in enumerate(tall):
        for c in range(RADIUS):
            select[i * RADIUS + c, spot[(r, c)]] = 1.0
            select[side + i * RADIUS + c, spot[(r, rows_lon - RADIUS + c)]] = 1.0
    select = select.astype(jnp.bfloat16)
    base = np.full((cells, keys_all), LOW_SCORE, np.float32)
    own_rows, own_cols = places[:cells, 0], places[:cells, 1]
    allowed = (np.abs(places[None, :, 0] - own_rows[:, None]) <= RADIUS) & (
        np.abs(places[None, :, 1] - own_cols[:, None]) <= RADIUS
    )
    base[:, :keys_n][allowed] = 0.0
    base = base.astype(jnp.bfloat16)
    key_rows = np.zeros((8, keys_all), np.int32)
    key_rows[:, :keys_n] = places[None, :, 0]
    key_lat = jnp.asarray(key_rows) + lax.axis_index("lat") * rows_lat
    inside = jnp.where((key_lat >= 0) & (key_lat < rows_lat * lat_count), 0.0, LOW_SCORE)
    inside = inside.astype(F32)

    dma = pltpu.SemaphoreType.DMA
    vm = pltpu.VMEM
    flat = grid_state.reshape(cells, model)
    cot = cotangent.reshape(cells, model)

    payload, placing = call(
        functools.partial(place_kernel, devices=devices, cap=cap, wide=rows_lon),
        (obs_tile.reshape(1, rows_obs), obs_cell.reshape(1, rows_obs), observations), "hhh",
        [((devices, cap, model + 128), BF, "h"), ((slots, rows_obs), BF, "h")],
        [vm((1, rows_obs), jnp.int32), vm((1, rows_obs), jnp.int32), vm((rows_obs, model), BF),
         vm((devices, cap, model + 128), BF), vm((slots, rows_obs), BF), dma((3,))],
        2 * rows_obs * slots * model, "place",
    )
    arrived = lax.all_to_all(payload, ("lat", "lon"), 0, 0, tiled=True)
    q_c, own_pairs, dhid = call(
        grid_kernel,
        (flat, cot, norm_gains, w_cross_query, w_cross_pairs, w_down), "hhvhhh",
        [((cells, model), BF, "h"), ((cells, 2 * model), BF, "h"), ((cells, ff), BF, "h")],
        [vm((cells, model), BF), vm((cells, model), BF), vm((cells, model), BF),
         vm((cells, 2 * model), BF), vm((cells, ff), BF),
         vm((cells, model), BF), vm((model, model), BF), vm((model, 2 * model), BF),
         vm((ff, model), BF), dma((5,)), dma((3,))],
        2 * cells * model * (3 * model + ff), "grid_proj",
    )
    state, top, bottom, slot_pairs, cross_w, cross_mix, own_w = call(
        functools.partial(cross_kernel, wide=rows_lon),
        (arrived, flat, q_c, own_pairs, norm_gains, w_cross_pairs, w_cross_out), "vhhhvhh",
        [((cells, model), F32, "h"), ((rim, model), BF), ((rim, model), BF),
         ((slots, 2 * model), BF, "h"), ((pairs_n, 2 * cells, slots), BF, "h"),
         ((cells, model), BF, "h"), ((cells, model), BF, "h")],
        [vm((slots, model + 128), BF), vm((model, 2 * model), BF), vm((model, model), BF),
         vm((GROUP, 2 * cells, slots), F32), vm((cells, slots), F32), vm((cells, model), BF),
         vm((cells, model), BF), vm((cells, 2 * model), BF), vm((cells, model), F32),
         vm((slots, 2 * model), BF), vm((pairs_n, 2 * cells, slots), BF), vm((cells, model), BF),
         vm((cells, model), BF), dma((2 * model // TILE,)), dma((9,))],
        2 * slots * model * 2 * model * 2, "cross",
    )
    south = line(top, -1)
    north = line(bottom, 1)
    q_n, kv_own = call(
        near_own_kernel, (top, bottom, w_near_proj), "vva",
        [((cells, model), BF), ((cells, 2 * model), BF)],
        [vm((cells, model), BF), vm((model, 3 * model), BF), dma((2,))],
        2 * cells * model * 3 * model, "near_own",
    )
    west_send, east_send = call(
        rim_kernel, (top, bottom, north, south, jnp.asarray(select), kv_own), "vvvvva",
        [((side, model), BF), ((side, model), BF)],
        [vm((cells + 2 * rim, model), BF)],
        2 * 2 * side * 2 * cells * model, "rim",
    )
    east = ring(west_send, -1)
    west = ring(east_send, 1)
    kv_rows, near_w, inner_mix, inner_peak, inner_sum = call(
        inner_kernel,
        (north, south, q_n, kv_own, jnp.asarray(base[:, : 2 * cells]), inside[:, : 2 * cells],
         w_near_proj), "vvvvvva",
        [((2 * rim, 2 * model), BF), ((pairs_n, 2 * cells, 2 * cells), BF, "h"),
         ((cells, model), F32), ((cells, model), F32), ((cells, model), F32)],
        [vm((2 * rim, model), BF), vm((model, 2 * model), BF), vm((2 * cells, 2 * model), BF),
         vm((cells, 2 * cells), F32), vm((GROUP, 2 * cells, 2 * cells), F32),
         vm((pairs_n, 2 * cells, 2 * cells), BF), dma((1,)), dma((1,))],
        4 * rim * model * 2 * model * 2, "inner",
    )
    outer = keys_all - 2 * cells
    after, hidden, dwest, deast, dq_rim, near_mix, dmix, dafter = call(
        near_kernel,
        (q_n, west, east, jnp.asarray(base[:, 2 * cells :]), inside[:, 2 * cells :], state, cot,
         dhid, norm_gains, inner_mix, inner_peak, inner_sum, w_near_proj, w_near_out, w_up),
        "vvvvvvvvvvvvaaa",
        [((cells, model), F32), ((cells, ff), BF), ((side, model), BF), ((side, model), BF),
         ((cells, model), F32), ((cells, model), BF), ((cells, model), BF),
         ((cells, model), F32)],
        [vm((model, 2 * model), BF), vm((model, model), BF), vm((model, ff), BF),
         vm((outer, 2 * model), BF), vm((outer, 2 * model), BF), vm((2 * side, model), BF),
         vm((pairs_n, 2 * cells, outer), BF), vm((GROUP, 2 * cells, outer), F32),
         vm((GROUP, 2 * cells, outer), BF), vm((cells, outer), F32), vm((cells, model), F32),
         vm((cells, model), BF), vm((cells, ff), BF), vm((cells, model), F32),
         vm((cells, model), BF), vm((cells, model), BF), dma((3,))],
        2e10, "near",
    )
    from_east = ring(dwest, -1)
    from_west = ring(deast, 1)
    middle = 2 * cells - PAIR
    dq_most, down_part, dn_rows = call(
        middle_back_kernel,
        (q_n, kv_own, kv_rows, near_mix, dmix, dq_rim, near_w, w_near_proj), "vvvvvvha",
        [((cells, model), F32), ((cells - PAIR, 2 * model), BF), ((2 * rim, model), F32)],
        [vm((model, 2 * model), BF), vm((middle, 2 * model), BF), vm((middle, 2 * model), BF),
         vm((pairs_n, 2 * cells, middle), BF), vm((GROUP, 2 * cells, middle), F32),
         vm((GROUP, 2 * cells, middle), BF), dma((2,))],
        4 * cells * model * 2 * model, "middle_back",
    )
    dnorth, dsouth = call(
        fold_kernel, (dn_rows, from_east, from_west, jnp.asarray(select[:, cells:])), "vvvv",
        [((rim, model), BF), ((rim, model), BF)],
        [vm((2 * side, model), BF)],
        2 * 2 * side * 2 * rim * model, "fold",
    )
    from_south = line(dnorth, -1)
    from_north = line(dsouth, 1)
    dn_own = call(
        own_back_kernel,
        (q_n, kv_own, near_mix, dmix, dq_most, down_part, from_east, from_west,
         jnp.asarray(select[:, :cells]), near_w, w_near_proj, dnorth), "vvvvvvvvvhaa",
        [((cells, model), F32)],
        [vm((cells, 3 * model), BF), vm((PAIR, 2 * model), BF),
         vm((pairs_n, 2 * cells, PAIR), BF), vm((GROUP, 2 * cells, PAIR), F32),
         vm((GROUP, 2 * cells, PAIR), BF), vm((2 * side, model), BF),
         vm((model, 3 * model), BF), dma((2,))],
        2 * cells * model * 4 * model, "own_back",
    )
    dstate, slot_grads, dq, down = call(
        cross_back_kernel,
        (dn_own, from_north, from_south, state, dafter, norm_gains, q_c, own_pairs, slot_pairs,
         cross_w, cross_mix, own_w, w_cross_pairs, w_cross_out), "vvvvvvvvvvvvaa",
        [((cells, model), F32, "h"), ((devices, cap, model), BF, "h"),
         ((cells, model), BF, "h"), ((cells, 2 * model), BF, "h")],
        [vm((model, 2 * model), BF), vm((model, model), BF), vm((cells, model), BF),
         vm((cells, model), BF), vm((slots, 2 * model), BF), vm((GROUP, 2 * cells, slots), F32),
         vm((GROUP, 2 * cells, slots), BF), vm((cells, model), F32), vm((cells, model), BF),
         vm((cells, 2 * model), BF), vm((devices, cap, model), BF), dma((2,)), dma((5,))],
        2 * slots * model * 2 * model * 2, "cross_back",
    )
    returned = lax.all_to_all(slot_grads, ("lat", "lon"), 0, 0, tiled=True)
    encoded = call(
        encode_kernel, (after, hidden, w_down, dq), "vvaa", [((cells, model), BF)],
        [vm((ff, model), BF), dma((1,))], 2 * cells * model * ff, "encode",
    )
    grid_grad = call(
        grid_back_kernel,
        (flat, dstate, norm_gains, dq, down, w_cross_query, w_cross_pairs), "vvvvvaa",
        [((cells, model), BF)],
        [vm((model, model), BF), vm((model, 2 * model), BF), vm((cells, model), F32), dma((2,))],
        2 * cells * model * 3 * model, "grid_back",
    )
    obs_grad = call(
        gather_kernel, (placing, returned), "hv", [((rows_obs, model), BF)],
        [vm((slots, rows_obs), BF), vm((slots, model), BF), dma((1,))], 2 * rows_obs * slots * model, "gather",
    )
    shape = (rows_lat, rows_lon, model)
    return encoded.reshape(shape), grid_grad.reshape(shape), obs_grad


def solution(mesh):
    return jax.shard_map(
        per_device,
        mesh=mesh,
        in_specs=(
            P("lat", "lon", None),
            P(("lat", "lon"), None),
            P(("lat", "lon"), None),
            P(("lat", "lon"), None),
            P("lat", "lon", None),
            P(), P(), P(), P(), P(), P(), P(), P(),
        ),
        out_specs=(P("lat", "lon", None), P("lat", "lon", None), P(("lat", "lon"), None)),
        check_vma=False,
    )
```

```python
import functools

import jax
import jax.numpy as jnp
import numpy as np
from jax import lax
from jax.experimental import pallas as pl
from jax.experimental.pallas import tpu as pltpu
from jax.sharding import PartitionSpec as P

HEADS = 16
RADIUS = 6
EPSILON = 1e-05
SPREAD = 32.0
LOW_SCORE = -1e30

BF = jnp.bfloat16
F32 = jnp.float32
NN = (((1,), (0,)), ((), ()))
NT = (((1,), (1,)), ((), ()))
TN = (((0,), (0,)), ((), ()))
CHUNK = 32
SOFT = 32
TILE = 1024
PAIR = 128
HALF = 64
SLACK_BYTES = 8 * 2**20
FEED_TILE = 1024
GROUP = 2
GELU_C = 0.7978845608028654
GELU_A = 0.044715


def dot(left, right, dims=NN):
    return lax.dot_general(left, right, dims, preferred_element_type=F32)


def iota(shape, dim):
    return lax.broadcasted_iota(jnp.int32, shape, dim)


def tiles_of(count, body, tile=TILE):
    @pl.loop(0, count // tile)
    def _(i):
        body(pl.multiple_of(i * tile, tile))


def row_chunks(count):
    return [pl.ds(i, CHUNK) for i in range(0, count, CHUNK)]


def unit(values):
    center = values - jnp.mean(values, -1, keepdims=True)
    scale = lax.rsqrt(jnp.mean(center * center, -1, keepdims=True) + EPSILON)
    return center * scale, scale


def norm_pull(values, gain, grad):
    normed, scale = unit(values)
    inner = grad * gain
    return scale * (
        inner
        - jnp.mean(inner, -1, keepdims=True)
        - normed * jnp.mean(inner * normed, -1, keepdims=True)
    )


def head_masks():
    left = (iota((1, PAIR), 1) < HALF).astype(F32)
    return left.astype(BF), (1.0 - left).astype(BF)


def stacked(values):
    left, right = head_masks()
    return jnp.concatenate([values * left, values * right], axis=0)


def merged(values):
    count = values.shape[0] // 2
    lanes = iota((count, PAIR), 1) < HALF
    return jnp.where(lanes, values[:count], values[count:])


def lane_sums(values):
    lanes = iota(values.shape, 1) < HALF
    first = jnp.sum(jnp.where(lanes, values, 0.0), -1, keepdims=True)
    second = jnp.sum(jnp.where(lanes, 0.0, values), -1, keepdims=True)
    return first, second


def fetch(sources, targets, sems):
    copies = [
        pltpu.make_async_copy(source, target, sems.at[i])
        for i, (source, target) in enumerate(zip(sources, targets))
    ]
    for copy in copies:
        copy.start()
    return copies


def call(body, ins, kinds, outs, scratch, flops, name):
    any_spec = pl.BlockSpec(memory_space=pl.ANY)
    vmem_spec = pl.BlockSpec(memory_space=pltpu.VMEM)
    moved = sum(x.size * x.dtype.itemsize for x in ins)
    moved += sum(int(np.prod(o[0])) * jnp.dtype(o[1]).itemsize for o in outs)
    held = sum(x.size * x.dtype.itemsize for x, k in zip(ins, kinds) if k == "v")
    held += sum(int(np.prod(o[0])) * jnp.dtype(o[1]).itemsize for o in outs if len(o) == 2)
    for item in scratch:
        if jnp.issubdtype(item.dtype, jnp.floating):
            held += int(np.prod(item.shape)) * jnp.dtype(item.dtype).itemsize
    single = len(outs) == 1
    shapes = [
        jax.ShapeDtypeStruct(*o) if len(o) == 2 else pltpu.HBM(o[0], o[1]) for o in outs
    ]
    specs = [vmem_spec if len(o) == 2 else any_spec for o in outs]
    ins = [
        pltpu.with_memory_space_constraint(x, pltpu.HBM) if k == "h" else x
        for x, k in zip(ins, kinds)
    ]
    return pl.pallas_call(
        body,
        name=name,
        out_shape=shapes[0] if single else shapes,
        in_specs=[vmem_spec if k == "v" else any_spec for k in kinds],
        out_specs=specs[0] if single else specs,
        scratch_shapes=scratch,
        compiler_params=pltpu.CompilerParams(vmem_limit_bytes=held + SLACK_BYTES),
        cost_estimate=pl.CostEstimate(
            flops=int(flops), bytes_accessed=int(moved), transcendentals=0
        ),
    )(*ins)


def place_kernel(
    tile_hbm, cell_hbm, obs_hbm, pay_hbm, place_hbm,
    tile_ref, cell_ref, obs_ref, pay_ref, place_ref, sems, *, devices, cap, wide,
):
    copies = fetch([tile_hbm, cell_hbm, obs_hbm], [tile_ref, cell_ref, obs_ref], sems)
    copies[0].wait()
    rows, model = obs_ref.shape
    slots = devices * cap
    tile = tile_ref[...]
    member = tile == iota((devices, rows), 0)
    earlier = (iota((rows, rows), 0) < iota((rows, rows), 1)).astype(F32).astype(BF)
    before = dot(member.astype(F32).astype(BF), earlier)
    rank = jnp.sum(jnp.where(member, before, 0.0), 0, keepdims=True).astype(jnp.int32)
    slot = tile * cap + rank
    placing = (slot == iota((slots, rows), 0)).astype(F32).astype(BF)
    place_ref[...] = placing
    copies[1].wait()
    copies[2].wait()
    cell = cell_ref[...]
    shift = wide.bit_length() - 1
    line_no = iota((128, rows), 0)
    codes = jnp.where(
        line_no == 0, (cell >> shift) + 1, jnp.where(line_no == 1, (cell & (wide - 1)) + 1, 0)
    )
    code_rows = dot(placing, codes.astype(F32).astype(BF), NT).astype(BF)
    pay_ref[:, :, model:] = code_rows.reshape(devices, cap, 128)
    moved = dot(placing, obs_ref[...]).astype(BF)
    pay_ref[:, :, :model] = moved.reshape(devices, cap, model)
    for copy in fetch([pay_ref, place_ref], [pay_hbm, place_hbm], sems):
        copy.wait()


def grid_kernel(
    grid_hbm, cot_hbm, gain_ref, wq_hbm, wp_hbm, wd_hbm, q_hbm, own_hbm, dh_hbm,
    grid_ref, cot_ref, q_ref, own_ref, dh_ref, nrm, wq, wp, wd, sems, out_sems,
):
    first, *copies = fetch(
        [grid_hbm, wq_hbm, wp_hbm, wd_hbm, cot_hbm], [grid_ref, wq, wp, wd, cot_ref], sems
    )
    cells, model = grid_ref.shape
    first.wait()
    for rows in row_chunks(cells):
        normed, _ = unit(grid_ref[rows, :].astype(F32))
        nrm[rows, :] = (normed * gain_ref[0:1, :]).astype(BF)
    copies[0].wait()

    def query(j):
        q_ref[:, pl.ds(j, TILE)] = (
            dot(nrm[...], wq[:, pl.ds(j, TILE)]) * HALF ** (-0.5)
        ).astype(BF)

    tiles_of(model, query)
    copies[1].wait()

    def own(j):
        own_ref[:, pl.ds(j, TILE)] = dot(nrm[...], wp[:, pl.ds(j, TILE)]).astype(BF)

    tiles_of(2 * model, own)
    copies[2].wait()
    copies[3].wait()

    def hidden(j):
        dh_ref[:, pl.ds(j, TILE)] = dot(cot_ref[...], wd[pl.ds(j, TILE), :], NT).astype(BF)

    tiles_of(dh_ref.shape[1], hidden)
    for copy in fetch([q_ref, own_ref, dh_ref], [q_hbm, own_hbm, dh_hbm], out_sems):
        copy.wait()


def cross_kernel(
    arr_ref, grid_hbm, q_hbm, own_hbm, gain_ref, wp_hbm, wo_hbm,
    state_hbm, top_ref, bottom_ref, pairs_hbm, wts_hbm, mix_hbm, ow_hbm,
    arr, wp, wo, scores, bias, grid_ref, q_ref, own_ref, state_ref, pairs_ref, wts_ref,
    mix_ref, ow_ref, sems, out_sems, *, wide,
):
    cells, model = grid_ref.shape
    parts = [pl.ds(j, TILE) for j in range(0, 2 * model, TILE)]
    copies = fetch([wp_hbm.at[:, c] for c in parts], [wp.at[:, c] for c in parts], sems)
    lates = out_sems.at[pl.ds(5, 4)]
    rim = top_ref.shape[0]
    slots = arr.shape[0]
    arr[...] = arr_ref[...].reshape(arr.shape)
    pick = (iota((8, 128), 0) == iota((8, 128), 1)).astype(F32).astype(BF)
    codes = dot(pick, arr[:, model:], NT)
    cell = iota((cells, slots), 0)
    shift = wide.bit_length() - 1
    row_gap = (cell >> shift).astype(F32) - (codes[0:1] - 1.0)
    col_gap = (cell & (wide - 1)).astype(F32) - (codes[1:2] - 1.0)
    near = -(row_gap * row_gap + col_gap * col_gap) * (1.0 / SPREAD)
    bias[...] = jnp.where(codes[0:1] > 0.5, near, LOW_SCORE)
    for i, cols in enumerate(parts):
        copies[i].wait()
        if i == 0:
            late = fetch(
                [q_hbm, own_hbm, wo_hbm, grid_hbm], [q_ref, own_ref, wo, grid_ref], lates
            )
        pairs_ref[:, cols] = dot(arr[:, :model], wp[:, cols]).astype(BF)
    leaving = fetch([pairs_ref], [pairs_hbm], out_sems.at[pl.ds(0, 1)])
    late[0].wait()
    late[1].wait()

    def soften(h, k, own_scores):
        own_weights = []
        for side in range(2):
            parts = []
            for i in range(0, cells, SOFT):
                own_score = own_scores[side][i : i + SOFT]
                x = scores[k, pl.ds(side * cells + i, SOFT), :] + bias[pl.ds(i, SOFT), :]
                peak = jnp.maximum(jnp.max(x, -1, keepdims=True), own_score)
                x = jnp.exp(x - peak)
                own_weight = jnp.exp(own_score - peak)
                inverse = 1.0 / (jnp.sum(x, -1, keepdims=True) + own_weight)
                wts_ref[h, pl.ds(side * cells + i, SOFT), :] = (x * inverse).astype(BF)
                parts.append(own_weight * inverse)
            own_weights.append(jnp.concatenate(parts, axis=0))
        lanes = iota((cells, PAIR), 1) < HALF
        return jnp.where(lanes, own_weights[0], own_weights[1]).astype(BF)

    @pl.loop(0, model // (PAIR * GROUP))
    def _(g):
        heads, own_scores, weights = [], [], []
        for k in range(GROUP):
            h = g * GROUP + k
            keys = pl.ds(pl.multiple_of(h * PAIR, PAIR), PAIR)
            vals = pl.ds(pl.multiple_of(model + h * PAIR, PAIR), PAIR)
            heads.append((h, keys, vals))
            q = q_ref[:, keys]
            scores[k] = dot(stacked(q), pairs_ref[:, keys], NT)
            own_scores.append(lane_sums(q.astype(F32) * own_ref[:, keys].astype(F32)))
        for k, (h, keys, vals) in enumerate(heads):
            weights.append(soften(h, k, own_scores[k]))
            ow_ref[:, keys] = weights[k]
        for k, (h, keys, vals) in enumerate(heads):
            mix = merged(dot(wts_ref[h], pairs_ref[:, vals]))
            mix_ref[:, keys] = (
                mix + weights[k].astype(F32) * own_ref[:, vals].astype(F32)
            ).astype(BF)

    leaving += fetch(
        [wts_ref, mix_ref, ow_ref], [wts_hbm, mix_hbm, ow_hbm], out_sems.at[pl.ds(1, 3)]
    )
    late[2].wait()
    late[3].wait()

    def project_out(j):
        state_ref[:, pl.ds(j, TILE)] = grid_ref[:, pl.ds(j, TILE)].astype(F32) + dot(
            mix_ref[...], wo[:, pl.ds(j, TILE)]
        )

    tiles_of(model, project_out)
    leaving += fetch([state_ref], [state_hbm], out_sems.at[pl.ds(4, 1)])
    for i in range(0, cells, CHUNK):
        normed, _ = unit(state_ref[pl.ds(i, CHUNK), :])
        normed = (normed * gain_ref[1:2, :]).astype(BF)
        if i < rim:
            top_ref[pl.ds(i, CHUNK), :] = normed
        else:
            bottom_ref[pl.ds(i - rim, CHUNK), :] = normed
    for copy in leaving:
        copy.wait()


def near_own_kernel(top_ref, bottom_ref, w_hbm, q_ref, kv_ref, nrm, w, sems):
    cells, model = nrm.shape
    rim = top_ref.shape[0]
    copies = fetch(
        [w_hbm.at[:, pl.ds(0, model)], w_hbm.at[:, pl.ds(model, 2 * model)]],
        [w.at[:, pl.ds(0, model)], w.at[:, pl.ds(model, 2 * model)]],
        sems,
    )
    nrm[pl.ds(0, rim), :] = top_ref[...]
    nrm[pl.ds(rim, rim), :] = bottom_ref[...]
    copies[0].wait()

    def query(j):
        q_ref[:, pl.ds(j, TILE)] = (
            dot(nrm[...], w[:, pl.ds(j, TILE)]) * HALF ** (-0.5)
        ).astype(BF)

    tiles_of(model, query)
    copies[1].wait()

    def pairs(j):
        kv_ref[:, pl.ds(j, TILE)] = dot(
            nrm[...], w[:, pl.ds(pl.multiple_of(model + j, TILE), TILE)]
        ).astype(BF)

    tiles_of(2 * model, pairs)


def rim_kernel(
    top_ref, bottom_ref, north_ref, south_ref, sel_ref, _, west_ref, east_ref, ext
):
    rim, model = north_ref.shape
    for i, part in enumerate((top_ref, bottom_ref, north_ref, south_ref)):
        ext[pl.ds(i * rim, rim), :] = part[...]
    side = west_ref.shape[0]

    def pick(j):
        both = dot(sel_ref[...], ext[:, pl.ds(j, TILE)]).astype(BF)
        west_ref[:, pl.ds(j, TILE)] = both[:side]
        east_ref[:, pl.ds(j, TILE)] = both[side:]

    tiles_of(model, pick)


def spread(first, second):
    lanes = iota((first.shape[0], PAIR), 1) < HALF
    return jnp.where(lanes, first, second)


def inner_kernel(
    north_ref, south_ref, q_ref, kvo_ref, base_ref, inside_ref, w_hbm,
    kvr_ref, wts_hbm, mix_ref, peak_ref, sum_ref,
    x, w, kv, bias, scores, wts, sems, out_sems,
):
    rim, model = north_ref.shape
    cells = q_ref.shape[0]
    copies = fetch([w_hbm.at[:, pl.ds(model, 2 * model)]], [w], sems)
    x[pl.ds(0, rim), :] = north_ref[...]
    x[pl.ds(rim, rim), :] = south_ref[...]
    kv[pl.ds(0, cells), :] = kvo_ref[...]
    bias[...] = base_ref[...].astype(F32) + inside_ref[0:1, :]
    copies[0].wait()

    def pairs(j):
        part = dot(x[...], w[:, pl.ds(j, TILE)]).astype(BF)
        kvr_ref[:, pl.ds(j, TILE)] = part
        kv[pl.ds(cells, cells), pl.ds(j, TILE)] = part

    tiles_of(2 * model, pairs)

    @pl.loop(0, model // (PAIR * GROUP))
    def _(g):
        heads = []
        for k in range(GROUP):
            h = g * GROUP + k
            keys = pl.ds(pl.multiple_of(h * PAIR, PAIR), PAIR)
            vals = pl.ds(pl.multiple_of(model + h * PAIR, PAIR), PAIR)
            heads.append((h, keys, vals))
            scores[k] = dot(stacked(q_ref[:, keys]), kv[:, keys], NT)
        for k, (h, keys, vals) in enumerate(heads):
            for start in range(0, 2 * cells, SOFT):
                rows = pl.ds(start, SOFT)
                v = scores[k, rows, :] + bias[pl.ds(start % cells, SOFT), :]
                peak = jnp.max(v, -1, keepdims=True)
                v = jnp.exp(v - peak)
                wts[h, rows, :] = v.astype(BF)
                peak_ref[h, rows, :] = jnp.broadcast_to(peak, (SOFT, PAIR))
                sum_ref[h, rows, :] = jnp.broadcast_to(
                    jnp.sum(v, -1, keepdims=True), (SOFT, PAIR)
                )
        for k, (h, keys, vals) in enumerate(heads):
            mix_ref[:, keys] = merged(dot(wts[h], kv[:, vals]))

    for copy in fetch([wts], [wts_hbm], out_sems):
        copy.wait()


def near_back_loop(q_ref, kv, kv_rows, wts, cols, mix, dmix, dkv, scores, ds, put):
    cells, model = q_ref.shape

    @pl.loop(0, model // (PAIR * GROUP))
    def _(g):
        heads, deltas = [], []
        for k in range(GROUP):
            h = g * GROUP + k
            keys = pl.ds(pl.multiple_of(h * PAIR, PAIR), PAIR)
            vals = pl.ds(pl.multiple_of(model + h * PAIR, PAIR), PAIR)
            heads.append((h, keys, vals))
            grad = dmix[:, keys]
            scores[k, :, pl.ds(0, cols.size)] = dot(stacked(grad), kv[kv_rows, vals], NT)
            deltas.append(lane_sums(grad.astype(F32) * mix[:, keys].astype(F32)))
        for k, (h, keys, vals) in enumerate(heads):
            for s in range(2):
                for i in range(0, cells, SOFT):
                    rows = pl.ds(s * cells + i, SOFT)
                    ds[k, rows, :] = (
                        wts[h, rows, cols].astype(F32)
                        * (scores[k, rows, pl.ds(0, cols.size)] - deltas[k][s][i : i + SOFT])
                    ).astype(BF)
        for k, (h, keys, vals) in enumerate(heads):
            put(keys, merged(dot(ds[k], kv[kv_rows, keys])))
            dkv[:, keys] = dot(stacked(q_ref[:, keys]), ds[k], TN).T.astype(BF)
            dkv[:, vals] = dot(stacked(dmix[:, keys]), wts[h, :, cols], TN).T.astype(BF)


def near_kernel(
    q_ref, west_ref, east_ref, base_ref, inside_ref, state_ref, cot_ref, dh_ref, gain_ref,
    mix_in_ref, peak_ref, sum_ref, wn_hbm, wo_hbm, wu_hbm,
    after_ref, hid_ref, dwest_ref, deast_ref, dq_ref, mix, dscaled_ref, dafter_ref,
    wkv, wo, wu, kv, dkv, x, wts, scores, ds, bias, share, nrm, du, acc, dab, dmix, sems,
):
    cells, model = state_ref.shape
    keys_all = kv.shape[0]
    side = west_ref.shape[0]
    ends = 2 * side
    copies = fetch([wn_hbm.at[:, pl.ds(model, 2 * model)]], [wkv], sems.at[pl.ds(0, 1)])
    x[pl.ds(0, side), :] = west_ref[...]
    x[pl.ds(side, side), :] = east_ref[...]
    kv[pl.ds(ends, keys_all - ends), :] = jnp.zeros((keys_all - ends, 2 * model), BF)
    bias[...] = base_ref[...].astype(F32) + inside_ref[0:1, :]
    copies[0].wait()
    copies += fetch([wo_hbm, wu_hbm], [wo, wu], sems.at[pl.ds(1, 2)])

    def project(j):
        kv[pl.ds(0, ends), pl.ds(j, TILE)] = dot(x[...], wkv[:, pl.ds(j, TILE)]).astype(BF)

    tiles_of(2 * model, project)

    def widened(values):
        return jnp.concatenate([values] * (keys_all // PAIR), axis=1)

    @pl.loop(0, model // (PAIR * GROUP))
    def _(g):
        heads = []
        for k in range(GROUP):
            h = g * GROUP + k
            keys = pl.ds(pl.multiple_of(h * PAIR, PAIR), PAIR)
            vals = pl.ds(pl.multiple_of(model + h * PAIR, PAIR), PAIR)
            heads.append((h, keys, vals))
            scores[k] = dot(stacked(q_ref[:, keys]), kv[:, keys], NT)
        for k, (h, keys, vals) in enumerate(heads):
            for i in range(0, cells, SOFT):
                here = pl.ds(i, SOFT)
                shares = []
                for s in range(2):
                    rows = pl.ds(s * cells + i, SOFT)
                    before = peak_ref[h, rows, :]
                    v = scores[k, rows, :] + bias[here, :]
                    peak = jnp.maximum(jnp.max(v, -1, keepdims=True), before)
                    v = jnp.exp(v - widened(peak))
                    part = jnp.exp(before - peak)
                    total = jnp.sum(v, -1, keepdims=True) + part * sum_ref[h, rows, :]
                    inverse = 1.0 / total
                    wts[h, rows, :] = (v * widened(inverse)).astype(BF)
                    shares.append(part * inverse)
                share[here, keys] = spread(*shares)
        for k, (h, keys, vals) in enumerate(heads):
            rims = merged(dot(wts[h], kv[:, vals]))
            mix[:, keys] = (rims + mix_in_ref[:, keys] * share[:, keys]).astype(BF)

    copies[1].wait()

    def project_out(j):
        after_ref[:, pl.ds(j, TILE)] = state_ref[:, pl.ds(j, TILE)] + dot(
            mix[...], wo[:, pl.ds(j, TILE)]
        )

    tiles_of(model, project_out)
    for rows in row_chunks(cells):
        normed, _ = unit(after_ref[rows, :])
        nrm[rows, :] = (normed * gain_ref[2:3, :]).astype(BF)
    copies[2].wait()

    def feed(j):
        cols = pl.ds(j, FEED_TILE)
        u = dot(nrm[...], wu[:, cols])
        square = u * u
        t = jnp.tanh(GELU_C * (u + GELU_A * (square * u)))
        half = 0.5 * (1.0 + t)
        hid_ref[:, cols] = (u * half).astype(BF)
        slope = half + (0.5 * GELU_C) * u * (1.0 - t * t) * (1.0 + 3.0 * GELU_A * square)
        du[:, cols] = (dh_ref[:, cols].astype(F32) * slope).astype(BF)

    tiles_of(du.shape[1], feed, FEED_TILE)

    def feed_back(j):
        acc[:, pl.ds(j, TILE)] = dot(du[...], wu[pl.ds(j, TILE), :], NT)

    tiles_of(model, feed_back)
    for rows in row_chunks(cells):
        grad = acc[rows, :].astype(BF).astype(F32)
        total = cot_ref[rows, :].astype(F32) + norm_pull(
            after_ref[rows, :], gain_ref[2:3, :], grad
        )
        dafter_ref[rows, :] = total
        dab[rows, :] = total.astype(BF)

    def mix_back(j):
        cols = pl.ds(j, TILE)
        grad = dot(dab[...], wo[cols, :], NT)
        dmix[:, cols] = grad.astype(BF)
        dscaled_ref[:, cols] = (grad * share[:, cols]).astype(BF)

    tiles_of(model, mix_back)
    outer = pl.ds(0, keys_all)

    def put(keys, dq):
        dq_ref[:, keys] = dq

    near_back_loop(q_ref, kv, outer, wts, outer, mix, dmix, dkv, scores, ds, put)

    def rim_back(j):
        both = dot(dkv[pl.ds(0, 2 * side), :], wkv[pl.ds(j, TILE), :], NT).astype(BF)
        dwest_ref[:, pl.ds(j, TILE)] = both[:side]
        deast_ref[:, pl.ds(j, TILE)] = both[side:]

    tiles_of(model, rim_back)


def middle_back_kernel(
    q_ref, kvo_ref, kvr_ref, mix, dmix, dq_in_ref, wts_hbm, wn_hbm,
    dq_ref, down_ref, dn_ref, wkv, kv, dkv, wts, scores, ds, sems,
):
    cells, model = q_ref.shape
    part = cells - PAIR
    copies = fetch(
        [wts_hbm.at[:, :, pl.ds(PAIR, kv.shape[0])], wn_hbm.at[:, pl.ds(model, 2 * model)]],
        [wts, wkv],
        sems,
    )
    kv[pl.ds(0, part), :] = kvo_ref[pl.ds(PAIR, part), :]
    kv[pl.ds(part, cells), :] = kvr_ref[...]
    copies[0].wait()

    def put(keys, dq):
        dq_ref[:, keys] = dq + dq_in_ref[:, keys]

    whole = pl.ds(0, kv.shape[0])
    near_back_loop(q_ref, kv, whole, wts, whole, mix, dmix, dkv, scores, ds, put)
    down_ref[...] = dkv[pl.ds(0, part), :]
    copies[1].wait()

    def back(j):
        dn_ref[:, pl.ds(j, TILE)] = dot(
            dkv[pl.ds(part, cells), :], wkv[pl.ds(j, TILE), :], NT
        )

    tiles_of(model, back)


def encode_kernel(after_ref, hid_ref, wd_hbm, _, enc_ref, wd, sems):
    copies = fetch([wd_hbm], [wd], sems)
    copies[0].wait()

    def down(j):
        enc_ref[:, pl.ds(j, TILE)] = (
            after_ref[:, pl.ds(j, TILE)] + dot(hid_ref[...], wd[:, pl.ds(j, TILE)])
        ).astype(BF)

    tiles_of(after_ref.shape[1], down)


def fold_kernel(dn_ref, from_east_ref, from_west_ref, sel_ref, north_ref, south_ref, x):
    rim, model = north_ref.shape
    side = from_east_ref.shape[0]
    x[pl.ds(0, side), :] = from_west_ref[...]
    x[pl.ds(side, side), :] = from_east_ref[...]

    def fold(j):
        cols = pl.ds(j, TILE)
        total = (dn_ref[:, cols] + dot(sel_ref[...], x[:, cols], TN)).astype(BF)
        north_ref[:, cols] = total[:rim]
        south_ref[:, cols] = total[rim:]

    tiles_of(model, fold)


def own_back_kernel(
    q_ref, kvo_ref, mix, dmix, dq_in_ref, down_ref, from_east_ref, from_west_ref, sel_ref,
    wts_hbm, w_hbm, _, dn_ref, dqkv, dkv, wts, scores, ds, x, w, sems,
):
    copies = fetch([wts_hbm.at[:, :, pl.ds(0, PAIR)], w_hbm], [wts, w], sems)
    cells, model = q_ref.shape
    side = from_east_ref.shape[0]
    x[pl.ds(0, side), :] = from_west_ref[...]
    x[pl.ds(side, side), :] = from_east_ref[...]
    copies[0].wait()

    def put(keys, dq):
        dqkv[:, keys] = ((dq + dq_in_ref[:, keys]) * HALF ** (-0.5)).astype(BF)

    whole = pl.ds(0, PAIR)
    near_back_loop(q_ref, kvo_ref, whole, wts, whole, mix, dmix, dkv, scores, ds, put)
    dqkv[pl.ds(0, PAIR), pl.ds(model, 2 * model)] = dkv[...]
    dqkv[pl.ds(PAIR, cells - PAIR), pl.ds(model, 2 * model)] = down_ref[...]
    copies[1].wait()

    def back(j):
        cols = pl.ds(j, TILE)
        dn_ref[:, cols] = dot(dqkv[...], w[cols, :], NT) + dot(
            sel_ref[...], x[:, cols], TN
        )

    tiles_of(model, back)


def cross_back_kernel(
    dn_ref, north_ref, south_ref, state_ref, dafter_ref, gain_ref, q_ref, own_ref, pairs_ref,
    wts_ref, mix_ref, ow_ref, wp_hbm, wo_hbm,
    dstate_hbm, slot_hbm, dq_hbm, down_hbm,
    wp, wo, dsb, dmix, dpairs, scores, ds, dstate_ref, dq_ref, down_ref, slot_ref, sems, out_sems,
):
    copies = fetch([wo_hbm, wp_hbm], [wo, wp], sems)
    cells, model = state_ref.shape
    rim = north_ref.shape[0]
    for i in range(0, cells, CHUNK):
        rows = pl.ds(i, CHUNK)
        other = north_ref[rows, :] if i < rim else south_ref[pl.ds(i - rim, CHUNK), :]
        grad = (dn_ref[rows, :] + other.astype(F32)).astype(BF).astype(F32)
        total = dafter_ref[rows, :] + norm_pull(state_ref[rows, :], gain_ref[1:2, :], grad)
        dstate_ref[rows, :] = total
        dsb[rows, :] = total.astype(BF)
    copies[0].wait()

    def mix_back(j):
        dmix[:, pl.ds(j, TILE)] = dot(dsb[...], wo[pl.ds(j, TILE), :], NT).astype(BF)

    tiles_of(model, mix_back)

    @pl.loop(0, model // (PAIR * GROUP))
    def _(g):
        heads, deltas, own_dots = [], [], []
        for k in range(GROUP):
            h = g * GROUP + k
            keys = pl.ds(pl.multiple_of(h * PAIR, PAIR), PAIR)
            vals = pl.ds(pl.multiple_of(model + h * PAIR, PAIR), PAIR)
            heads.append((h, keys, vals))
            grad = dmix[:, keys]
            grad_f = grad.astype(F32)
            scores[k] = dot(stacked(grad), pairs_ref[:, vals], NT)
            deltas.append(lane_sums(grad_f * mix_ref[:, keys].astype(F32)))
            own_dots.append(lane_sums(grad_f * own_ref[:, vals].astype(F32)))
        for k, (h, keys, vals) in enumerate(heads):
            for s in range(2):
                for i in range(0, cells, SOFT):
                    rows = pl.ds(s * cells + i, SOFT)
                    ds[k, rows, :] = (
                        wts_ref[h, rows, :].astype(F32)
                        * (scores[k, rows, :] - deltas[k][s][i : i + SOFT])
                    ).astype(BF)
        for k, (h, keys, vals) in enumerate(heads):
            lanes = iota((cells, PAIR), 1) < HALF
            weight = ow_ref[:, keys].astype(F32)
            own_grad = weight * jnp.where(
                lanes, own_dots[k][0] - deltas[k][0], own_dots[k][1] - deltas[k][1]
            )
            q = q_ref[:, keys]
            grad = dmix[:, keys]
            dq = merged(dot(ds[k], pairs_ref[:, keys]))
            dq = dq + own_grad * own_ref[:, keys].astype(F32)
            dq_ref[:, keys] = (dq * HALF ** (-0.5)).astype(BF)
            down_ref[:, keys] = (own_grad * q.astype(F32)).astype(BF)
            down_ref[:, vals] = (weight * grad.astype(F32)).astype(BF)
            dpairs[:, keys] = dot(stacked(q), ds[k], TN).T.astype(BF)
            dpairs[:, vals] = dot(stacked(grad), wts_ref[h], TN).T.astype(BF)

    leaving = fetch(
        [dstate_ref, dq_ref, down_ref], [dstate_hbm, dq_hbm, down_hbm],
        out_sems.at[pl.ds(0, 3)],
    )
    copies[1].wait()
    half = model // 2
    for i in range(2):
        cols = pl.ds(i * half, half)
        grads = dot(dpairs[...], wp[cols, :], NT).astype(BF)
        slot_ref[:, :, cols] = grads.reshape(slot_ref.shape[:2] + (half,))
        leaving += fetch(
            [slot_ref.at[:, :, cols]], [slot_hbm.at[:, :, cols]], out_sems.at[pl.ds(3 + i, 1)]
        )
    for copy in leaving:
        copy.wait()


def gather_kernel(place_hbm, ret_ref, out_ref, place_ref, ret, sems):
    copies = fetch([place_hbm], [place_ref], sems)
    ret[...] = ret_ref[...].reshape(ret.shape)
    copies[0].wait()
    out_ref[...] = dot(place_ref[...], ret[...], TN).astype(BF)


def grid_back_kernel(
    grid_ref, dstate_ref, gain_ref, dq_ref, down_ref, wq_hbm, wp_hbm, out_ref, wq, wp, acc, sems
):
    copies = fetch([wq_hbm, wp_hbm], [wq, wp], sems)
    cells, model = grid_ref.shape
    for copy in copies:
        copy.wait()

    def back(j):
        acc[:, pl.ds(j, TILE)] = dot(dq_ref[...], wq[pl.ds(j, TILE), :], NT) + dot(
            down_ref[...], wp[pl.ds(j, TILE), :], NT
        )

    tiles_of(model, back)
    for rows in row_chunks(cells):
        grad = acc[rows, :].astype(BF).astype(F32)
        out_ref[rows, :] = (
            dstate_ref[rows, :]
            + norm_pull(grid_ref[rows, :].astype(F32), gain_ref[0:1, :], grad)
        ).astype(BF)


def ring(value, by):
    size = lax.axis_size("lon")
    return lax.ppermute(value, "lon", [(i, (i + by) % size) for i in range(size)])


def line(value, by):
    size = lax.axis_size("lat")
    pairs = [(i, i + by) for i in range(size) if 0 <= i + by < size]
    return lax.ppermute(value, "lat", pairs)


def key_places(rows_lat, rows_lon):
    places = [(r, c) for r in range(rows_lat) for c in range(rows_lon)]
    places += [(r, c) for r in range(-RADIUS, 0) for c in range(rows_lon)]
    places += [(rows_lat + r, c) for r in range(RADIUS) for c in range(rows_lon)]
    ext = list(places)
    tall = range(-RADIUS, rows_lat + RADIUS)
    places += [(r, c) for r in tall for c in range(-RADIUS, 0)]
    places += [(r, rows_lon + c) for r in tall for c in range(RADIUS)]
    return np.array(places), ext


def per_device(
    grid_state, observations, obs_tile, obs_cell, cotangent, norm_gains,
    w_cross_query, w_cross_pairs, w_cross_out, w_near_proj, w_near_out, w_up, w_down,
):
    rows_lat, rows_lon, model = grid_state.shape
    lat_count = lax.axis_size("lat")
    devices = lat_count * lax.axis_size("lon")
    rows_obs = observations.shape[0]
    cap = max(2, 2 * rows_obs // devices)
    slots = devices * cap
    cells = rows_lat * rows_lon
    ff = w_up.shape[1]
    pairs_n = model // PAIR
    rim = RADIUS * rows_lon
    side = RADIUS * (rows_lat + 2 * RADIUS)
    places, ext_places = key_places(rows_lat, rows_lon)
    keys_n = len(places)
    keys_all = -(-keys_n // 256) * 256
    spot = {place: i for i, place in enumerate(ext_places)}
    tall = range(-RADIUS, rows_lat + RADIUS)
    select = np.zeros((2 * side, len(ext_places)), np.float32)
    for i, r in enumerate(tall):
        for c in range(RADIUS):
            select[i * RADIUS + c, spot[(r, c)]] = 1.0
            select[side + i * RADIUS + c, spot[(r, rows_lon - RADIUS + c)]] = 1.0
    select = select.astype(jnp.bfloat16)
    base = np.full((cells, keys_all), LOW_SCORE, np.float32)
    own_rows, own_cols = places[:cells, 0], places[:cells, 1]
    allowed = (np.abs(places[None, :, 0] - own_rows[:, None]) <= RADIUS) & (
        np.abs(places[None, :, 1] - own_cols[:, None]) <= RADIUS
    )
    base[:, :keys_n][allowed] = 0.0
    base = base.astype(jnp.bfloat16)
    key_rows = np.zeros((8, keys_all), np.int32)
    key_rows[:, :keys_n] = places[None, :, 0]
    key_lat = jnp.asarray(key_rows) + lax.axis_index("lat") * rows_lat
    inside = jnp.where((key_lat >= 0) & (key_lat < rows_lat * lat_count), 0.0, LOW_SCORE)
    inside = inside.astype(F32)

    dma = pltpu.SemaphoreType.DMA
    vm = pltpu.VMEM
    flat = grid_state.reshape(cells, model)
    cot = cotangent.reshape(cells, model)

    payload, placing = call(
        functools.partial(place_kernel, devices=devices, cap=cap, wide=rows_lon),
        (obs_tile.reshape(1, rows_obs), obs_cell.reshape(1, rows_obs), observations), "hhh",
        [((devices, cap, model + 128), BF, "h"), ((slots, rows_obs), BF, "h")],
        [vm((1, rows_obs), jnp.int32), vm((1, rows_obs), jnp.int32), vm((rows_obs, model), BF),
         vm((devices, cap, model + 128), BF), vm((slots, rows_obs), BF), dma((3,))],
        2 * rows_obs * slots * model, "place",
    )
    arrived = lax.all_to_all(payload, ("lat", "lon"), 0, 0, tiled=True)
    q_c, own_pairs, dhid = call(
        grid_kernel,
        (flat, cot, norm_gains, w_cross_query, w_cross_pairs, w_down), "hhvhhh",
        [((cells, model), BF, "h"), ((cells, 2 * model), BF, "h"), ((cells, ff), BF, "h")],
        [vm((cells, model), BF), vm((cells, model), BF), vm((cells, model), BF),
         vm((cells, 2 * model), BF), vm((cells, ff), BF),
         vm((cells, model), BF), vm((model, model), BF), vm((model, 2 * model), BF),
         vm((ff, model), BF), dma((5,)), dma((3,))],
        2 * cells * model * (3 * model + ff), "grid_proj",
    )
    state, top, bottom, slot_pairs, cross_w, cross_mix, own_w = call(
        functools.partial(cross_kernel, wide=rows_lon),
        (arrived, flat, q_c, own_pairs, norm_gains, w_cross_pairs, w_cross_out), "vhhhvhh",
        [((cells, model), F32, "h"), ((rim, model), BF), ((rim, model), BF),
         ((slots, 2 * model), BF, "h"), ((pairs_n, 2 * cells, slots), BF, "h"),
         ((cells, model), BF, "h"), ((cells, model), BF, "h")],
        [vm((slots, model + 128), BF), vm((model, 2 * model), BF), vm((model, model), BF),
         vm((GROUP, 2 * cells, slots), F32), vm((cells, slots), F32), vm((cells, model), BF),
         vm((cells, model), BF), vm((cells, 2 * model), BF), vm((cells, model), F32),
         vm((slots, 2 * model), BF), vm((pairs_n, 2 * cells, slots), BF), vm((cells, model), BF),
         vm((cells, model), BF), dma((2 * model // TILE,)), dma((9,))],
        2 * slots * model * 2 * model * 2, "cross",
    )
    south = line(top, -1)
    north = line(bottom, 1)
    q_n, kv_own = call(
        near_own_kernel, (top, bottom, w_near_proj), "vva",
        [((cells, model), BF), ((cells, 2 * model), BF)],
        [vm((cells, model), BF), vm((model, 3 * model), BF), dma((2,))],
        2 * cells * model * 3 * model, "near_own",
    )
    west_send, east_send = call(
        rim_kernel, (top, bottom, north, south, jnp.asarray(select), kv_own), "vvvvva",
        [((side, model), BF), ((side, model), BF)],
        [vm((cells + 2 * rim, model), BF)],
        2 * 2 * side * 2 * cells * model, "rim",
    )
    east = ring(west_send, -1)
    west = ring(east_send, 1)
    kv_rows, near_w, inner_mix, inner_peak, inner_sum = call(
        inner_kernel,
        (north, south, q_n, kv_own, jnp.asarray(base[:, : 2 * cells]), inside[:, : 2 * cells],
         w_near_proj), "vvvvvva",
        [((2 * rim, 2 * model), BF), ((pairs_n, 2 * cells, 2 * cells), BF, "h"),
         ((cells, model), F32), ((pairs_n, 2 * cells, PAIR), F32),
         ((pairs_n, 2 * cells, PAIR), F32)],
        [vm((2 * rim, model), BF), vm((model, 2 * model), BF), vm((2 * cells, 2 * model), BF),
         vm((cells, 2 * cells), F32), vm((GROUP, 2 * cells, 2 * cells), F32),
         vm((pairs_n, 2 * cells, 2 * cells), BF), dma((1,)), dma((1,))],
        4 * rim * model * 2 * model * 2, "inner",
    )
    outer = keys_all - 2 * cells
    after, hidden, dwest, deast, dq_rim, near_mix, dmix, dafter = call(
        near_kernel,
        (q_n, west, east, jnp.asarray(base[:, 2 * cells :]), inside[:, 2 * cells :], state, cot,
         dhid, norm_gains, inner_mix, inner_peak, inner_sum, w_near_proj, w_near_out, w_up),
        "vvvvvvvvvvvvaaa",
        [((cells, model), F32), ((cells, ff), BF), ((side, model), BF), ((side, model), BF),
         ((cells, model), F32), ((cells, model), BF), ((cells, model), BF),
         ((cells, model), F32)],
        [vm((model, 2 * model), BF), vm((model, model), BF), vm((model, ff), BF),
         vm((outer, 2 * model), BF), vm((outer, 2 * model), BF), vm((2 * side, model), BF),
         vm((pairs_n, 2 * cells, outer), BF), vm((GROUP, 2 * cells, outer), F32),
         vm((GROUP, 2 * cells, outer), BF), vm((cells, outer), F32), vm((cells, model), F32),
         vm((cells, model), BF), vm((cells, ff), BF), vm((cells, model), F32),
         vm((cells, model), BF), vm((cells, model), BF), dma((3,))],
        2e10, "near",
    )
    from_east = ring(dwest, -1)
    from_west = ring(deast, 1)
    middle = 2 * cells - PAIR
    dq_most, down_part, dn_rows = call(
        middle_back_kernel,
        (q_n, kv_own, kv_rows, near_mix, dmix, dq_rim, near_w, w_near_proj), "vvvvvvha",
        [((cells, model), F32), ((cells - PAIR, 2 * model), BF), ((2 * rim, model), F32)],
        [vm((model, 2 * model), BF), vm((middle, 2 * model), BF), vm((middle, 2 * model), BF),
         vm((pairs_n, 2 * cells, middle), BF), vm((GROUP, 2 * cells, middle), F32),
         vm((GROUP, 2 * cells, middle), BF), dma((2,))],
        4 * cells * model * 2 * model, "middle_back",
    )
    dnorth, dsouth = call(
        fold_kernel, (dn_rows, from_east, from_west, jnp.asarray(select[:, cells:])), "vvvv",
        [((rim, model), BF), ((rim, model), BF)],
        [vm((2 * side, model), BF)],
        2 * 2 * side * 2 * rim * model, "fold",
    )
    from_south = line(dnorth, -1)
    from_north = line(dsouth, 1)
    dn_own = call(
        own_back_kernel,
        (q_n, kv_own, near_mix, dmix, dq_most, down_part, from_east, from_west,
         jnp.asarray(select[:, :cells]), near_w, w_near_proj, dnorth), "vvvvvvvvvhaa",
        [((cells, model), F32)],
        [vm((cells, 3 * model), BF), vm((PAIR, 2 * model), BF),
         vm((pairs_n, 2 * cells, PAIR), BF), vm((GROUP, 2 * cells, PAIR), F32),
         vm((GROUP, 2 * cells, PAIR), BF), vm((2 * side, model), BF),
         vm((model, 3 * model), BF), dma((2,))],
        2 * cells * model * 4 * model, "own_back",
    )
    dstate, slot_grads, dq, down = call(
        cross_back_kernel,
        (dn_own, from_north, from_south, state, dafter, norm_gains, q_c, own_pairs, slot_pairs,
         cross_w, cross_mix, own_w, w_cross_pairs, w_cross_out), "vvvvvvvvvvvvaa",
        [((cells, model), F32, "h"), ((devices, cap, model), BF, "h"),
         ((cells, model), BF, "h"), ((cells, 2 * model), BF, "h")],
        [vm((model, 2 * model), BF), vm((model, model), BF), vm((cells, model), BF),
         vm((cells, model), BF), vm((slots, 2 * model), BF), vm((GROUP, 2 * cells, slots), F32),
         vm((GROUP, 2 * cells, slots), BF), vm((cells, model), F32), vm((cells, model), BF),
         vm((cells, 2 * model), BF), vm((devices, cap, model), BF), dma((2,)), dma((5,))],
        2 * slots * model * 2 * model * 2, "cross_back",
    )
    returned = lax.all_to_all(slot_grads, ("lat", "lon"), 0, 0, tiled=True)
    encoded = call(
        encode_kernel, (after, hidden, w_down, dq), "vvaa", [((cells, model), BF)],
        [vm((ff, model), BF), dma((1,))], 2 * cells * model * ff, "encode",
    )
    grid_grad = call(
        grid_back_kernel,
        (flat, dstate, norm_gains, dq, down, w_cross_query, w_cross_pairs), "vvvvvaa",
        [((cells, model), BF)],
        [vm((model, model), BF), vm((model, 2 * model), BF), vm((cells, model), F32), dma((2,))],
        2 * cells * model * 3 * model, "grid_back",
    )
    obs_grad = call(
        gather_kernel, (placing, returned), "hv", [((rows_obs, model), BF)],
        [vm((slots, rows_obs), BF), vm((slots, model), BF), dma((1,))], 2 * rows_obs * slots * model, "gather",
    )
    shape = (rows_lat, rows_lon, model)
    return encoded.reshape(shape), grid_grad.reshape(shape), obs_grad


def solution(mesh):
    return jax.shard_map(
        per_device,
        mesh=mesh,
        in_specs=(
            P("lat", "lon", None),
            P(("lat", "lon"), None),
            P(("lat", "lon"), None),
            P(("lat", "lon"), None),
            P("lat", "lon", None),
            P(), P(), P(), P(), P(), P(), P(), P(),
        ),
        out_specs=(P("lat", "lon", None), P("lat", "lon", None), P(("lat", "lon"), None)),
        check_vma=False,
    )
```

```python
import functools

import jax
import jax.numpy as jnp
import numpy as np
from jax import lax
from jax.experimental import pallas as pl
from jax.experimental.pallas import tpu as pltpu
from jax.sharding import PartitionSpec as P

HEADS = 16
RADIUS = 6
EPSILON = 1e-05
SPREAD = 32.0
LOW_SCORE = -1e30

BF = jnp.bfloat16
F32 = jnp.float32
NN = (((1,), (0,)), ((), ()))
NT = (((1,), (1,)), ((), ()))
TN = (((0,), (0,)), ((), ()))
CHUNK = 32
SOFT = 32
TILE = 1024
PAIR = 128
HALF = 64
SLACK_BYTES = 8 * 2**20
FEED_TILE = 1024
GROUP = 2
GELU_C = 0.7978845608028654
GELU_A = 0.044715


def dot(left, right, dims=NN):
    return lax.dot_general(left, right, dims, preferred_element_type=F32)


def iota(shape, dim):
    return lax.broadcasted_iota(jnp.int32, shape, dim)


def tiles_of(count, body, tile=TILE):
    @pl.loop(0, count // tile)
    def _(i):
        body(pl.multiple_of(i * tile, tile))


def row_chunks(count):
    return [pl.ds(i, CHUNK) for i in range(0, count, CHUNK)]


def unit(values):
    center = values - jnp.mean(values, -1, keepdims=True)
    scale = lax.rsqrt(jnp.mean(center * center, -1, keepdims=True) + EPSILON)
    return center * scale, scale


def norm_pull(values, gain, grad):
    normed, scale = unit(values)
    inner = grad * gain
    return scale * (
        inner
        - jnp.mean(inner, -1, keepdims=True)
        - normed * jnp.mean(inner * normed, -1, keepdims=True)
    )


def head_masks():
    left = (iota((1, PAIR), 1) < HALF).astype(F32)
    return left.astype(BF), (1.0 - left).astype(BF)


def stacked(values):
    left, right = head_masks()
    return jnp.concatenate([values * left, values * right], axis=0)


def merged(values):
    count = values.shape[0] // 2
    lanes = iota((count, PAIR), 1) < HALF
    return jnp.where(lanes, values[:count], values[count:])


def lane_sums(values):
    lanes = iota(values.shape, 1) < HALF
    first = jnp.sum(jnp.where(lanes, values, 0.0), -1, keepdims=True)
    second = jnp.sum(jnp.where(lanes, 0.0, values), -1, keepdims=True)
    return first, second


def fetch(sources, targets, sems):
    copies = [
        pltpu.make_async_copy(source, target, sems.at[i])
        for i, (source, target) in enumerate(zip(sources, targets))
    ]
    for copy in copies:
        copy.start()
    return copies


def call(body, ins, kinds, outs, scratch, flops, name):
    any_spec = pl.BlockSpec(memory_space=pl.ANY)
    vmem_spec = pl.BlockSpec(memory_space=pltpu.VMEM)
    moved = sum(x.size * x.dtype.itemsize for x in ins)
    moved += sum(int(np.prod(o[0])) * jnp.dtype(o[1]).itemsize for o in outs)
    held = sum(x.size * x.dtype.itemsize for x, k in zip(ins, kinds) if k == "v")
    held += sum(int(np.prod(o[0])) * jnp.dtype(o[1]).itemsize for o in outs if len(o) == 2)
    for item in scratch:
        if jnp.issubdtype(item.dtype, jnp.floating):
            held += int(np.prod(item.shape)) * jnp.dtype(item.dtype).itemsize
    single = len(outs) == 1
    shapes = [
        jax.ShapeDtypeStruct(*o) if len(o) == 2 else pltpu.HBM(o[0], o[1]) for o in outs
    ]
    specs = [vmem_spec if len(o) == 2 else any_spec for o in outs]
    ins = [
        pltpu.with_memory_space_constraint(x, pltpu.HBM) if k == "h" else x
        for x, k in zip(ins, kinds)
    ]
    return pl.pallas_call(
        body,
        name=name,
        out_shape=shapes[0] if single else shapes,
        in_specs=[vmem_spec if k == "v" else any_spec for k in kinds],
        out_specs=specs[0] if single else specs,
        scratch_shapes=scratch,
        compiler_params=pltpu.CompilerParams(vmem_limit_bytes=held + SLACK_BYTES),
        cost_estimate=pl.CostEstimate(
            flops=int(flops), bytes_accessed=int(moved), transcendentals=0
        ),
    )(*ins)


def place_kernel(
    tile_hbm, cell_hbm, obs_hbm, pay_hbm, place_hbm,
    tile_ref, cell_ref, obs_ref, pay_ref, place_ref, sems, *, devices, cap, wide,
):
    copies = fetch([tile_hbm, cell_hbm, obs_hbm], [tile_ref, cell_ref, obs_ref], sems)
    copies[0].wait()
    rows, model = obs_ref.shape
    slots = devices * cap
    tile = tile_ref[...]
    member = tile == iota((devices, rows), 0)
    earlier = (iota((rows, rows), 0) < iota((rows, rows), 1)).astype(F32).astype(BF)
    before = dot(member.astype(F32).astype(BF), earlier)
    rank = jnp.sum(jnp.where(member, before, 0.0), 0, keepdims=True).astype(jnp.int32)
    slot = tile * cap + rank
    placing = (slot == iota((slots, rows), 0)).astype(F32).astype(BF)
    place_ref[...] = placing
    copies[1].wait()
    copies[2].wait()
    cell = cell_ref[...]
    shift = wide.bit_length() - 1
    line_no = iota((128, rows), 0)
    codes = jnp.where(
        line_no == 0, (cell >> shift) + 1, jnp.where(line_no == 1, (cell & (wide - 1)) + 1, 0)
    )
    code_rows = dot(placing, codes.astype(F32).astype(BF), NT).astype(BF)
    pay_ref[:, :, model:] = code_rows.reshape(devices, cap, 128)
    moved = dot(placing, obs_ref[...]).astype(BF)
    pay_ref[:, :, :model] = moved.reshape(devices, cap, model)
    for copy in fetch([pay_ref, place_ref], [pay_hbm, place_hbm], sems):
        copy.wait()


def grid_kernel(
    grid_hbm, cot_hbm, gain_ref, wq_hbm, wp_hbm, wd_hbm, q_hbm, own_hbm, dh_hbm,
    grid_ref, cot_ref, q_ref, own_ref, dh_ref, nrm, wq, wp, wd, sems, out_sems,
):
    first, *copies = fetch(
        [grid_hbm, wq_hbm, wp_hbm, wd_hbm, cot_hbm], [grid_ref, wq, wp, wd, cot_ref], sems
    )
    cells, model = grid_ref.shape
    first.wait()
    for rows in row_chunks(cells):
        normed, _ = unit(grid_ref[rows, :].astype(F32))
        nrm[rows, :] = (normed * gain_ref[0:1, :]).astype(BF)
    copies[0].wait()

    def query(j):
        q_ref[:, pl.ds(j, TILE)] = (
            dot(nrm[...], wq[:, pl.ds(j, TILE)]) * HALF ** (-0.5)
        ).astype(BF)

    tiles_of(model, query)
    copies[1].wait()

    def own(j):
        own_ref[:, pl.ds(j, TILE)] = dot(nrm[...], wp[:, pl.ds(j, TILE)]).astype(BF)

    tiles_of(2 * model, own)
    copies[2].wait()
    copies[3].wait()

    def hidden(j):
        dh_ref[:, pl.ds(j, TILE)] = dot(cot_ref[...], wd[pl.ds(j, TILE), :], NT).astype(BF)

    tiles_of(dh_ref.shape[1], hidden)
    for copy in fetch([q_ref, own_ref, dh_ref], [q_hbm, own_hbm, dh_hbm], out_sems):
        copy.wait()


def cross_kernel(
    arr_ref, grid_hbm, q_hbm, own_hbm, gain_ref, wp_hbm, wo_hbm,
    state_hbm, top_ref, bottom_ref, pairs_hbm, wts_hbm, mix_hbm, ow_hbm,
    arr, wp, wo, scores, bias, grid_ref, q_ref, own_ref, state_ref, pairs_ref, wts_ref,
    mix_ref, ow_ref, sems, out_sems, *, wide,
):
    cells, model = grid_ref.shape
    parts = [pl.ds(j, TILE) for j in range(0, 2 * model, TILE)]
    copies = fetch([wp_hbm.at[:, c] for c in parts], [wp.at[:, c] for c in parts], sems)
    lates = out_sems.at[pl.ds(5, 4)]
    rim = top_ref.shape[0]
    slots = arr.shape[0]
    arr[...] = arr_ref[...].reshape(arr.shape)
    pick = (iota((8, 128), 0) == iota((8, 128), 1)).astype(F32).astype(BF)
    codes = dot(pick, arr[:, model:], NT)
    cell = iota((cells, slots), 0)
    shift = wide.bit_length() - 1
    row_gap = (cell >> shift).astype(F32) - (codes[0:1] - 1.0)
    col_gap = (cell & (wide - 1)).astype(F32) - (codes[1:2] - 1.0)
    near = -(row_gap * row_gap + col_gap * col_gap) * (1.0 / SPREAD)
    bias[...] = jnp.where(codes[0:1] > 0.5, near, LOW_SCORE)
    for i, cols in enumerate(parts):
        copies[i].wait()
        if i == 0:
            late = fetch(
                [q_hbm, own_hbm, wo_hbm, grid_hbm], [q_ref, own_ref, wo, grid_ref], lates
            )
        pairs_ref[:, cols] = dot(arr[:, :model], wp[:, cols]).astype(BF)
    leaving = fetch([pairs_ref], [pairs_hbm], out_sems.at[pl.ds(0, 1)])
    late[0].wait()
    late[1].wait()

    def soften(h, k, own_scores):
        own_weights = []
        for side in range(2):
            parts = []
            for i in range(0, cells, SOFT):
                own_score = own_scores[side][i : i + SOFT]
                x = scores[k, pl.ds(side * cells + i, SOFT), :] + bias[pl.ds(i, SOFT), :]
                peak = jnp.maximum(jnp.max(x, -1, keepdims=True), own_score)
                x = jnp.exp(x - peak)
                own_weight = jnp.exp(own_score - peak)
                inverse = 1.0 / (jnp.sum(x, -1, keepdims=True) + own_weight)
                wts_ref[h, pl.ds(side * cells + i, SOFT), :] = (x * inverse).astype(BF)
                parts.append(own_weight * inverse)
            own_weights.append(jnp.concatenate(parts, axis=0))
        lanes = iota((cells, PAIR), 1) < HALF
        return jnp.where(lanes, own_weights[0], own_weights[1]).astype(BF)

    @pl.loop(0, model // (PAIR * GROUP))
    def _(g):
        heads, own_scores, weights = [], [], []
        for k in range(GROUP):
            h = g * GROUP + k
            keys = pl.ds(pl.multiple_of(h * PAIR, PAIR), PAIR)
            vals = pl.ds(pl.multiple_of(model + h * PAIR, PAIR), PAIR)
            heads.append((h, keys, vals))
            q = q_ref[:, keys]
            scores[k] = dot(stacked(q), pairs_ref[:, keys], NT)
            own_scores.append(lane_sums(q.astype(F32) * own_ref[:, keys].astype(F32)))
        for k, (h, keys, vals) in enumerate(heads):
            weights.append(soften(h, k, own_scores[k]))
            ow_ref[:, keys] = weights[k]
        for k, (h, keys, vals) in enumerate(heads):
            mix = merged(dot(wts_ref[h], pairs_ref[:, vals]))
            mix_ref[:, keys] = (
                mix + weights[k].astype(F32) * own_ref[:, vals].astype(F32)
            ).astype(BF)

    leaving += fetch(
        [wts_ref, mix_ref, ow_ref], [wts_hbm, mix_hbm, ow_hbm], out_sems.at[pl.ds(1, 3)]
    )
    late[2].wait()
    late[3].wait()

    def project_out(j):
        state_ref[:, pl.ds(j, TILE)] = grid_ref[:, pl.ds(j, TILE)].astype(F32) + dot(
            mix_ref[...], wo[:, pl.ds(j, TILE)]
        )

    tiles_of(model, project_out)
    leaving += fetch([state_ref], [state_hbm], out_sems.at[pl.ds(4, 1)])
    for i in range(0, cells, CHUNK):
        normed, _ = unit(state_ref[pl.ds(i, CHUNK), :])
        normed = (normed * gain_ref[1:2, :]).astype(BF)
        if i < rim:
            top_ref[pl.ds(i, CHUNK), :] = normed
        else:
            bottom_ref[pl.ds(i - rim, CHUNK), :] = normed
    for copy in leaving:
        copy.wait()


def near_own_kernel(top_ref, bottom_ref, w_hbm, q_ref, kv_ref, nrm, w, sems):
    cells, model = nrm.shape
    rim = top_ref.shape[0]
    copies = fetch(
        [w_hbm.at[:, pl.ds(0, model)], w_hbm.at[:, pl.ds(model, 2 * model)]],
        [w.at[:, pl.ds(0, model)], w.at[:, pl.ds(model, 2 * model)]],
        sems,
    )
    nrm[pl.ds(0, rim), :] = top_ref[...]
    nrm[pl.ds(rim, rim), :] = bottom_ref[...]
    copies[0].wait()

    def query(j):
        q_ref[:, pl.ds(j, TILE)] = (
            dot(nrm[...], w[:, pl.ds(j, TILE)]) * HALF ** (-0.5)
        ).astype(BF)

    tiles_of(model, query)
    copies[1].wait()

    def pairs(j):
        kv_ref[:, pl.ds(j, TILE)] = dot(
            nrm[...], w[:, pl.ds(pl.multiple_of(model + j, TILE), TILE)]
        ).astype(BF)

    tiles_of(2 * model, pairs)


def rim_kernel(
    top_ref, bottom_ref, north_ref, south_ref, sel_ref, _, west_ref, east_ref, ext
):
    rim, model = north_ref.shape
    for i, part in enumerate((top_ref, bottom_ref, north_ref, south_ref)):
        ext[pl.ds(i * rim, rim), :] = part[...]
    side = west_ref.shape[0]

    def pick(j):
        both = dot(sel_ref[...], ext[:, pl.ds(j, TILE)]).astype(BF)
        west_ref[:, pl.ds(j, TILE)] = both[:side]
        east_ref[:, pl.ds(j, TILE)] = both[side:]

    tiles_of(model, pick)


def spread(first, second):
    lanes = iota((first.shape[0], PAIR), 1) < HALF
    return jnp.where(lanes, first, second)


def inner_kernel(
    north_ref, south_ref, q_ref, kvo_ref, base_ref, inside_ref, w_hbm,
    kvr_ref, wts_hbm, mix_ref, peak_ref, sum_ref,
    x, w, kv, bias, scores, wts, sems, out_sems,
):
    rim, model = north_ref.shape
    cells = q_ref.shape[0]
    copies = fetch([w_hbm.at[:, pl.ds(model, 2 * model)]], [w], sems)
    x[pl.ds(0, rim), :] = north_ref[...]
    x[pl.ds(rim, rim), :] = south_ref[...]
    kv[pl.ds(0, cells), :] = kvo_ref[...]
    bias[...] = base_ref[...].astype(F32) + inside_ref[0:1, :]
    copies[0].wait()

    def pairs(j):
        part = dot(x[...], w[:, pl.ds(j, TILE)]).astype(BF)
        kvr_ref[:, pl.ds(j, TILE)] = part
        kv[pl.ds(cells, cells), pl.ds(j, TILE)] = part

    tiles_of(2 * model, pairs)

    @pl.loop(0, model // (PAIR * GROUP))
    def _(g):
        heads = []
        for k in range(GROUP):
            h = g * GROUP + k
            keys = pl.ds(pl.multiple_of(h * PAIR, PAIR), PAIR)
            vals = pl.ds(pl.multiple_of(model + h * PAIR, PAIR), PAIR)
            heads.append((h, keys, vals))
            scores[k] = dot(stacked(q_ref[:, keys]), kv[:, keys], NT)
        for k, (h, keys, vals) in enumerate(heads):
            for start in range(0, 2 * cells, SOFT):
                rows = pl.ds(start, SOFT)
                v = scores[k, rows, :] + bias[pl.ds(start % cells, SOFT), :]
                peak = jnp.max(v, -1, keepdims=True)
                v = jnp.exp(v - peak)
                wts[h, rows, :] = v.astype(BF)
                peak_ref[h, rows, :] = jnp.broadcast_to(peak, (SOFT, PAIR))
                sum_ref[h, rows, :] = jnp.broadcast_to(
                    jnp.sum(v, -1, keepdims=True), (SOFT, PAIR)
                )
        for k, (h, keys, vals) in enumerate(heads):
            mix_ref[:, keys] = merged(dot(wts[h], kv[:, vals]))

    for copy in fetch([wts], [wts_hbm], out_sems):
        copy.wait()


def near_back_loop(q_ref, kv, kv_rows, wts, cols, mix, dmix, dkv, scores, ds, put):
    cells, model = q_ref.shape

    @pl.loop(0, model // (PAIR * GROUP))
    def _(g):
        heads, deltas = [], []
        for k in range(GROUP):
            h = g * GROUP + k
            keys = pl.ds(pl.multiple_of(h * PAIR, PAIR), PAIR)
            vals = pl.ds(pl.multiple_of(model + h * PAIR, PAIR), PAIR)
            heads.append((h, keys, vals))
            grad = dmix[:, keys]
            scores[k, :, pl.ds(0, cols.size)] = dot(stacked(grad), kv[kv_rows, vals], NT)
            deltas.append(lane_sums(grad.astype(F32) * mix[:, keys].astype(F32)))
        for k, (h, keys, vals) in enumerate(heads):
            for s in range(2):
                for i in range(0, cells, SOFT):
                    rows = pl.ds(s * cells + i, SOFT)
                    ds[k, rows, :] = (
                        wts[h, rows, cols].astype(F32)
                        * (scores[k, rows, pl.ds(0, cols.size)] - deltas[k][s][i : i + SOFT])
                    ).astype(BF)
        for k, (h, keys, vals) in enumerate(heads):
            put(keys, merged(dot(ds[k], kv[kv_rows, keys])))
            dkv[:, keys] = dot(stacked(q_ref[:, keys]), ds[k], TN).T.astype(BF)
            dkv[:, vals] = dot(stacked(dmix[:, keys]), wts[h, :, cols], TN).T.astype(BF)


def near_kernel(
    q_ref, west_ref, east_ref, base_ref, inside_ref, state_ref, cot_ref, dh_ref, gain_ref,
    mix_in_ref, peak_ref, sum_ref, wn_hbm, wo_hbm, wu_hbm,
    after_ref, hid_ref, dwest_ref, deast_ref, dq_ref, mix, dscaled_ref, dafter_ref,
    wkv, wo, wu, kv, dkv, x, wts, scores, ds, bias, share, nrm, du, acc, dab, dmix, sems,
):
    cells, model = state_ref.shape
    keys_all = kv.shape[0]
    side = west_ref.shape[0]
    ends = 2 * side
    copies = fetch([wn_hbm.at[:, pl.ds(model, 2 * model)]], [wkv], sems.at[pl.ds(0, 1)])
    x[pl.ds(0, side), :] = west_ref[...]
    x[pl.ds(side, side), :] = east_ref[...]
    kv[pl.ds(ends, keys_all - ends), :] = jnp.zeros((keys_all - ends, 2 * model), BF)
    bias[...] = base_ref[...].astype(F32) + inside_ref[0:1, :]
    copies[0].wait()
    copies += fetch([wo_hbm, wu_hbm], [wo, wu], sems.at[pl.ds(1, 2)])

    def project(j):
        kv[pl.ds(0, ends), pl.ds(j, TILE)] = dot(x[...], wkv[:, pl.ds(j, TILE)]).astype(BF)

    tiles_of(2 * model, project)

    def widened(values):
        return jnp.concatenate([values] * (keys_all // PAIR), axis=1)

    @pl.loop(0, model // (PAIR * GROUP))
    def _(g):
        heads = []
        for k in range(GROUP):
            h = g * GROUP + k
            keys = pl.ds(pl.multiple_of(h * PAIR, PAIR), PAIR)
            vals = pl.ds(pl.multiple_of(model + h * PAIR, PAIR), PAIR)
            heads.append((h, keys, vals))
            scores[k] = dot(stacked(q_ref[:, keys]), kv[:, keys], NT)
        for k, (h, keys, vals) in enumerate(heads):
            for i in range(0, cells, SOFT):
                here = pl.ds(i, SOFT)
                shares = []
                for s in range(2):
                    rows = pl.ds(s * cells + i, SOFT)
                    before = peak_ref[h, rows, :]
                    v = scores[k, rows, :] + bias[here, :]
                    peak = jnp.maximum(jnp.max(v, -1, keepdims=True), before)
                    v = jnp.exp(v - widened(peak))
                    part = jnp.exp(before - peak)
                    total = jnp.sum(v, -1, keepdims=True) + part * sum_ref[h, rows, :]
                    inverse = 1.0 / total
                    wts[h, rows, :] = (v * widened(inverse)).astype(BF)
                    shares.append(part * inverse)
                share[here, keys] = spread(*shares)
        for k, (h, keys, vals) in enumerate(heads):
            rims = merged(dot(wts[h], kv[:, vals]))
            mix[:, keys] = (rims + mix_in_ref[:, keys] * share[:, keys]).astype(BF)

    copies[1].wait()

    def project_out(j):
        after_ref[:, pl.ds(j, TILE)] = state_ref[:, pl.ds(j, TILE)] + dot(
            mix[...], wo[:, pl.ds(j, TILE)]
        )

    tiles_of(model, project_out)
    for rows in row_chunks(cells):
        normed, _ = unit(after_ref[rows, :])
        nrm[rows, :] = (normed * gain_ref[2:3, :]).astype(BF)
    copies[2].wait()

    def feed(j):
        cols = pl.ds(j, FEED_TILE)
        u = dot(nrm[...], wu[:, cols])
        square = u * u
        t = jnp.tanh(GELU_C * (u + GELU_A * (square * u)))
        half = 0.5 * (1.0 + t)
        hid_ref[:, cols] = (u * half).astype(BF)
        slope = half + (0.5 * GELU_C) * u * (1.0 - t * t) * (1.0 + 3.0 * GELU_A * square)
        du[:, cols] = (dh_ref[:, cols].astype(F32) * slope).astype(BF)

    tiles_of(du.shape[1], feed, FEED_TILE)

    def feed_back(j):
        acc[:, pl.ds(j, TILE)] = dot(du[...], wu[pl.ds(j, TILE), :], NT)

    tiles_of(model, feed_back)
    for rows in row_chunks(cells):
        grad = acc[rows, :].astype(BF).astype(F32)
        total = cot_ref[rows, :].astype(F32) + norm_pull(
            after_ref[rows, :], gain_ref[2:3, :], grad
        )
        dafter_ref[rows, :] = total
        dab[rows, :] = total.astype(BF)

    def mix_back(j):
        cols = pl.ds(j, TILE)
        grad = dot(dab[...], wo[cols, :], NT)
        dmix[:, cols] = grad.astype(BF)
        dscaled_ref[:, cols] = (grad * share[:, cols]).astype(BF)

    tiles_of(model, mix_back)
    outer = pl.ds(0, keys_all)

    def put(keys, dq):
        dq_ref[:, keys] = dq

    near_back_loop(q_ref, kv, outer, wts, outer, mix, dmix, dkv, scores, ds, put)

    def rim_back(j):
        both = dot(dkv[pl.ds(0, 2 * side), :], wkv[pl.ds(j, TILE), :], NT).astype(BF)
        dwest_ref[:, pl.ds(j, TILE)] = both[:side]
        deast_ref[:, pl.ds(j, TILE)] = both[side:]

    tiles_of(model, rim_back)


def middle_back_kernel(
    q_ref, kvo_ref, kvr_ref, mix, dmix, dq_in_ref, wts_hbm, wn_hbm,
    dq_ref, down_ref, dn_ref, wkv, kv, dkv, wts, scores, ds, sems,
):
    cells, model = q_ref.shape
    part = cells - PAIR
    copies = fetch(
        [wts_hbm.at[:, :, pl.ds(PAIR, kv.shape[0])], wn_hbm.at[:, pl.ds(model, 2 * model)]],
        [wts, wkv],
        sems,
    )
    kv[pl.ds(0, part), :] = kvo_ref[pl.ds(PAIR, part), :]
    kv[pl.ds(part, cells), :] = kvr_ref[...]
    copies[0].wait()

    def put(keys, dq):
        dq_ref[:, keys] = dq + dq_in_ref[:, keys]

    whole = pl.ds(0, kv.shape[0])
    near_back_loop(q_ref, kv, whole, wts, whole, mix, dmix, dkv, scores, ds, put)
    down_ref[...] = dkv[pl.ds(0, part), :]
    copies[1].wait()

    def back(j):
        dn_ref[:, pl.ds(j, TILE)] = dot(
            dkv[pl.ds(part, cells), :], wkv[pl.ds(j, TILE), :], NT
        )

    tiles_of(model, back)


def encode_kernel(after_ref, hid_ref, wd_hbm, _, enc_ref, wd, sems):
    copies = fetch([wd_hbm], [wd], sems)
    copies[0].wait()

    def down(j):
        enc_ref[:, pl.ds(j, TILE)] = (
            after_ref[:, pl.ds(j, TILE)] + dot(hid_ref[...], wd[:, pl.ds(j, TILE)])
        ).astype(BF)

    tiles_of(after_ref.shape[1], down)


def fold_kernel(dn_ref, from_east_ref, from_west_ref, sel_ref, north_ref, south_ref, x):
    rim, model = north_ref.shape
    side = from_east_ref.shape[0]
    x[pl.ds(0, side), :] = from_west_ref[...]
    x[pl.ds(side, side), :] = from_east_ref[...]

    def fold(j):
        cols = pl.ds(j, TILE)
        total = (dn_ref[:, cols] + dot(sel_ref[...], x[:, cols], TN)).astype(BF)
        north_ref[:, cols] = total[:rim]
        south_ref[:, cols] = total[rim:]

    tiles_of(model, fold)


def own_back_kernel(
    q_ref, kvo_ref, mix, dmix, dq_in_ref, down_ref, from_east_ref, from_west_ref, sel_ref,
    wts_hbm, w_hbm, _, dn_ref, dqkv, dkv, wts, scores, ds, x, w, sems,
):
    copies = fetch([wts_hbm.at[:, :, pl.ds(0, PAIR)], w_hbm], [wts, w], sems)
    cells, model = q_ref.shape
    side = from_east_ref.shape[0]
    x[pl.ds(0, side), :] = from_west_ref[...]
    x[pl.ds(side, side), :] = from_east_ref[...]
    copies[0].wait()

    def put(keys, dq):
        dqkv[:, keys] = ((dq + dq_in_ref[:, keys]) * HALF ** (-0.5)).astype(BF)

    whole = pl.ds(0, PAIR)
    near_back_loop(q_ref, kvo_ref, whole, wts, whole, mix, dmix, dkv, scores, ds, put)
    dqkv[pl.ds(0, PAIR), pl.ds(model, 2 * model)] = dkv[...]
    dqkv[pl.ds(PAIR, cells - PAIR), pl.ds(model, 2 * model)] = down_ref[...]
    copies[1].wait()

    def back(j):
        cols = pl.ds(j, TILE)
        dn_ref[:, cols] = dot(dqkv[...], w[cols, :], NT) + dot(
            sel_ref[...], x[:, cols], TN
        )

    tiles_of(model, back)


def cross_back_kernel(
    dn_ref, north_ref, south_ref, state_ref, dafter_ref, gain_ref, q_ref, pairs_ref,
    wts_ref, mix_ref, wp_hbm, wo_hbm,
    dstate_hbm, slot_hbm, dmix_hbm, ds_hbm,
    wp, wo, dsb, dmix, dpairs, scores, ds, dstate_ref, slot_ref, sems, out_sems,
):
    copies = fetch([wo_hbm, wp_hbm], [wo, wp], sems)
    cells, model = state_ref.shape
    rim = north_ref.shape[0]
    for i in range(0, cells, CHUNK):
        rows = pl.ds(i, CHUNK)
        other = north_ref[rows, :] if i < rim else south_ref[pl.ds(i - rim, CHUNK), :]
        grad = (dn_ref[rows, :] + other.astype(F32)).astype(BF).astype(F32)
        total = dafter_ref[rows, :] + norm_pull(state_ref[rows, :], gain_ref[1:2, :], grad)
        dstate_ref[rows, :] = total
        dsb[rows, :] = total.astype(BF)
    copies[0].wait()

    def mix_back(j):
        dmix[:, pl.ds(j, TILE)] = dot(dsb[...], wo[pl.ds(j, TILE), :], NT).astype(BF)

    tiles_of(model, mix_back)

    @pl.loop(0, model // (PAIR * GROUP))
    def _(g):
        heads, deltas = [], []
        for k in range(GROUP):
            h = g * GROUP + k
            keys = pl.ds(pl.multiple_of(h * PAIR, PAIR), PAIR)
            vals = pl.ds(pl.multiple_of(model + h * PAIR, PAIR), PAIR)
            heads.append((h, keys, vals))
            grad = dmix[:, keys]
            scores[k] = dot(stacked(grad), pairs_ref[:, vals], NT)
            deltas.append(lane_sums(grad.astype(F32) * mix_ref[:, keys].astype(F32)))
        for k, (h, keys, vals) in enumerate(heads):
            for s in range(2):
                for i in range(0, cells, SOFT):
                    rows = pl.ds(s * cells + i, SOFT)
                    ds[h, rows, :] = (
                        wts_ref[h, rows, :].astype(F32)
                        * (scores[k, rows, :] - deltas[k][s][i : i + SOFT])
                    ).astype(BF)
        for k, (h, keys, vals) in enumerate(heads):
            dpairs[:, keys] = dot(stacked(q_ref[:, keys]), ds[h], TN).T.astype(BF)
            dpairs[:, vals] = dot(stacked(dmix[:, keys]), wts_ref[h], TN).T.astype(BF)

    leaving = fetch(
        [dstate_ref, dmix, ds], [dstate_hbm, dmix_hbm, ds_hbm],
        out_sems.at[pl.ds(0, 3)],
    )
    copies[1].wait()
    half = model // 2
    for i in range(2):
        cols = pl.ds(i * half, half)
        grads = dot(dpairs[...], wp[cols, :], NT).astype(BF)
        slot_ref[:, :, cols] = grads.reshape(slot_ref.shape[:2] + (half,))
        leaving += fetch(
            [slot_ref.at[:, :, cols]], [slot_hbm.at[:, :, cols]], out_sems.at[pl.ds(3 + i, 1)]
        )
    for copy in leaving:
        copy.wait()


def gather_kernel(place_hbm, ret_ref, out_ref, place_ref, ret, sems):
    copies = fetch([place_hbm], [place_ref], sems)
    ret[...] = ret_ref[...].reshape(ret.shape)
    copies[0].wait()
    out_ref[...] = dot(place_ref[...], ret[...], TN).astype(BF)


def grid_back_kernel(
    grid_hbm, dstate_hbm, gain_ref, q_hbm, own_hbm, mix_hbm, ow_hbm, dmix_hbm,
    pairs_hbm, ds_hbm, wq_hbm, wp_hbm, out_ref,
    grid_ref, dstate_ref, q_ref, own_ref, mix_ref, ow_ref, dmix,
    pairs, ds, dq_ref, down_ref, wq, wp, acc, sems,
):
    cells, model = grid_ref.shape
    first = fetch(
        [q_hbm, own_hbm, mix_hbm, ow_hbm, dmix_hbm, pairs_hbm.at[:, pl.ds(0, model)], ds_hbm],
        [q_ref, own_ref, mix_ref, ow_ref, dmix, pairs, ds],
        sems.at[pl.ds(0, 7)],
    )
    copies = fetch(
        [wq_hbm, wp_hbm, grid_hbm, dstate_hbm],
        [wq, wp, grid_ref, dstate_ref],
        sems.at[pl.ds(7, 4)],
    )
    for copy in first:
        copy.wait()

    def one(h):
        keys = pl.ds(pl.multiple_of(h * PAIR, PAIR), PAIR)
        vals = pl.ds(pl.multiple_of(model + h * PAIR, PAIR), PAIR)
        grad = dmix[:, keys].astype(F32)
        weight = ow_ref[:, keys].astype(F32)
        gap = own_ref[:, vals].astype(F32) - mix_ref[:, keys].astype(F32)
        own_grad = weight * spread(*lane_sums(grad * gap))
        dq = merged(dot(ds[h], pairs[:, keys])) + own_grad * own_ref[:, keys].astype(F32)
        dq_ref[:, keys] = (dq * HALF ** (-0.5)).astype(BF)
        down_ref[:, keys] = (own_grad * q_ref[:, keys].astype(F32)).astype(BF)
        down_ref[:, vals] = (weight * grad).astype(BF)

    @pl.loop(0, model // (PAIR * GROUP))
    def _(g):
        for k in range(GROUP):
            one(g * GROUP + k)

    for copy in copies:
        copy.wait()

    def back(j):
        acc[:, pl.ds(j, TILE)] = dot(dq_ref[...], wq[pl.ds(j, TILE), :], NT) + dot(
            down_ref[...], wp[pl.ds(j, TILE), :], NT
        )

    tiles_of(model, back)
    for rows in row_chunks(cells):
        grad = acc[rows, :].astype(BF).astype(F32)
        out_ref[rows, :] = (
            dstate_ref[rows, :]
            + norm_pull(grid_ref[rows, :].astype(F32), gain_ref[0:1, :], grad)
        ).astype(BF)


def ring(value, by):
    size = lax.axis_size("lon")
    return lax.ppermute(value, "lon", [(i, (i + by) % size) for i in range(size)])


def line(value, by):
    size = lax.axis_size("lat")
    pairs = [(i, i + by) for i in range(size) if 0 <= i + by < size]
    return lax.ppermute(value, "lat", pairs)


def key_places(rows_lat, rows_lon):
    places = [(r, c) for r in range(rows_lat) for c in range(rows_lon)]
    places += [(r, c) for r in range(-RADIUS, 0) for c in range(rows_lon)]
    places += [(rows_lat + r, c) for r in range(RADIUS) for c in range(rows_lon)]
    ext = list(places)
    tall = range(-RADIUS, rows_lat + RADIUS)
    places += [(r, c) for r in tall for c in range(-RADIUS, 0)]
    places += [(r, rows_lon + c) for r in tall for c in range(RADIUS)]
    return np.array(places), ext


def per_device(
    grid_state, observations, obs_tile, obs_cell, cotangent, norm_gains,
    w_cross_query, w_cross_pairs, w_cross_out, w_near_proj, w_near_out, w_up, w_down,
):
    rows_lat, rows_lon, model = grid_state.shape
    lat_count = lax.axis_size("lat")
    devices = lat_count * lax.axis_size("lon")
    rows_obs = observations.shape[0]
    cap = max(2, 2 * rows_obs // devices)
    slots = devices * cap
    cells = rows_lat * rows_lon
    ff = w_up.shape[1]
    pairs_n = model // PAIR
    rim = RADIUS * rows_lon
    side = RADIUS * (rows_lat + 2 * RADIUS)
    places, ext_places = key_places(rows_lat, rows_lon)
    keys_n = len(places)
    keys_all = -(-keys_n // 256) * 256
    spot = {place: i for i, place in enumerate(ext_places)}
    tall = range(-RADIUS, rows_lat + RADIUS)
    select = np.zeros((2 * side, len(ext_places)), np.float32)
    for i, r in enumerate(tall):
        for c in range(RADIUS):
            select[i * RADIUS + c, spot[(r, c)]] = 1.0
            select[side + i * RADIUS + c, spot[(r, rows_lon - RADIUS + c)]] = 1.0
    select = select.astype(jnp.bfloat16)
    base = np.full((cells, keys_all), LOW_SCORE, np.float32)
    own_rows, own_cols = places[:cells, 0], places[:cells, 1]
    allowed = (np.abs(places[None, :, 0] - own_rows[:, None]) <= RADIUS) & (
        np.abs(places[None, :, 1] - own_cols[:, None]) <= RADIUS
    )
    base[:, :keys_n][allowed] = 0.0
    base = base.astype(jnp.bfloat16)
    key_rows = np.zeros((8, keys_all), np.int32)
    key_rows[:, :keys_n] = places[None, :, 0]
    key_lat = jnp.asarray(key_rows) + lax.axis_index("lat") * rows_lat
    inside = jnp.where((key_lat >= 0) & (key_lat < rows_lat * lat_count), 0.0, LOW_SCORE)
    inside = inside.astype(F32)

    dma = pltpu.SemaphoreType.DMA
    vm = pltpu.VMEM
    flat = grid_state.reshape(cells, model)
    cot = cotangent.reshape(cells, model)

    payload, placing = call(
        functools.partial(place_kernel, devices=devices, cap=cap, wide=rows_lon),
        (obs_tile.reshape(1, rows_obs), obs_cell.reshape(1, rows_obs), observations), "hhh",
        [((devices, cap, model + 128), BF, "h"), ((slots, rows_obs), BF, "h")],
        [vm((1, rows_obs), jnp.int32), vm((1, rows_obs), jnp.int32), vm((rows_obs, model), BF),
         vm((devices, cap, model + 128), BF), vm((slots, rows_obs), BF), dma((3,))],
        2 * rows_obs * slots * model, "place",
    )
    arrived = lax.all_to_all(payload, ("lat", "lon"), 0, 0, tiled=True)
    q_c, own_pairs, dhid = call(
        grid_kernel,
        (flat, cot, norm_gains, w_cross_query, w_cross_pairs, w_down), "hhvhhh",
        [((cells, model), BF, "h"), ((cells, 2 * model), BF, "h"), ((cells, ff), BF, "h")],
        [vm((cells, model), BF), vm((cells, model), BF), vm((cells, model), BF),
         vm((cells, 2 * model), BF), vm((cells, ff), BF),
         vm((cells, model), BF), vm((model, model), BF), vm((model, 2 * model), BF),
         vm((ff, model), BF), dma((5,)), dma((3,))],
        2 * cells * model * (3 * model + ff), "grid_proj",
    )
    state, top, bottom, slot_pairs, cross_w, cross_mix, own_w = call(
        functools.partial(cross_kernel, wide=rows_lon),
        (arrived, flat, q_c, own_pairs, norm_gains, w_cross_pairs, w_cross_out), "vhhhvhh",
        [((cells, model), F32, "h"), ((rim, model), BF), ((rim, model), BF),
         ((slots, 2 * model), BF, "h"), ((pairs_n, 2 * cells, slots), BF, "h"),
         ((cells, model), BF, "h"), ((cells, model), BF, "h")],
        [vm((slots, model + 128), BF), vm((model, 2 * model), BF), vm((model, model), BF),
         vm((GROUP, 2 * cells, slots), F32), vm((cells, slots), F32), vm((cells, model), BF),
         vm((cells, model), BF), vm((cells, 2 * model), BF), vm((cells, model), F32),
         vm((slots, 2 * model), BF), vm((pairs_n, 2 * cells, slots), BF), vm((cells, model), BF),
         vm((cells, model), BF), dma((2 * model // TILE,)), dma((9,))],
        2 * slots * model * 2 * model * 2, "cross",
    )
    south = line(top, -1)
    north = line(bottom, 1)
    q_n, kv_own = call(
        near_own_kernel, (top, bottom, w_near_proj), "vva",
        [((cells, model), BF), ((cells, 2 * model), BF)],
        [vm((cells, model), BF), vm((model, 3 * model), BF), dma((2,))],
        2 * cells * model * 3 * model, "near_own",
    )
    west_send, east_send = call(
        rim_kernel, (top, bottom, north, south, jnp.asarray(select), kv_own), "vvvvva",
        [((side, model), BF), ((side, model), BF)],
        [vm((cells + 2 * rim, model), BF)],
        2 * 2 * side * 2 * cells * model, "rim",
    )
    east = ring(west_send, -1)
    west = ring(east_send, 1)
    kv_rows, near_w, inner_mix, inner_peak, inner_sum = call(
        inner_kernel,
        (north, south, q_n, kv_own, jnp.asarray(base[:, : 2 * cells]), inside[:, : 2 * cells],
         w_near_proj), "vvvvvva",
        [((2 * rim, 2 * model), BF), ((pairs_n, 2 * cells, 2 * cells), BF, "h"),
         ((cells, model), F32), ((pairs_n, 2 * cells, PAIR), F32),
         ((pairs_n, 2 * cells, PAIR), F32)],
        [vm((2 * rim, model), BF), vm((model, 2 * model), BF), vm((2 * cells, 2 * model), BF),
         vm((cells, 2 * cells), F32), vm((GROUP, 2 * cells, 2 * cells), F32),
         vm((pairs_n, 2 * cells, 2 * cells), BF), dma((1,)), dma((1,))],
        4 * rim * model * 2 * model * 2, "inner",
    )
    outer = keys_all - 2 * cells
    after, hidden, dwest, deast, dq_rim, near_mix, dmix, dafter = call(
        near_kernel,
        (q_n, west, east, jnp.asarray(base[:, 2 * cells :]), inside[:, 2 * cells :], state, cot,
         dhid, norm_gains, inner_mix, inner_peak, inner_sum, w_near_proj, w_near_out, w_up),
        "vvvvvvvvvvvvaaa",
        [((cells, model), F32), ((cells, ff), BF), ((side, model), BF), ((side, model), BF),
         ((cells, model), F32), ((cells, model), BF), ((cells, model), BF),
         ((cells, model), F32)],
        [vm((model, 2 * model), BF), vm((model, model), BF), vm((model, ff), BF),
         vm((outer, 2 * model), BF), vm((outer, 2 * model), BF), vm((2 * side, model), BF),
         vm((pairs_n, 2 * cells, outer), BF), vm((GROUP, 2 * cells, outer), F32),
         vm((GROUP, 2 * cells, outer), BF), vm((cells, outer), F32), vm((cells, model), F32),
         vm((cells, model), BF), vm((cells, ff), BF), vm((cells, model), F32),
         vm((cells, model), BF), vm((cells, model), BF), dma((3,))],
        2e10, "near",
    )
    from_east = ring(dwest, -1)
    from_west = ring(deast, 1)
    middle = 2 * cells - PAIR
    dq_most, down_part, dn_rows = call(
        middle_back_kernel,
        (q_n, kv_own, kv_rows, near_mix, dmix, dq_rim, near_w, w_near_proj), "vvvvvvha",
        [((cells, model), F32), ((cells - PAIR, 2 * model), BF), ((2 * rim, model), F32)],
        [vm((model, 2 * model), BF), vm((middle, 2 * model), BF), vm((middle, 2 * model), BF),
         vm((pairs_n, 2 * cells, middle), BF), vm((GROUP, 2 * cells, middle), F32),
         vm((GROUP, 2 * cells, middle), BF), dma((2,))],
        4 * cells * model * 2 * model, "middle_back",
    )
    dnorth, dsouth = call(
        fold_kernel, (dn_rows, from_east, from_west, jnp.asarray(select[:, cells:])), "vvvv",
        [((rim, model), BF), ((rim, model), BF)],
        [vm((2 * side, model), BF)],
        2 * 2 * side * 2 * rim * model, "fold",
    )
    from_south = line(dnorth, -1)
    from_north = line(dsouth, 1)
    dn_own = call(
        own_back_kernel,
        (q_n, kv_own, near_mix, dmix, dq_most, down_part, from_east, from_west,
         jnp.asarray(select[:, :cells]), near_w, w_near_proj, dnorth), "vvvvvvvvvhaa",
        [((cells, model), F32)],
        [vm((cells, 3 * model), BF), vm((PAIR, 2 * model), BF),
         vm((pairs_n, 2 * cells, PAIR), BF), vm((GROUP, 2 * cells, PAIR), F32),
         vm((GROUP, 2 * cells, PAIR), BF), vm((2 * side, model), BF),
         vm((model, 3 * model), BF), dma((2,))],
        2 * cells * model * 4 * model, "own_back",
    )
    dstate, slot_grads, dmix_c, ds_c = call(
        cross_back_kernel,
        (dn_own, from_north, from_south, state, dafter, norm_gains, q_c, slot_pairs,
         cross_w, cross_mix, w_cross_pairs, w_cross_out), "vvvvvvvvvvaa",
        [((cells, model), F32, "h"), ((devices, cap, model), BF, "h"),
         ((cells, model), BF, "h"), ((pairs_n, 2 * cells, slots), BF, "h")],
        [vm((model, 2 * model), BF), vm((model, model), BF), vm((cells, model), BF),
         vm((cells, model), BF), vm((slots, 2 * model), BF), vm((GROUP, 2 * cells, slots), F32),
         vm((pairs_n, 2 * cells, slots), BF), vm((cells, model), F32),
         vm((devices, cap, model), BF), dma((2,)), dma((5,))],
        2 * slots * model * 2 * model * 2, "cross_back",
    )
    returned = lax.all_to_all(slot_grads, ("lat", "lon"), 0, 0, tiled=True)
    encoded = call(
        encode_kernel, (after, hidden, w_down, dmix_c), "vvha", [((cells, model), BF)],
        [vm((ff, model), BF), dma((1,))], 2 * cells * model * ff, "encode",
    )
    grid_grad = call(
        grid_back_kernel,
        (flat, dstate, norm_gains, q_c, own_pairs, cross_mix, own_w, dmix_c, slot_pairs, ds_c,
         w_cross_query, w_cross_pairs), "hhvhhhhhhhhh",
        [((cells, model), BF)],
        [vm((cells, model), BF), vm((cells, model), F32), vm((cells, model), BF),
         vm((cells, 2 * model), BF), vm((cells, model), BF), vm((cells, model), BF),
         vm((cells, model), BF), vm((slots, model), BF), vm((pairs_n, 2 * cells, slots), BF), vm((cells, model), BF),
         vm((cells, 2 * model), BF), vm((model, model), BF), vm((model, 2 * model), BF),
         vm((cells, model), F32), dma((11,))],
        2 * cells * model * 3 * model, "grid_back",
    )
    obs_grad = call(
        gather_kernel, (placing, returned), "hv", [((rows_obs, model), BF)],
        [vm((slots, rows_obs), BF), vm((slots, model), BF), dma((1,))], 2 * rows_obs * slots * model, "gather",
    )
    shape = (rows_lat, rows_lon, model)
    return encoded.reshape(shape), grid_grad.reshape(shape), obs_grad


def solution(mesh):
    return jax.shard_map(
        per_device,
        mesh=mesh,
        in_specs=(
            P("lat", "lon", None),
            P(("lat", "lon"), None),
            P(("lat", "lon"), None),
            P(("lat", "lon"), None),
            P("lat", "lon", None),
            P(), P(), P(), P(), P(), P(), P(), P(),
        ),
        out_specs=(P("lat", "lon", None), P("lat", "lon", None), P(("lat", "lon"), None)),
        check_vma=False,
    )
```

```python
import functools

import jax
import jax.numpy as jnp
import numpy as np
from jax import lax
from jax.experimental import pallas as pl
from jax.experimental.pallas import tpu as pltpu
from jax.sharding import PartitionSpec as P

HEADS = 16
RADIUS = 6
EPSILON = 1e-05
SPREAD = 32.0
LOW_SCORE = -1e30

BF = jnp.bfloat16
F32 = jnp.float32
NN = (((1,), (0,)), ((), ()))
NT = (((1,), (1,)), ((), ()))
TN = (((0,), (0,)), ((), ()))
CHUNK = 32
SOFT = 32
TILE = 1024
PAIR = 128
HALF = 64
SLACK_BYTES = 8 * 2**20
FEED_TILE = 1024
GROUP = 2
GELU_C = 0.7978845608028654
GELU_A = 0.044715


def dot(left, right, dims=NN):
    return lax.dot_general(left, right, dims, preferred_element_type=F32)


def iota(shape, dim):
    return lax.broadcasted_iota(jnp.int32, shape, dim)


def tiles_of(count, body, tile=TILE):
    @pl.loop(0, count // tile)
    def _(i):
        body(pl.multiple_of(i * tile, tile))


def row_chunks(count):
    return [pl.ds(i, CHUNK) for i in range(0, count, CHUNK)]


def unit(values):
    center = values - jnp.mean(values, -1, keepdims=True)
    scale = lax.rsqrt(jnp.mean(center * center, -1, keepdims=True) + EPSILON)
    return center * scale, scale


def norm_pull(values, gain, grad):
    normed, scale = unit(values)
    inner = grad * gain
    return scale * (
        inner
        - jnp.mean(inner, -1, keepdims=True)
        - normed * jnp.mean(inner * normed, -1, keepdims=True)
    )


def head_masks():
    left = (iota((1, PAIR), 1) < HALF).astype(F32)
    return left.astype(BF), (1.0 - left).astype(BF)


def stacked(values):
    left, right = head_masks()
    return jnp.concatenate([values * left, values * right], axis=0)


def merged(values):
    count = values.shape[0] // 2
    lanes = iota((count, PAIR), 1) < HALF
    return jnp.where(lanes, values[:count], values[count:])


def lane_sums(values):
    lanes = iota(values.shape, 1) < HALF
    first = jnp.sum(jnp.where(lanes, values, 0.0), -1, keepdims=True)
    second = jnp.sum(jnp.where(lanes, 0.0, values), -1, keepdims=True)
    return first, second


def fetch(sources, targets, sems):
    copies = [
        pltpu.make_async_copy(source, target, sems.at[i])
        for i, (source, target) in enumerate(zip(sources, targets))
    ]
    for copy in copies:
        copy.start()
    return copies


def call(body, ins, kinds, outs, scratch, flops, name):
    any_spec = pl.BlockSpec(memory_space=pl.ANY)
    vmem_spec = pl.BlockSpec(memory_space=pltpu.VMEM)
    moved = sum(x.size * x.dtype.itemsize for x in ins)
    moved += sum(int(np.prod(o[0])) * jnp.dtype(o[1]).itemsize for o in outs)
    held = sum(x.size * x.dtype.itemsize for x, k in zip(ins, kinds) if k == "v")
    held += sum(int(np.prod(o[0])) * jnp.dtype(o[1]).itemsize for o in outs if len(o) == 2)
    for item in scratch:
        if jnp.issubdtype(item.dtype, jnp.floating):
            held += int(np.prod(item.shape)) * jnp.dtype(item.dtype).itemsize
    single = len(outs) == 1
    shapes = [
        jax.ShapeDtypeStruct(*o) if len(o) == 2 else pltpu.HBM(o[0], o[1]) for o in outs
    ]
    specs = [vmem_spec if len(o) == 2 else any_spec for o in outs]
    ins = [
        pltpu.with_memory_space_constraint(x, pltpu.HBM) if k == "h" else x
        for x, k in zip(ins, kinds)
    ]
    return pl.pallas_call(
        body,
        name=name,
        out_shape=shapes[0] if single else shapes,
        in_specs=[vmem_spec if k == "v" else any_spec for k in kinds],
        out_specs=specs[0] if single else specs,
        scratch_shapes=scratch,
        compiler_params=pltpu.CompilerParams(vmem_limit_bytes=held + SLACK_BYTES),
        cost_estimate=pl.CostEstimate(
            flops=int(flops), bytes_accessed=int(moved), transcendentals=0
        ),
    )(*ins)


def place_kernel(
    tile_hbm, cell_hbm, obs_hbm, pay_hbm, place_hbm,
    tile_ref, cell_ref, obs_ref, pay_ref, place_ref, sems, *, devices, cap, wide,
):
    copies = fetch([tile_hbm, cell_hbm, obs_hbm], [tile_ref, cell_ref, obs_ref], sems)
    copies[0].wait()
    rows, model = obs_ref.shape
    slots = devices * cap
    tile = tile_ref[...]
    member = tile == iota((devices, rows), 0)
    earlier = (iota((rows, rows), 0) < iota((rows, rows), 1)).astype(F32).astype(BF)
    before = dot(member.astype(F32).astype(BF), earlier)
    rank = jnp.sum(jnp.where(member, before, 0.0), 0, keepdims=True).astype(jnp.int32)
    share = 2 * devices
    slot = (rank >> 1) * share + tile * 2 + (rank & 1)
    placing = (slot == iota((slots, rows), 0)).astype(F32).astype(BF)
    place_ref[...] = placing
    copies[1].wait()
    copies[2].wait()
    cell = cell_ref[...]
    shift = wide.bit_length() - 1
    line_no = iota((PAIR, rows), 0)
    moved = dot(placing, obs_ref[...]).astype(BF)
    code_rows = jnp.zeros((share, PAIR), F32)
    for part in range(cap // 2):
        rows_here = slice(part * share, (part + 1) * share)
        for j in range(model // PAIR):
            piece = moved[rows_here, j * PAIR : (j + 1) * PAIR]
            pay_ref[:, j * (cap // 2) + part] = piece.reshape(devices, 2, PAIR)
        codes = jnp.where(
            line_no == 2 * part,
            (cell >> shift) + 1,
            jnp.where(line_no == 2 * part + 1, (cell & (wide - 1)) + 1, 0),
        )
        code_rows = code_rows + dot(placing[rows_here], codes.astype(F32).astype(BF), NT)
    pay_ref[:, pay_ref.shape[1] - 1] = code_rows.astype(BF).reshape(devices, 2, PAIR)
    for copy in fetch([pay_ref, place_ref], [pay_hbm, place_hbm], sems):
        copy.wait()


def grid_kernel(
    grid_hbm, cot_hbm, gain_ref, wq_hbm, wp_hbm, wd_hbm, q_hbm, own_hbm, dh_hbm,
    grid_ref, cot_ref, q_ref, own_ref, dh_ref, nrm, wq, wp, wd, sems, out_sems,
):
    first, *copies = fetch(
        [grid_hbm, wq_hbm, wp_hbm, wd_hbm, cot_hbm], [grid_ref, wq, wp, wd, cot_ref], sems
    )
    cells, model = grid_ref.shape
    first.wait()
    for rows in row_chunks(cells):
        normed, _ = unit(grid_ref[rows, :].astype(F32))
        nrm[rows, :] = (normed * gain_ref[0:1, :]).astype(BF)
    copies[0].wait()

    def query(j):
        q_ref[:, pl.ds(j, TILE)] = (
            dot(nrm[...], wq[:, pl.ds(j, TILE)]) * HALF ** (-0.5)
        ).astype(BF)

    tiles_of(model, query)
    copies[1].wait()

    def own(j):
        own_ref[:, pl.ds(j, TILE)] = dot(nrm[...], wp[:, pl.ds(j, TILE)]).astype(BF)

    tiles_of(2 * model, own)
    copies[2].wait()
    copies[3].wait()

    def hidden(j):
        dh_ref[:, pl.ds(j, TILE)] = dot(cot_ref[...], wd[pl.ds(j, TILE), :], NT).astype(BF)

    tiles_of(dh_ref.shape[1], hidden)
    for copy in fetch([q_ref, own_ref, dh_ref], [q_hbm, own_hbm, dh_hbm], out_sems):
        copy.wait()


def cross_kernel(
    arr_ref, grid_hbm, q_hbm, own_hbm, gain_ref, wp_hbm, wo_hbm,
    state_hbm, top_ref, bottom_ref, pairs_hbm, wts_hbm, mix_hbm, ow_hbm,
    arr, wp, wo, scores, bias, grid_ref, q_ref, own_ref, state_ref, pairs_ref, wts_ref,
    mix_ref, ow_ref, sems, out_sems, *, wide,
):
    cells, model = grid_ref.shape
    parts = [pl.ds(j, TILE) for j in range(0, 2 * model, TILE)]
    copies = fetch([wp_hbm.at[:, c] for c in parts], [wp.at[:, c] for c in parts], sems)
    lates = out_sems.at[pl.ds(5, 4)]
    rim = top_ref.shape[0]
    slots = arr.shape[0]
    devices = arr_ref.shape[0]
    share = 2 * devices
    halves = slots // share
    for part in range(halves):
        for j in range(model // PAIR):
            arr[part * share : (part + 1) * share, j * PAIR : (j + 1) * PAIR] = arr_ref[
                :, j * halves + part
            ].reshape(share, PAIR)
    pick = (iota((8, 128), 0) == iota((8, 128), 1)).astype(F32).astype(BF)
    lines = dot(pick, arr_ref[:, arr_ref.shape[1] - 1].reshape(share, PAIR), NT)
    codes = [
        jnp.concatenate([lines[2 * p + i : 2 * p + i + 1] for p in range(halves)], axis=1)
        for i in range(2)
    ]
    cell = iota((cells, slots), 0)
    shift = wide.bit_length() - 1
    row_gap = (cell >> shift).astype(F32) - (codes[0] - 1.0)
    col_gap = (cell & (wide - 1)).astype(F32) - (codes[1] - 1.0)
    near = -(row_gap * row_gap + col_gap * col_gap) * (1.0 / SPREAD)
    bias[...] = jnp.where(codes[0] > 0.5, near, LOW_SCORE)
    for i, cols in enumerate(parts):
        copies[i].wait()
        if i == 0:
            late = fetch(
                [q_hbm, own_hbm, wo_hbm, grid_hbm], [q_ref, own_ref, wo, grid_ref], lates
            )
        pairs_ref[:, cols] = dot(arr[...], wp[:, cols]).astype(BF)
    leaving = fetch([pairs_ref], [pairs_hbm], out_sems.at[pl.ds(0, 1)])
    late[0].wait()
    late[1].wait()

    def soften(h, k, own_scores):
        own_weights = []
        for side in range(2):
            parts = []
            for i in range(0, cells, SOFT):
                own_score = own_scores[side][i : i + SOFT]
                x = scores[k, pl.ds(side * cells + i, SOFT), :] + bias[pl.ds(i, SOFT), :]
                peak = jnp.maximum(jnp.max(x, -1, keepdims=True), own_score)
                x = jnp.exp(x - peak)
                own_weight = jnp.exp(own_score - peak)
                inverse = 1.0 / (jnp.sum(x, -1, keepdims=True) + own_weight)
                wts_ref[h, pl.ds(side * cells + i, SOFT), :] = (x * inverse).astype(BF)
                parts.append(own_weight * inverse)
            own_weights.append(jnp.concatenate(parts, axis=0))
        lanes = iota((cells, PAIR), 1) < HALF
        return jnp.where(lanes, own_weights[0], own_weights[1]).astype(BF)

    @pl.loop(0, model // (PAIR * GROUP))
    def _(g):
        heads, own_scores, weights = [], [], []
        for k in range(GROUP):
            h = g * GROUP + k
            keys = pl.ds(pl.multiple_of(h * PAIR, PAIR), PAIR)
            vals = pl.ds(pl.multiple_of(model + h * PAIR, PAIR), PAIR)
            heads.append((h, keys, vals))
            q = q_ref[:, keys]
            scores[k] = dot(stacked(q), pairs_ref[:, keys], NT)
            own_scores.append(lane_sums(q.astype(F32) * own_ref[:, keys].astype(F32)))
        for k, (h, keys, vals) in enumerate(heads):
            weights.append(soften(h, k, own_scores[k]))
            ow_ref[:, keys] = weights[k]
        for k, (h, keys, vals) in enumerate(heads):
            mix = merged(dot(wts_ref[h], pairs_ref[:, vals]))
            mix_ref[:, keys] = (
                mix + weights[k].astype(F32) * own_ref[:, vals].astype(F32)
            ).astype(BF)

    leaving += fetch(
        [wts_ref, mix_ref, ow_ref], [wts_hbm, mix_hbm, ow_hbm], out_sems.at[pl.ds(1, 3)]
    )
    late[2].wait()
    late[3].wait()

    def project_out(j):
        state_ref[:, pl.ds(j, TILE)] = grid_ref[:, pl.ds(j, TILE)].astype(F32) + dot(
            mix_ref[...], wo[:, pl.ds(j, TILE)]
        )

    tiles_of(model, project_out)
    leaving += fetch([state_ref], [state_hbm], out_sems.at[pl.ds(4, 1)])
    for i in range(0, cells, CHUNK):
        normed, _ = unit(state_ref[pl.ds(i, CHUNK), :])
        normed = (normed * gain_ref[1:2, :]).astype(BF)
        if i < rim:
            top_ref[pl.ds(i, CHUNK), :] = normed
        else:
            bottom_ref[pl.ds(i - rim, CHUNK), :] = normed
    for copy in leaving:
        copy.wait()


def near_own_kernel(top_ref, bottom_ref, w_hbm, q_ref, kv_ref, nrm, w, sems):
    cells, model = nrm.shape
    rim = top_ref.shape[0]
    copies = fetch(
        [w_hbm.at[:, pl.ds(0, model)], w_hbm.at[:, pl.ds(model, 2 * model)]],
        [w.at[:, pl.ds(0, model)], w.at[:, pl.ds(model, 2 * model)]],
        sems,
    )
    nrm[pl.ds(0, rim), :] = top_ref[...]
    nrm[pl.ds(rim, rim), :] = bottom_ref[...]
    copies[0].wait()

    def query(j):
        q_ref[:, pl.ds(j, TILE)] = (
            dot(nrm[...], w[:, pl.ds(j, TILE)]) * HALF ** (-0.5)
        ).astype(BF)

    tiles_of(model, query)
    copies[1].wait()

    def pairs(j):
        kv_ref[:, pl.ds(j, TILE)] = dot(
            nrm[...], w[:, pl.ds(pl.multiple_of(model + j, TILE), TILE)]
        ).astype(BF)

    tiles_of(2 * model, pairs)


def rim_kernel(
    top_ref, bottom_ref, north_ref, south_ref, sel_ref, _, west_ref, east_ref, ext
):
    rim, model = north_ref.shape
    for i, part in enumerate((top_ref, bottom_ref, north_ref, south_ref)):
        ext[pl.ds(i * rim, rim), :] = part[...]
    side = west_ref.shape[0]

    def pick(j):
        both = dot(sel_ref[...], ext[:, pl.ds(j, TILE)]).astype(BF)
        west_ref[:, pl.ds(j, TILE)] = both[:side]
        east_ref[:, pl.ds(j, TILE)] = both[side:]

    tiles_of(model, pick)


def spread(first, second):
    lanes = iota((first.shape[0], PAIR), 1) < HALF
    return jnp.where(lanes, first, second)


def inner_kernel(
    north_ref, south_ref, q_ref, kvo_ref, base_ref, inside_ref, w_hbm,
    kvr_ref, wts_hbm, mix_ref, peak_ref, sum_ref,
    x, w, kv, bias, scores, wts, sems, out_sems,
):
    rim, model = north_ref.shape
    cells = q_ref.shape[0]
    copies = fetch([w_hbm.at[:, pl.ds(model, 2 * model)]], [w], sems)
    x[pl.ds(0, rim), :] = north_ref[...]
    x[pl.ds(rim, rim), :] = south_ref[...]
    kv[pl.ds(0, cells), :] = kvo_ref[...]
    bias[...] = base_ref[...].astype(F32) + inside_ref[0:1, :]
    copies[0].wait()

    def pairs(j):
        part = dot(x[...], w[:, pl.ds(j, TILE)]).astype(BF)
        kvr_ref[:, pl.ds(j, TILE)] = part
        kv[pl.ds(cells, cells), pl.ds(j, TILE)] = part

    tiles_of(2 * model, pairs)

    @pl.loop(0, model // (PAIR * GROUP))
    def _(g):
        heads = []
        for k in range(GROUP):
            h = g * GROUP + k
            keys = pl.ds(pl.multiple_of(h * PAIR, PAIR), PAIR)
            vals = pl.ds(pl.multiple_of(model + h * PAIR, PAIR), PAIR)
            heads.append((h, keys, vals))
            scores[k] = dot(stacked(q_ref[:, keys]), kv[:, keys], NT)
        for k, (h, keys, vals) in enumerate(heads):
            for start in range(0, 2 * cells, SOFT):
                rows = pl.ds(start, SOFT)
                v = scores[k, rows, :] + bias[pl.ds(start % cells, SOFT), :]
                peak = jnp.max(v, -1, keepdims=True)
                v = jnp.exp(v - peak)
                wts[h, rows, :] = v.astype(BF)
                peak_ref[h, rows, :] = jnp.broadcast_to(peak, (SOFT, PAIR))
                sum_ref[h, rows, :] = jnp.broadcast_to(
                    jnp.sum(v, -1, keepdims=True), (SOFT, PAIR)
                )
        for k, (h, keys, vals) in enumerate(heads):
            mix_ref[:, keys] = merged(dot(wts[h], kv[:, vals]))

    for copy in fetch([wts], [wts_hbm], out_sems):
        copy.wait()


def near_back_loop(q_ref, kv, kv_rows, wts, cols, mix, dmix, dkv, scores, ds, put):
    cells, model = q_ref.shape

    @pl.loop(0, model // (PAIR * GROUP))
    def _(g):
        heads, deltas = [], []
        for k in range(GROUP):
            h = g * GROUP + k
            keys = pl.ds(pl.multiple_of(h * PAIR, PAIR), PAIR)
            vals = pl.ds(pl.multiple_of(model + h * PAIR, PAIR), PAIR)
            heads.append((h, keys, vals))
            grad = dmix[:, keys]
            scores[k, :, pl.ds(0, cols.size)] = dot(stacked(grad), kv[kv_rows, vals], NT)
            deltas.append(lane_sums(grad.astype(F32) * mix[:, keys].astype(F32)))
        for k, (h, keys, vals) in enumerate(heads):
            for s in range(2):
                for i in range(0, cells, SOFT):
                    rows = pl.ds(s * cells + i, SOFT)
                    ds[k, rows, :] = (
                        wts[h, rows, cols].astype(F32)
                        * (scores[k, rows, pl.ds(0, cols.size)] - deltas[k][s][i : i + SOFT])
                    ).astype(BF)
        for k, (h, keys, vals) in enumerate(heads):
            put(keys, merged(dot(ds[k], kv[kv_rows, keys])))
            dkv[:, keys] = dot(stacked(q_ref[:, keys]), ds[k], TN).T.astype(BF)
            dkv[:, vals] = dot(stacked(dmix[:, keys]), wts[h, :, cols], TN).T.astype(BF)


def near_kernel(
    q_ref, west_ref, east_ref, base_ref, inside_ref, state_ref, cot_ref, dh_ref, gain_ref,
    mix_in_ref, peak_ref, sum_ref, wn_hbm, wo_hbm, wu_hbm,
    after_hbm, hid_hbm, dwest_ref, deast_ref, dq_ref, mix, dscaled_ref, dafter_ref,
    wkv, wo, wu, kv, dkv, x, wts, scores, ds, bias, share, nrm, du, acc, dab, dmix,
    after_ref, hid_ref, sems, out_sems,
):
    cells, model = state_ref.shape
    keys_all = kv.shape[0]
    side = west_ref.shape[0]
    ends = 2 * side
    copies = fetch([wn_hbm.at[:, pl.ds(model, 2 * model)]], [wkv], sems.at[pl.ds(0, 1)])
    x[pl.ds(0, side), :] = west_ref[...]
    x[pl.ds(side, side), :] = east_ref[...]
    kv[pl.ds(ends, keys_all - ends), :] = jnp.zeros((keys_all - ends, 2 * model), BF)
    bias[...] = base_ref[...].astype(F32) + inside_ref[0:1, :]
    copies[0].wait()
    copies += fetch([wo_hbm, wu_hbm], [wo, wu], sems.at[pl.ds(1, 2)])

    def project(j):
        kv[pl.ds(0, ends), pl.ds(j, TILE)] = dot(x[...], wkv[:, pl.ds(j, TILE)]).astype(BF)

    tiles_of(2 * model, project)

    def widened(values):
        return jnp.concatenate([values] * (keys_all // PAIR), axis=1)

    @pl.loop(0, model // (PAIR * GROUP))
    def _(g):
        heads = []
        for k in range(GROUP):
            h = g * GROUP + k
            keys = pl.ds(pl.multiple_of(h * PAIR, PAIR), PAIR)
            vals = pl.ds(pl.multiple_of(model + h * PAIR, PAIR), PAIR)
            heads.append((h, keys, vals))
            scores[k] = dot(stacked(q_ref[:, keys]), kv[:, keys], NT)
        for k, (h, keys, vals) in enumerate(heads):
            for i in range(0, cells, SOFT):
                here = pl.ds(i, SOFT)
                shares = []
                for s in range(2):
                    rows = pl.ds(s * cells + i, SOFT)
                    before = peak_ref[h, rows, :]
                    v = scores[k, rows, :] + bias[here, :]
                    peak = jnp.maximum(jnp.max(v, -1, keepdims=True), before)
                    v = jnp.exp(v - widened(peak))
                    part = jnp.exp(before - peak)
                    total = jnp.sum(v, -1, keepdims=True) + part * sum_ref[h, rows, :]
                    inverse = 1.0 / total
                    wts[h, rows, :] = (v * widened(inverse)).astype(BF)
                    shares.append(part * inverse)
                share[here, keys] = spread(*shares)
        for k, (h, keys, vals) in enumerate(heads):
            rims = merged(dot(wts[h], kv[:, vals]))
            mix[:, keys] = (rims + mix_in_ref[:, keys] * share[:, keys]).astype(BF)

    copies[1].wait()

    def project_out(j):
        after_ref[:, pl.ds(j, TILE)] = state_ref[:, pl.ds(j, TILE)] + dot(
            mix[...], wo[:, pl.ds(j, TILE)]
        )

    tiles_of(model, project_out)
    for rows in row_chunks(cells):
        normed, _ = unit(after_ref[rows, :])
        nrm[rows, :] = (normed * gain_ref[2:3, :]).astype(BF)
    copies[2].wait()

    def feed(j):
        cols = pl.ds(j, FEED_TILE)
        u = dot(nrm[...], wu[:, cols])
        square = u * u
        t = jnp.tanh(GELU_C * (u + GELU_A * (square * u)))
        half = 0.5 * (1.0 + t)
        hid_ref[:, cols] = (u * half).astype(BF)
        slope = half + (0.5 * GELU_C) * u * (1.0 - t * t) * (1.0 + 3.0 * GELU_A * square)
        du[:, cols] = (dh_ref[:, cols].astype(F32) * slope).astype(BF)

    tiles_of(du.shape[1], feed, FEED_TILE)
    leaving = fetch([after_ref, hid_ref], [after_hbm, hid_hbm], out_sems)

    def feed_back(j):
        acc[:, pl.ds(j, TILE)] = dot(du[...], wu[pl.ds(j, TILE), :], NT)

    tiles_of(model, feed_back)
    for rows in row_chunks(cells):
        grad = acc[rows, :].astype(BF).astype(F32)
        total = cot_ref[rows, :].astype(F32) + norm_pull(
            after_ref[rows, :], gain_ref[2:3, :], grad
        )
        dafter_ref[rows, :] = total
        dab[rows, :] = total.astype(BF)

    def mix_back(j):
        cols = pl.ds(j, TILE)
        grad = dot(dab[...], wo[cols, :], NT)
        dmix[:, cols] = grad.astype(BF)
        dscaled_ref[:, cols] = (grad * share[:, cols]).astype(BF)

    tiles_of(model, mix_back)
    outer = pl.ds(0, keys_all)

    def put(keys, dq):
        dq_ref[:, keys] = dq

    near_back_loop(q_ref, kv, outer, wts, outer, mix, dmix, dkv, scores, ds, put)

    def rim_back(j):
        both = dot(dkv[pl.ds(0, 2 * side), :], wkv[pl.ds(j, TILE), :], NT).astype(BF)
        dwest_ref[:, pl.ds(j, TILE)] = both[:side]
        deast_ref[:, pl.ds(j, TILE)] = both[side:]

    tiles_of(model, rim_back)
    for copy in leaving:
        copy.wait()


def middle_back_kernel(
    q_ref, kvo_ref, kvr_ref, mix, dmix, dq_in_ref, wts_hbm, wn_hbm,
    dq_ref, down_ref, dn_ref, wkv, kv, dkv, wts, scores, ds, sems,
):
    cells, model = q_ref.shape
    part = cells - PAIR
    copies = fetch(
        [wts_hbm.at[:, :, pl.ds(PAIR, kv.shape[0])], wn_hbm.at[:, pl.ds(model, 2 * model)]],
        [wts, wkv],
        sems,
    )
    kv[pl.ds(0, part), :] = kvo_ref[pl.ds(PAIR, part), :]
    kv[pl.ds(part, cells), :] = kvr_ref[...]
    copies[0].wait()

    def put(keys, dq):
        dq_ref[:, keys] = dq + dq_in_ref[:, keys]

    whole = pl.ds(0, kv.shape[0])
    near_back_loop(q_ref, kv, whole, wts, whole, mix, dmix, dkv, scores, ds, put)
    down_ref[...] = dkv[pl.ds(0, part), :]
    copies[1].wait()

    def back(j):
        dn_ref[:, pl.ds(j, TILE)] = dot(
            dkv[pl.ds(part, cells), :], wkv[pl.ds(j, TILE), :], NT
        )

    tiles_of(model, back)


def encode_kernel(after_ref, hid_ref, wd_hbm, _, enc_ref, wd, sems):
    copies = fetch([wd_hbm], [wd], sems)
    copies[0].wait()

    def down(j):
        enc_ref[:, pl.ds(j, TILE)] = (
            after_ref[:, pl.ds(j, TILE)] + dot(hid_ref[...], wd[:, pl.ds(j, TILE)])
        ).astype(BF)

    tiles_of(after_ref.shape[1], down)


def fold_kernel(dn_ref, from_east_ref, from_west_ref, sel_ref, north_ref, south_ref, x):
    rim, model = north_ref.shape
    side = from_east_ref.shape[0]
    x[pl.ds(0, side), :] = from_west_ref[...]
    x[pl.ds(side, side), :] = from_east_ref[...]

    def fold(j):
        cols = pl.ds(j, TILE)
        total = (dn_ref[:, cols] + dot(sel_ref[...], x[:, cols], TN)).astype(BF)
        north_ref[:, cols] = total[:rim]
        south_ref[:, cols] = total[rim:]

    tiles_of(model, fold)


def own_back_kernel(
    q_ref, kvo_ref, mix, dmix, dq_in_ref, down_ref, from_east_ref, from_west_ref, sel_ref,
    wts_hbm, w_hbm, _, dn_ref, dqkv, dkv, wts, scores, ds, x, w, sems,
):
    copies = fetch([wts_hbm.at[:, :, pl.ds(0, PAIR)], w_hbm], [wts, w], sems)
    cells, model = q_ref.shape
    side = from_east_ref.shape[0]
    x[pl.ds(0, side), :] = from_west_ref[...]
    x[pl.ds(side, side), :] = from_east_ref[...]
    copies[0].wait()

    def put(keys, dq):
        dqkv[:, keys] = ((dq + dq_in_ref[:, keys]) * HALF ** (-0.5)).astype(BF)

    whole = pl.ds(0, PAIR)
    near_back_loop(q_ref, kvo_ref, whole, wts, whole, mix, dmix, dkv, scores, ds, put)
    dqkv[pl.ds(0, PAIR), pl.ds(model, 2 * model)] = dkv[...]
    dqkv[pl.ds(PAIR, cells - PAIR), pl.ds(model, 2 * model)] = down_ref[...]
    copies[1].wait()

    def back(j):
        cols = pl.ds(j, TILE)
        dn_ref[:, cols] = dot(dqkv[...], w[cols, :], NT) + dot(
            sel_ref[...], x[:, cols], TN
        )

    tiles_of(model, back)


def cross_back_kernel(
    dn_ref, north_ref, south_ref, state_ref, dafter_ref, gain_ref, q_ref, pairs_ref,
    wts_ref, mix_ref, wp_hbm, wo_hbm,
    dstate_hbm, slot_hbm, dmix_hbm, ds_hbm,
    wp, wo, dsb, dmix, dpairs, scores, ds, dstate_ref, slot_ref, sems, out_sems,
):
    copies = fetch([wo_hbm, wp_hbm], [wo, wp], sems)
    cells, model = state_ref.shape
    rim = north_ref.shape[0]
    for i in range(0, cells, CHUNK):
        rows = pl.ds(i, CHUNK)
        other = north_ref[rows, :] if i < rim else south_ref[pl.ds(i - rim, CHUNK), :]
        grad = (dn_ref[rows, :] + other.astype(F32)).astype(BF).astype(F32)
        total = dafter_ref[rows, :] + norm_pull(state_ref[rows, :], gain_ref[1:2, :], grad)
        dstate_ref[rows, :] = total
        dsb[rows, :] = total.astype(BF)
    copies[0].wait()

    def mix_back(j):
        dmix[:, pl.ds(j, TILE)] = dot(dsb[...], wo[pl.ds(j, TILE), :], NT).astype(BF)

    tiles_of(model, mix_back)

    @pl.loop(0, model // (PAIR * GROUP))
    def _(g):
        heads, deltas = [], []
        for k in range(GROUP):
            h = g * GROUP + k
            keys = pl.ds(pl.multiple_of(h * PAIR, PAIR), PAIR)
            vals = pl.ds(pl.multiple_of(model + h * PAIR, PAIR), PAIR)
            heads.append((h, keys, vals))
            grad = dmix[:, keys]
            scores[k] = dot(stacked(grad), pairs_ref[:, vals], NT)
            deltas.append(lane_sums(grad.astype(F32) * mix_ref[:, keys].astype(F32)))
        for k, (h, keys, vals) in enumerate(heads):
            for s in range(2):
                for i in range(0, cells, SOFT):
                    rows = pl.ds(s * cells + i, SOFT)
                    ds[h, rows, :] = (
                        wts_ref[h, rows, :].astype(F32)
                        * (scores[k, rows, :] - deltas[k][s][i : i + SOFT])
                    ).astype(BF)
        for k, (h, keys, vals) in enumerate(heads):
            dpairs[:, keys] = dot(stacked(q_ref[:, keys]), ds[h], TN).T.astype(BF)
            dpairs[:, vals] = dot(stacked(dmix[:, keys]), wts_ref[h], TN).T.astype(BF)

    leaving = fetch(
        [dstate_ref, dmix, ds], [dstate_hbm, dmix_hbm, ds_hbm],
        out_sems.at[pl.ds(0, 3)],
    )
    copies[1].wait()
    half = model // 2
    for i in range(2):
        cols = pl.ds(i * half, half)
        grads = dot(dpairs[...], wp[cols, :], NT).astype(BF)
        for part in range(slot_ref.shape[1] // 2):
            count = 2 * slot_ref.shape[0]
            slot_ref[:, 2 * part : 2 * part + 2, cols] = grads[
                part * count : (part + 1) * count
            ].reshape(slot_ref.shape[0], 2, half)
        leaving += fetch(
            [slot_ref.at[:, :, cols]], [slot_hbm.at[:, :, cols]], out_sems.at[pl.ds(3 + i, 1)]
        )
    for copy in leaving:
        copy.wait()


def gather_kernel(place_hbm, ret_ref, out_ref, place_ref, ret, sems):
    copies = fetch([place_hbm], [place_ref], sems)
    count = 2 * ret_ref.shape[0]
    for part in range(ret_ref.shape[1] // 2):
        ret[part * count : (part + 1) * count] = ret_ref[:, 2 * part : 2 * part + 2].reshape(
            count, ret.shape[1]
        )
    copies[0].wait()
    out_ref[...] = dot(place_ref[...], ret[...], TN).astype(BF)


def grid_back_kernel(
    grid_hbm, dstate_hbm, gain_ref, q_hbm, own_hbm, mix_hbm, ow_hbm, dmix_hbm,
    pairs_hbm, ds_hbm, wq_hbm, wp_hbm, out_ref,
    grid_ref, dstate_ref, q_ref, own_ref, mix_ref, ow_ref, dmix,
    pairs, ds, dq_ref, down_ref, wq, wp, acc, sems,
):
    cells, model = grid_ref.shape
    first = fetch(
        [q_hbm, own_hbm, mix_hbm, ow_hbm, dmix_hbm, pairs_hbm.at[:, pl.ds(0, model)], ds_hbm],
        [q_ref, own_ref, mix_ref, ow_ref, dmix, pairs, ds],
        sems.at[pl.ds(0, 7)],
    )
    copies = fetch(
        [wq_hbm, wp_hbm, grid_hbm, dstate_hbm],
        [wq, wp, grid_ref, dstate_ref],
        sems.at[pl.ds(7, 4)],
    )
    for copy in first:
        copy.wait()

    def one(h):
        keys = pl.ds(pl.multiple_of(h * PAIR, PAIR), PAIR)
        vals = pl.ds(pl.multiple_of(model + h * PAIR, PAIR), PAIR)
        grad = dmix[:, keys].astype(F32)
        weight = ow_ref[:, keys].astype(F32)
        gap = own_ref[:, vals].astype(F32) - mix_ref[:, keys].astype(F32)
        own_grad = weight * spread(*lane_sums(grad * gap))
        dq = merged(dot(ds[h], pairs[:, keys])) + own_grad * own_ref[:, keys].astype(F32)
        dq_ref[:, keys] = (dq * HALF ** (-0.5)).astype(BF)
        down_ref[:, keys] = (own_grad * q_ref[:, keys].astype(F32)).astype(BF)
        down_ref[:, vals] = (weight * grad).astype(BF)

    @pl.loop(0, model // (PAIR * GROUP))
    def _(g):
        for k in range(GROUP):
            one(g * GROUP + k)

    for copy in copies:
        copy.wait()

    def back(j):
        acc[:, pl.ds(j, TILE)] = dot(dq_ref[...], wq[pl.ds(j, TILE), :], NT) + dot(
            down_ref[...], wp[pl.ds(j, TILE), :], NT
        )

    tiles_of(model, back)
    for rows in row_chunks(cells):
        grad = acc[rows, :].astype(BF).astype(F32)
        out_ref[rows, :] = (
            dstate_ref[rows, :]
            + norm_pull(grid_ref[rows, :].astype(F32), gain_ref[0:1, :], grad)
        ).astype(BF)


def ring(value, by):
    size = lax.axis_size("lon")
    return lax.ppermute(value, "lon", [(i, (i + by) % size) for i in range(size)])


def line(value, by):
    size = lax.axis_size("lat")
    pairs = [(i, i + by) for i in range(size) if 0 <= i + by < size]
    return lax.ppermute(value, "lat", pairs)


def key_places(rows_lat, rows_lon):
    places = [(r, c) for r in range(rows_lat) for c in range(rows_lon)]
    places += [(r, c) for r in range(-RADIUS, 0) for c in range(rows_lon)]
    places += [(rows_lat + r, c) for r in range(RADIUS) for c in range(rows_lon)]
    ext = list(places)
    tall = range(-RADIUS, rows_lat + RADIUS)
    places += [(r, c) for r in tall for c in range(-RADIUS, 0)]
    places += [(r, rows_lon + c) for r in tall for c in range(RADIUS)]
    return np.array(places), ext


def per_device(
    grid_state, observations, obs_tile, obs_cell, cotangent, norm_gains,
    w_cross_query, w_cross_pairs, w_cross_out, w_near_proj, w_near_out, w_up, w_down,
):
    rows_lat, rows_lon, model = grid_state.shape
    lat_count = lax.axis_size("lat")
    devices = lat_count * lax.axis_size("lon")
    rows_obs = observations.shape[0]
    cap = max(2, 2 * rows_obs // devices)
    slots = devices * cap
    cells = rows_lat * rows_lon
    ff = w_up.shape[1]
    pairs_n = model // PAIR
    rim = RADIUS * rows_lon
    side = RADIUS * (rows_lat + 2 * RADIUS)
    places, ext_places = key_places(rows_lat, rows_lon)
    keys_n = len(places)
    keys_all = -(-keys_n // 256) * 256
    spot = {place: i for i, place in enumerate(ext_places)}
    tall = range(-RADIUS, rows_lat + RADIUS)
    select = np.zeros((2 * side, len(ext_places)), np.float32)
    for i, r in enumerate(tall):
        for c in range(RADIUS):
            select[i * RADIUS + c, spot[(r, c)]] = 1.0
            select[side + i * RADIUS + c, spot[(r, rows_lon - RADIUS + c)]] = 1.0
    select = select.astype(jnp.bfloat16)
    base = np.full((cells, keys_all), LOW_SCORE, np.float32)
    own_rows, own_cols = places[:cells, 0], places[:cells, 1]
    allowed = (np.abs(places[None, :, 0] - own_rows[:, None]) <= RADIUS) & (
        np.abs(places[None, :, 1] - own_cols[:, None]) <= RADIUS
    )
    base[:, :keys_n][allowed] = 0.0
    base = base.astype(jnp.bfloat16)
    key_rows = np.zeros((8, keys_all), np.int32)
    key_rows[:, :keys_n] = places[None, :, 0]
    key_lat = jnp.asarray(key_rows) + lax.axis_index("lat") * rows_lat
    inside = jnp.where((key_lat >= 0) & (key_lat < rows_lat * lat_count), 0.0, LOW_SCORE)
    inside = inside.astype(F32)

    dma = pltpu.SemaphoreType.DMA
    vm = pltpu.VMEM
    flat = grid_state.reshape(cells, model)
    cot = cotangent.reshape(cells, model)

    sent = (devices, cap // 2 * (model // PAIR) + 1, 2, PAIR)
    payload, placing = call(
        functools.partial(place_kernel, devices=devices, cap=cap, wide=rows_lon),
        (obs_tile.reshape(1, rows_obs), obs_cell.reshape(1, rows_obs), observations), "hhh",
        [(sent, BF, "h"), ((slots, rows_obs), BF, "h")],
        [vm((1, rows_obs), jnp.int32), vm((1, rows_obs), jnp.int32), vm((rows_obs, model), BF),
         vm(sent, BF), vm((slots, rows_obs), BF), dma((3,))],
        2 * rows_obs * slots * model, "place",
    )
    arrived = lax.all_to_all(payload, ("lat", "lon"), 0, 0, tiled=True)
    q_c, own_pairs, dhid = call(
        grid_kernel,
        (flat, cot, norm_gains, w_cross_query, w_cross_pairs, w_down), "hhvhhh",
        [((cells, model), BF, "h"), ((cells, 2 * model), BF, "h"), ((cells, ff), BF, "h")],
        [vm((cells, model), BF), vm((cells, model), BF), vm((cells, model), BF),
         vm((cells, 2 * model), BF), vm((cells, ff), BF),
         vm((cells, model), BF), vm((model, model), BF), vm((model, 2 * model), BF),
         vm((ff, model), BF), dma((5,)), dma((3,))],
        2 * cells * model * (3 * model + ff), "grid_proj",
    )
    state, top, bottom, slot_pairs, cross_w, cross_mix, own_w = call(
        functools.partial(cross_kernel, wide=rows_lon),
        (arrived, flat, q_c, own_pairs, norm_gains, w_cross_pairs, w_cross_out), "vhhhvhh",
        [((cells, model), F32, "h"), ((rim, model), BF), ((rim, model), BF),
         ((slots, 2 * model), BF, "h"), ((pairs_n, 2 * cells, slots), BF, "h"),
         ((cells, model), BF, "h"), ((cells, model), BF, "h")],
        [vm((slots, model), BF), vm((model, 2 * model), BF), vm((model, model), BF),
         vm((GROUP, 2 * cells, slots), F32), vm((cells, slots), F32), vm((cells, model), BF),
         vm((cells, model), BF), vm((cells, 2 * model), BF), vm((cells, model), F32),
         vm((slots, 2 * model), BF), vm((pairs_n, 2 * cells, slots), BF), vm((cells, model), BF),
         vm((cells, model), BF), dma((2 * model // TILE,)), dma((9,))],
        2 * slots * model * 2 * model * 2, "cross",
    )
    south = line(top, -1)
    north = line(bottom, 1)
    q_n, kv_own = call(
        near_own_kernel, (top, bottom, w_near_proj), "vva",
        [((cells, model), BF), ((cells, 2 * model), BF)],
        [vm((cells, model), BF), vm((model, 3 * model), BF), dma((2,))],
        2 * cells * model * 3 * model, "near_own",
    )
    west_send, east_send = call(
        rim_kernel, (top, bottom, north, south, jnp.asarray(select), kv_own), "vvvvva",
        [((side, model), BF), ((side, model), BF)],
        [vm((cells + 2 * rim, model), BF)],
        2 * 2 * side * 2 * cells * model, "rim",
    )
    east = ring(west_send, -1)
    west = ring(east_send, 1)
    kv_rows, near_w, inner_mix, inner_peak, inner_sum = call(
        inner_kernel,
        (north, south, q_n, kv_own, jnp.asarray(base[:, : 2 * cells]), inside[:, : 2 * cells],
         w_near_proj), "vvvvvva",
        [((2 * rim, 2 * model), BF), ((pairs_n, 2 * cells, 2 * cells), BF, "h"),
         ((cells, model), F32), ((pairs_n, 2 * cells, PAIR), F32),
         ((pairs_n, 2 * cells, PAIR), F32)],
        [vm((2 * rim, model), BF), vm((model, 2 * model), BF), vm((2 * cells, 2 * model), BF),
         vm((cells, 2 * cells), F32), vm((GROUP, 2 * cells, 2 * cells), F32),
         vm((pairs_n, 2 * cells, 2 * cells), BF), dma((1,)), dma((1,))],
        4 * rim * model * 2 * model * 2, "inner",
    )
    outer = keys_all - 2 * cells
    after, hidden, dwest, deast, dq_rim, near_mix, dmix, dafter = call(
        near_kernel,
        (q_n, west, east, jnp.asarray(base[:, 2 * cells :]), inside[:, 2 * cells :], state, cot,
         dhid, norm_gains, inner_mix, inner_peak, inner_sum, w_near_proj, w_near_out, w_up),
        "vvvvvvvvvvvvaaa",
        [((cells, model), F32, "h"), ((cells, ff), BF, "h"), ((side, model), BF),
         ((side, model), BF), ((cells, model), F32), ((cells, model), BF), ((cells, model), BF),
         ((cells, model), F32)],
        [vm((model, 2 * model), BF), vm((model, model), BF), vm((model, ff), BF),
         vm((outer, 2 * model), BF), vm((outer, 2 * model), BF), vm((2 * side, model), BF),
         vm((pairs_n, 2 * cells, outer), BF), vm((GROUP, 2 * cells, outer), F32),
         vm((GROUP, 2 * cells, outer), BF), vm((cells, outer), F32), vm((cells, model), F32),
         vm((cells, model), BF), vm((cells, ff), BF), vm((cells, model), F32),
         vm((cells, model), BF), vm((cells, model), BF), vm((cells, model), F32),
         vm((cells, ff), BF), dma((3,)), dma((2,))],
        2e10, "near",
    )
    from_east = ring(dwest, -1)
    from_west = ring(deast, 1)
    middle = 2 * cells - PAIR
    dq_most, down_part, dn_rows = call(
        middle_back_kernel,
        (q_n, kv_own, kv_rows, near_mix, dmix, dq_rim, near_w, w_near_proj), "vvvvvvha",
        [((cells, model), F32), ((cells - PAIR, 2 * model), BF), ((2 * rim, model), F32)],
        [vm((model, 2 * model), BF), vm((middle, 2 * model), BF), vm((middle, 2 * model), BF),
         vm((pairs_n, 2 * cells, middle), BF), vm((GROUP, 2 * cells, middle), F32),
         vm((GROUP, 2 * cells, middle), BF), dma((2,))],
        4 * cells * model * 2 * model, "middle_back",
    )
    dnorth, dsouth = call(
        fold_kernel, (dn_rows, from_east, from_west, jnp.asarray(select[:, cells:])), "vvvv",
        [((rim, model), BF), ((rim, model), BF)],
        [vm((2 * side, model), BF)],
        2 * 2 * side * 2 * rim * model, "fold",
    )
    from_south = line(dnorth, -1)
    from_north = line(dsouth, 1)
    dn_own = call(
        own_back_kernel,
        (q_n, kv_own, near_mix, dmix, dq_most, down_part, from_east, from_west,
         jnp.asarray(select[:, :cells]), near_w, w_near_proj, dnorth), "vvvvvvvvvhaa",
        [((cells, model), F32)],
        [vm((cells, 3 * model), BF), vm((PAIR, 2 * model), BF),
         vm((pairs_n, 2 * cells, PAIR), BF), vm((GROUP, 2 * cells, PAIR), F32),
         vm((GROUP, 2 * cells, PAIR), BF), vm((2 * side, model), BF),
         vm((model, 3 * model), BF), dma((2,))],
        2 * cells * model * 4 * model, "own_back",
    )
    dstate, slot_grads, dmix_c, ds_c = call(
        cross_back_kernel,
        (dn_own, from_north, from_south, state, dafter, norm_gains, q_c, slot_pairs,
         cross_w, cross_mix, w_cross_pairs, w_cross_out), "vvvvvvvvvvaa",
        [((cells, model), F32, "h"), ((devices, cap, model), BF, "h"),
         ((cells, model), BF, "h"), ((pairs_n, 2 * cells, slots), BF, "h")],
        [vm((model, 2 * model), BF), vm((model, model), BF), vm((cells, model), BF),
         vm((cells, model), BF), vm((slots, 2 * model), BF), vm((GROUP, 2 * cells, slots), F32),
         vm((pairs_n, 2 * cells, slots), BF), vm((cells, model), F32),
         vm((devices, cap, model), BF), dma((2,)), dma((5,))],
        2 * slots * model * 2 * model * 2, "cross_back",
    )
    returned = lax.all_to_all(slot_grads, ("lat", "lon"), 0, 0, tiled=True)
    encoded = call(
        encode_kernel, (after, hidden, w_down, dmix_c), "vvha", [((cells, model), BF)],
        [vm((ff, model), BF), dma((1,))], 2 * cells * model * ff, "encode",
    )
    grid_grad = call(
        grid_back_kernel,
        (flat, dstate, norm_gains, q_c, own_pairs, cross_mix, own_w, dmix_c, slot_pairs, ds_c,
         w_cross_query, w_cross_pairs), "hhvhhhhhhhhh",
        [((cells, model), BF)],
        [vm((cells, model), BF), vm((cells, model), F32), vm((cells, model), BF),
         vm((cells, 2 * model), BF), vm((cells, model), BF), vm((cells, model), BF),
         vm((cells, model), BF), vm((slots, model), BF), vm((pairs_n, 2 * cells, slots), BF), vm((cells, model), BF),
         vm((cells, 2 * model), BF), vm((model, model), BF), vm((model, 2 * model), BF),
         vm((cells, model), F32), dma((11,))],
        2 * cells * model * 3 * model, "grid_back",
    )
    obs_grad = call(
        gather_kernel, (placing, returned), "hv", [((rows_obs, model), BF)],
        [vm((slots, rows_obs), BF), vm((slots, model), BF), dma((1,))], 2 * rows_obs * slots * model, "gather",
    )
    shape = (rows_lat, rows_lon, model)
    return encoded.reshape(shape), grid_grad.reshape(shape), obs_grad


def solution(mesh):
    return jax.shard_map(
        per_device,
        mesh=mesh,
        in_specs=(
            P("lat", "lon", None),
            P(("lat", "lon"), None),
            P(("lat", "lon"), None),
            P(("lat", "lon"), None),
            P("lat", "lon", None),
            P(), P(), P(), P(), P(), P(), P(), P(),
        ),
        out_specs=(P("lat", "lon", None), P("lat", "lon", None), P(("lat", "lon"), None)),
        check_vma=False,
    )
```
